128 devices in a mesh: dp: 4 (over x), ctx: 32 (over z, y, core).
Axes of the slice: x: 4, y: 4, z: 4, core: 2. Of those that a mesh axis runs over, the one named last changes fastest.
Arguments:
- inputs: bfloat16 [16384, 896], P(('dp', 'ctx')), may hold values from -6 to 6
- cotangent: bfloat16 [16384, 896], P(('dp', 'ctx')), may hold values from -6 to 6
- span_order: int32 [64], replicated, may hold values from 0 to 63, as said below
- positions: int32 [16384], P(('dp', 'ctx')), may hold values from 0 to 1023, as said below
- attn_gain: bfloat16 [896], P('dp'), may hold values from 0.5 to 1.5
- qkv_weight: bfloat16 [896, 1152], P('dp'), may hold values from -0.1875 to 0.1875
- qkv_bias: bfloat16 [1152], P('dp'), may hold values from -3 to 3
- out_weight: bfloat16 [896, 896], P('dp'), may hold values from -0.375 to 0.375
- mlp_gain: bfloat16 [896], P('dp'), may hold values from 0.5 to 1.5
- gate_weight: bfloat16 [896, 4864], P('dp'), may hold values from -0.1875 to 0.1875
- up_weight: bfloat16 [896, 4864], P('dp'), may hold values from -0.1875 to 0.1875
- down_weight: bfloat16 [4864, 896], P('dp'), may hold values from -0.078125 to 0.078125
Outputs:
- output: bfloat16 [16384, 896], P(('dp', 'ctx'))
- input_grad: bfloat16 [16384, 896], P(('dp', 'ctx'))
- attn_gain_grad: float32 [896], P('dp')
- qkv_weight_grad: float32 [896, 1152], P('dp')
- qkv_bias_grad: float32 [1024], P('dp')
- value_bias_grad: float32 [128], P('dp')
- out_weight_grad: float32 [896, 896], P('dp')
- mlp_gain_grad: float32 [896], P('dp')
- gate_weight_grad: float32 [896, 4864], P('dp')
- up_weight_grad: float32 [896, 4864], P('dp')
- down_weight_grad: float32 [4864, 896], P('dp')
The draws below stay inside these ranges and needn't reach their ends.
Inputs may be any that keep to these rules, and one draw needn't show every extreme that they name: `span_order`: entries 2c and 2c + 1 hold two spans j and 63 - j, in either order; every span appears once. `positions`: each token's position within its document. Documents are runs of consecutive places of a sequence, none longer than 1024 tokens, and positions count from 0 at a run's start, increasing by one along place.
All inputs are finite; a program needn't handle non-finite values.
Results may differ from the reference program's by a relative error of at most 0.03.
Values may be sent and summed in bfloat16 or wider, within the bound.
A program may use at most 192 MiB of HBM per device.

```python
from functools import partial
import jax
import jax.numpy as jnp
from jax import lax

D = 896
QH = 14
KVH = 2
HD = 64
FF = 4864
CH = 64
SEQS = 4
SPANS = 64
LENGTH = 4096
TOKENS = 16384


doc_rate = 700


def mirrored_order(key):
    first = jax.random.permutation(jax.random.fold_in(key, 11), SPANS // 2).astype(jnp.int32)
    flipped = jax.random.randint(jax.random.fold_in(key, 12), (SPANS // 2,), 0, 2, dtype=jnp.int32)
    partner = SPANS - 1 - first
    leading = jnp.where(flipped == 1, partner, first)
    trailing = jnp.where(flipped == 1, first, partner)
    return jnp.stack([leading, trailing], axis=1).reshape(SPANS).astype(jnp.int32)


def draw_span_order(key, part):
    return mirrored_order(key)


def draw_positions(key, part):
    order = mirrored_order(key)
    doc_block = min(1024, LENGTH)
    slots = jnp.arange(LENGTH, dtype=jnp.int32)
    random_starts = jax.random.randint(jax.random.fold_in(key, 13), (SEQS, LENGTH), 0, doc_rate, dtype=jnp.int32) == 0
    random_starts = random_starts & (slots[None, :] >= doc_block)
    forced = (slots % doc_block == 0)[None, :]
    starts = random_starts | forced
    marks = jnp.where(starts, slots[None, :], 0)
    begins = lax.cummax(marks, axis=1)
    natural = slots[None, :] - begins
    source = order[slots // CH] * CH + slots % CH
    return jnp.take(natural, source, axis=1).reshape(SEQS * LENGTH).astype(jnp.int32)


def block_levels(key, dims, shards, low, high):
    def one(dim, blocks):
        draws = jax.random.uniform(jax.random.fold_in(jax.random.fold_in(key, 6), dim), (blocks,), jnp.float32, low / len(shards), high / len(shards))
        return jnp.repeat(jnp.exp(draws), dims[dim] // blocks).reshape((-1,) + (1,) * (len(dims) - dim - 1))

    level = one(*shards[0])
    for cut in shards[1:]:
        level = level * one(*cut)
    return level


def noise(stream_key, shape, deviation, bound, cuts=(), kind=jnp.bfloat16):
    drawn = deviation * jax.random.normal(stream_key, shape, jnp.float32)
    if cuts:
        drawn = drawn * block_levels(stream_key, shape, cuts, -0.22, 0.18)
    return jnp.clip(drawn, -bound, bound).astype(kind)


def setup_inputs(seed: int = 0) -> dict:
    splits = jax.random.split(jax.random.key(seed), 13)
    return {
        "inputs": noise(splits[0], (TOKENS, D), 1.0, 6.0, ((0, 128),)),
        "cotangent": noise(splits[1], (TOKENS, D), 1.0, 6.0, ((0, 128),)),
        "span_order": draw_span_order(jax.random.fold_in(splits[12], 71), 0),
        "positions": draw_positions(jax.random.fold_in(splits[12], 71), 0),
        "attn_gain": jnp.clip(1.0 + 0.1 * jax.random.normal(splits[4], (D,), jnp.float32), 0.5, 1.5).astype(jnp.bfloat16),
        "qkv_weight": noise(splits[5], (D, (QH + 2 * KVH) * HD), D ** -0.5, 0.1875, ((0, 4),)),
        "qkv_bias": noise(splits[6], ((QH + 2 * KVH) * HD,), 0.5, 3.0, ((0, 4),)),
        "out_weight": noise(splits[7], (QH * HD, D), (D // 4) ** -0.5, 0.375, ((0, 4),)),
        "mlp_gain": jnp.clip(1.0 + 0.1 * jax.random.normal(splits[8], (D,), jnp.float32), 0.5, 1.5).astype(jnp.bfloat16),
        "gate_weight": noise(splits[9], (D, FF), D ** -0.5, 0.1875, ((0, 4),)),
        "up_weight": noise(splits[10], (D, FF), D ** -0.5, 0.1875, ((0, 4),)),
        "down_weight": noise(splits[11], (FF, D), FF ** -0.5, 0.078125, ((0, 4),)),
    }


@jax.custom_vjp
def low(v):
    return lax.optimization_barrier(v.astype(jnp.bfloat16)).astype(jnp.float32)

@jax.custom_vjp
def low_back(v):
    return v

def low_keep(v):
    return (low(v), None)

def low_pass(kept, grad):
    return (grad,)

def back_keep(v):
    return (v, None)

def back_low(kept, grad):
    return (low(grad),)
low.defvjp(low_keep, low_pass)
low_back.defvjp(back_keep, back_low)
exact_mode = lax.Precision.HIGHEST
norm_eps = 1e-06
rope_base = 1000000.0
masked_score = -1e+30

def rms_apply(values, gain):
    mean_square = lax.optimization_barrier(jnp.mean(values * values, axis=-1, keepdims=True))
    return values * lax.rsqrt(mean_square + norm_eps) * gain

def half_turn(values):
    middle = values.shape[-1] // 2
    return jnp.concatenate([-values[..., middle:], values[..., :middle]], axis=-1)

def rotate(values, cosine, sine):
    return values * cosine + half_turn(values) * sine

def rope_tables(positions):
    middle = HD // 2
    inverse = rope_base ** (-(jnp.arange(middle).astype(jnp.float32) * 2.0) / HD)
    angles = positions.astype(jnp.float32)[:, None] * inverse[None, :]
    angles = jnp.concatenate([angles, angles], axis=-1)
    return (jnp.cos(angles), jnp.sin(angles))

def attend(query_part, query_places, keys_seq, values_seq, key_places):
    group_size = QH // KVH
    block_rows = query_part.shape[0]
    grouped = query_part.reshape(block_rows, KVH, group_size, HD)
    scores = jnp.einsum('qhgd,khd->hgqk', grouped, keys_seq, precision=exact_mode) * HD ** (-0.5)
    scores = low_back(scores)
    allowed = key_places[None, :] <= query_places[:, None]
    scores = jnp.where(allowed[None, None], scores, masked_score)
    topmost = lax.optimization_barrier(jnp.max(scores, axis=-1, keepdims=True))
    expont = jnp.exp(scores - topmost)
    weights = low(expont / lax.optimization_barrier(jnp.sum(expont, axis=-1, keepdims=True)))
    attended = jnp.einsum('hgqk,khd->qhgd', weights, values_seq, precision=exact_mode)
    return attended.reshape(block_rows, QH * HD)

def forward(places, cosine, sine, inputs, attn_gain, qkv_weight, qkv_bias, out_weight, mlp_gain, gate_weight, up_weight, down_weight):
    q_cols = QH * HD
    k_cols = KVH * HD
    normed_attn = low(rms_apply(inputs, attn_gain))
    mixed_proj = low_back(jnp.dot(normed_attn, qkv_weight, precision=exact_mode) + qkv_bias)
    query_all = mixed_proj[:, :q_cols].reshape(TOKENS, QH, HD)
    keys_all = mixed_proj[:, q_cols:q_cols + k_cols].reshape(TOKENS, KVH, HD)
    values_all = mixed_proj[:, q_cols + k_cols:].reshape(TOKENS, KVH, HD)
    query_all = low(rotate(query_all, cosine[:, None, :], sine[:, None, :]))
    keys_all = low(rotate(keys_all, cosine[:, None, :], sine[:, None, :]))
    values_all = low(values_all)
    query_block = min(512, LENGTH)
    block_total = LENGTH // query_block
    place_blocks = places.reshape(block_total, query_block)
    attend_saved = jax.checkpoint(attend)

    def one_sequence(seq_parts):
        query_seq, keys_seq, values_seq = seq_parts
        query_parts = query_seq.reshape(block_total, query_block, QH, HD)

        def one_block(block_parts):
            return attend_saved(block_parts[0], block_parts[1], keys_seq, values_seq, places)
        return lax.map(one_block, (query_parts, place_blocks)).reshape(LENGTH, q_cols)
    attended = lax.map(one_sequence, (query_all.reshape(SEQS, LENGTH, QH, HD), keys_all.reshape(SEQS, LENGTH, KVH, HD), values_all.reshape(SEQS, LENGTH, KVH, HD)))
    attended_low = low(low_back(attended.reshape(TOKENS, q_cols)))
    branch = low_back(jnp.dot(attended_low, out_weight, precision=exact_mode))
    residual = inputs + branch
    normed_mlp = low(rms_apply(residual, mlp_gain))
    gate_proj = low_back(jnp.dot(normed_mlp, gate_weight, precision=exact_mode))
    up_proj = low_back(jnp.dot(normed_mlp, up_weight, precision=exact_mode))
    hidden = low(jax.nn.silu(gate_proj) * up_proj)
    return residual + jnp.dot(hidden, down_weight, precision=exact_mode)

def reference(inputs, cotangent, span_order, positions, attn_gain, qkv_weight, qkv_bias, out_weight, mlp_gain, gate_weight, up_weight, down_weight):
    slots = jnp.arange(LENGTH).astype(jnp.int32)
    places = (span_order[slots // CH] * CH + slots % CH).astype(jnp.int32)
    cosine, sine = rope_tables(positions)
    widened = [inputs, attn_gain, qkv_weight, qkv_bias, out_weight, mlp_gain, gate_weight, up_weight, down_weight]
    widened = [item.astype(jnp.float32) for item in widened]
    result, pull_back = jax.vjp(partial(forward, places, cosine, sine), *widened)
    grads = pull_back(cotangent.astype(jnp.float32))
    qk_cols = (QH + KVH) * HD
    return (result.astype(jnp.bfloat16), grads[0].astype(jnp.bfloat16), grads[1], grads[2], grads[3][:qk_cols], grads[3][qk_cols:], grads[4], grads[5], grads[6], grads[7], grads[8])
```

```python
import functools

import jax
import jax.numpy as jnp
from jax import lax
from jax.experimental import pallas as pl
from jax.experimental.pallas import tpu as pltpu
from jax.sharding import Mesh, PartitionSpec as P

QH = 14
KVH = 2
HD = 64
GROUP = QH // KVH
D = 896
FF = 4864
SPAN = 64
CHUNK = 256

norm_eps = 1e-06
rope_base = 1000000.0
masked_score = -1e30
CTX = ("z", "y", "core")


def rms_apply(values, gain):
    mean_square = jnp.mean(values * values, axis=-1, keepdims=True)
    return values * lax.rsqrt(mean_square + norm_eps) * gain


def half_turn(values):
    middle = values.shape[-1] // 2
    return jnp.concatenate([-values[..., middle:], values[..., :middle]], axis=-1)


def rotate(values, cosine, sine):
    return values * cosine + half_turn(values) * sine


def rope_tables(positions, head_dim):
    middle = head_dim // 2
    inverse = rope_base ** (-(jnp.arange(middle).astype(jnp.float32) * 2.0) / head_dim)
    angles = positions.astype(jnp.float32)[:, None] * inverse[None, :]
    angles = jnp.concatenate([angles, angles], axis=-1)
    return (jnp.cos(angles), jnp.sin(angles))


def swiglu(gate_in, up_in):
    return jax.nn.silu(gate_in) * up_in


def dot(a, b, ca=1, cb=0):
    return lax.dot_general(a, b, (((ca,), (cb,)), ((), ())), preferred_element_type=jnp.float32)


def causal_copy(order_ref, kv_ref, sorted_ref):
    def move(slot, unused):
        source = pl.multiple_of(slot * SPAN, SPAN)
        target = pl.multiple_of(order_ref[slot] * SPAN, SPAN)
        sorted_ref[pl.ds(target, SPAN), :] = kv_ref[pl.ds(source, SPAN), :]
        return unused

    lax.fori_loop(0, kv_ref.shape[0] // SPAN, move, 0)


def visible(start, place, rows):
    key_place = lax.broadcasted_iota(jnp.int32, (CHUNK, rows), 0) + start
    lane = lax.broadcasted_iota(jnp.int32, (CHUNK, rows), 1)
    return key_place <= place * SPAN + lane % SPAN


def attend_kernel(order_ref, mine_ref, kv_ref, q_ref, out_ref, lse_ref, sorted_ref):
    causal_copy(order_ref, kv_ref, sorted_ref)
    rows = q_ref.shape[-1]
    for half in range(2):
        place = mine_ref[half]
        last = place * SPAN // CHUNK

        def step(index, carry, masked, half=half, place=place):
            start = pl.multiple_of(index * CHUNK, CHUNK)
            keys = sorted_ref[pl.ds(start, CHUNK), :128]
            values = sorted_ref[pl.ds(start, CHUNK), 128:]
            result = []
            for head in range(KVH):
                top, total, mixed = carry[head]
                scores = dot(keys, q_ref[half, head])
                if masked:
                    scores = jnp.where(visible(start, place, rows), scores, masked_score)
                new_top = jnp.maximum(top, jnp.max(scores, axis=0, keepdims=True))
                shrink = jnp.exp(top - new_top)
                weights = jnp.exp(scores - new_top)
                total = total * shrink + jnp.sum(weights, axis=0, keepdims=True)
                mixed = mixed * shrink + dot(values, weights.astype(jnp.bfloat16), 0, 0)
                result.append((new_top, total, mixed))
            return tuple(result)

        empty = tuple(
            (
                jnp.full((1, rows), masked_score, jnp.float32),
                jnp.zeros((1, rows), jnp.float32),
                jnp.zeros((128, rows), jnp.float32),
            )
            for head in range(KVH)
        )
        carry = lax.fori_loop(0, last, functools.partial(step, masked=False), empty)
        carry = step(last, carry, True)
        for head in range(KVH):
            top, total, mixed = carry[head]
            out_ref[half, head] = mixed[head * HD : (head + 1) * HD] / total
            lse_ref[half, head] = top + jnp.log(total)


def attend(order, mine, kv_all, q_pad):
    halves, heads, unused, rows = q_pad.shape
    smem = pl.BlockSpec(memory_space=pltpu.SMEM)
    vmem = pl.BlockSpec(memory_space=pltpu.VMEM)
    return pl.pallas_call(
        attend_kernel,
        out_shape=(
            jax.ShapeDtypeStruct((halves, heads, HD, rows), jnp.float32),
            jax.ShapeDtypeStruct((halves, heads, 1, rows), jnp.float32),
        ),
        in_specs=[smem, smem, vmem, vmem],
        out_specs=(vmem, vmem),
        scratch_shapes=[pltpu.VMEM(kv_all.shape, kv_all.dtype)],
        compiler_params=pltpu.CompilerParams(vmem_limit_bytes=48 * 1024 * 1024),
        cost_estimate=pl.CostEstimate(
            flops=3_000_000_000, bytes_accessed=6_000_000, transcendentals=4_000_000
        ),
        name="attend",
    )(order, mine, kv_all, q_pad)


def attend_back_kernel(
    order_ref,
    mine_ref,
    kv_ref,
    q_ref,
    q_rows_ref,
    do_ref,
    do_rows_ref,
    lse_ref,
    delta_ref,
    dq_ref,
    dkv_ref,
    sorted_ref,
    sum_ref,
):
    causal_copy(order_ref, kv_ref, sorted_ref)
    sum_ref[...] = jnp.zeros_like(sum_ref)
    rows = q_ref.shape[-1]
    for half in range(2):
        place = mine_ref[half]
        last = place * SPAN // CHUNK

        def step(index, carry, masked, half=half, place=place):
            start = pl.multiple_of(index * CHUNK, CHUNK)
            keys = sorted_ref[pl.ds(start, CHUNK), :128]
            values = sorted_ref[pl.ds(start, CHUNK), 128:]
            d_keys = sum_ref[pl.ds(start, CHUNK), :128]
            d_values = sum_ref[pl.ds(start, CHUNK), 128:]
            result = []
            for head in range(KVH):
                scores = dot(keys, q_ref[half, head])
                probs = jnp.exp(scores - lse_ref[half, head])
                if masked:
                    probs = jnp.where(visible(start, place, rows), probs, 0.0)
                d_probs = dot(values, do_ref[half, head])
                d_scores = (probs * (d_probs - delta_ref[half, head])).astype(jnp.bfloat16)
                d_values += dot(probs.astype(jnp.bfloat16), do_rows_ref[half, head])
                d_keys += dot(d_scores, q_rows_ref[half, head])
                result.append(carry[head] + dot(keys, d_scores, 0, 0))
            sum_ref[pl.ds(start, CHUNK), :128] = d_keys
            sum_ref[pl.ds(start, CHUNK), 128:] = d_values
            return tuple(result)

        empty = tuple(jnp.zeros((128, rows), jnp.float32) for head in range(KVH))
        carry = lax.fori_loop(0, last, functools.partial(step, masked=False), empty)
        carry = step(last, carry, True)
        for head in range(KVH):
            dq_ref[half, head] = carry[head][head * HD : (head + 1) * HD] * (HD**-0.5)

    def move(slot, unused):
        target = pl.multiple_of(slot * SPAN, SPAN)
        source = pl.multiple_of(order_ref[slot] * SPAN, SPAN)
        dkv_ref[pl.ds(target, SPAN), :] = sum_ref[pl.ds(source, SPAN), :].astype(jnp.bfloat16)
        return unused

    lax.fori_loop(0, dkv_ref.shape[0] // SPAN, move, 0)


def attend_back(order, mine, kv_all, q_pad, q_rows, do_pad, do_rows, lse, delta):
    halves, heads, unused, rows = q_pad.shape
    smem = pl.BlockSpec(memory_space=pltpu.SMEM)
    vmem = pl.BlockSpec(memory_space=pltpu.VMEM)
    return pl.pallas_call(
        attend_back_kernel,
        out_shape=(
            jax.ShapeDtypeStruct((halves, heads, HD, rows), jnp.float32),
            jax.ShapeDtypeStruct(kv_all.shape, jnp.bfloat16),
        ),
        in_specs=[smem, smem] + [vmem] * 7,
        out_specs=(vmem, vmem),
        scratch_shapes=[
            pltpu.VMEM(kv_all.shape, kv_all.dtype),
            pltpu.VMEM(kv_all.shape, jnp.float32),
        ],
        compiler_params=pltpu.CompilerParams(vmem_limit_bytes=48 * 1024 * 1024),
        cost_estimate=pl.CostEstimate(
            flops=8_000_000_000, bytes_accessed=9_000_000, transcendentals=4_000_000
        ),
        name="attend_back",
    )(order, mine, kv_all, q_pad, q_rows, do_pad, do_rows, lse, delta)


def split_rows(tokens):
    parts = tokens.reshape(2, SPAN, KVH, GROUP, HD)
    return parts.transpose(0, 2, 3, 1, 4).reshape(2, KVH, GROUP * SPAN, HD)


def pad_heads(rows):
    return jnp.stack(
        [
            jnp.pad(rows[:, 0], ((0, 0), (0, 0), (0, HD))),
            jnp.pad(rows[:, 1], ((0, 0), (0, 0), (HD, 0))),
        ],
        axis=1,
    )


def join_rows(columns):
    parts = columns.reshape(2, KVH, HD, GROUP, SPAN)
    return parts.transpose(0, 4, 1, 3, 2).reshape(2 * SPAN, QH * HD)


def body(
    inputs,
    cotangent,
    span_order,
    positions,
    attn_gain,
    qkv_weight,
    qkv_bias,
    out_weight,
    mlp_gain,
    gate_weight,
    up_weight,
    down_weight,
):
    token_count = inputs.shape[0]
    q_cols = QH * HD
    k_cols = KVH * HD
    slices = lax.axis_size("dp")
    own_rows = D // slices
    part = FF // (slices * 2)
    dp = lax.axis_index("dp")
    core = lax.axis_index("core")
    slot = (lax.axis_index("z") * lax.axis_size("y") + lax.axis_index("y")) * 2 + core

    qkv_full = lax.all_gather(qkv_weight, "dp", axis=0, tiled=True)
    small = lax.all_gather(jnp.concatenate([attn_gain, mlp_gain, qkv_bias]), "dp", axis=0)
    gain_one_wide = small[:, :own_rows].reshape(D).astype(jnp.float32)
    gain_two_wide = small[:, own_rows : 2 * own_rows].reshape(D).astype(jnp.float32)
    bias_full = small[:, 2 * own_rows :].reshape(-1).astype(jnp.float32)
    out_full = lax.all_gather(out_weight, "dp", axis=0, tiled=True)

    stacked = jnp.stack([gate_weight, up_weight])
    stacked = stacked.reshape(2, own_rows, slices, 2, part)
    stacked = lax.dynamic_index_in_dim(stacked, core, axis=3, keepdims=False)
    stacked = stacked.transpose(2, 0, 1, 3)
    received = lax.all_to_all(stacked, "dp", 0, 0, tiled=True)
    gate_part = received[:, 0].reshape(D, part)
    up_part = received[:, 1].reshape(D, part)
    down_part = lax.dynamic_slice_in_dim(down_weight, core * part, part, axis=0)
    cot_all = lax.all_gather(cotangent, ("dp", "core"), axis=0, tiled=True)

    inputs_wide = inputs.astype(jnp.float32)
    normed_one = rms_apply(inputs_wide, gain_one_wide).astype(jnp.bfloat16)
    mixed_proj = dot(normed_one, qkv_full) + bias_full
    cosine, sine = rope_tables(positions, HD)
    cosine = cosine[:, None, :]
    sine = sine[:, None, :]
    query_rot = rotate(
        mixed_proj[:, :q_cols].reshape(token_count, QH, HD), cosine, sine
    ).astype(jnp.bfloat16)
    key_rot = rotate(
        mixed_proj[:, q_cols : q_cols + k_cols].reshape(token_count, KVH, HD), cosine, sine
    )
    key_rot = key_rot.astype(jnp.bfloat16).reshape(token_count, k_cols)
    value_low = mixed_proj[:, q_cols + k_cols :].astype(jnp.bfloat16)
    kv_all = lax.all_gather(
        jnp.concatenate([key_rot, value_low], axis=1), CTX, axis=0, tiled=True
    )
    mine = lax.dynamic_slice_in_dim(span_order, 2 * slot, 2)
    q_rows = pad_heads(split_rows(query_rot * jnp.bfloat16(HD**-0.5)))
    q_pad = q_rows.transpose(0, 1, 3, 2)
    attended_cols, lse = attend(span_order, mine, kv_all, q_pad)
    attended_wide = join_rows(attended_cols)
    attended_low = attended_wide.astype(jnp.bfloat16)
    residual = inputs_wide + dot(attended_low, out_full)
    normed_two = rms_apply(residual, gain_two_wide).astype(jnp.bfloat16)

    normed_all = lax.all_gather(normed_two, ("dp", "core"), axis=0, tiled=True)
    gate_proj = dot(normed_all, gate_part)
    up_proj = dot(normed_all, up_part)
    hidden_low = swiglu(gate_proj, up_proj).astype(jnp.bfloat16)
    out_sum = dot(hidden_low, down_part).astype(jnp.bfloat16)
    d_hidden = dot(cot_all, down_part, 1, 1)
    d_gate, d_up = jax.vjp(swiglu, gate_proj, up_proj)[1](d_hidden)
    d_gate = d_gate.astype(jnp.bfloat16)
    d_up = d_up.astype(jnp.bfloat16)
    d_norm_sum = (dot(d_gate, gate_part, 1, 1) + dot(d_up, up_part, 1, 1)).astype(jnp.bfloat16)
    down_grad = dot(hidden_low, cot_all, 0, 0).astype(jnp.bfloat16)
    gate_grad = dot(normed_all, d_gate, 0, 0).astype(jnp.bfloat16)
    up_grad = dot(normed_all, d_up, 0, 0).astype(jnp.bfloat16)
    d_normed_two = lax.psum_scatter(
        d_norm_sum, ("dp", "core"), scatter_dimension=0, tiled=True
    ).astype(jnp.float32)
    output = (
        residual
        + lax.psum_scatter(out_sum, ("dp", "core"), scatter_dimension=0, tiled=True).astype(
            jnp.float32
        )
    ).astype(jnp.bfloat16)
    down_grad, gate_grad, up_grad = lax.psum((down_grad, gate_grad, up_grad), ("z", "y"))

    d_resid_part, gain_two_grad = jax.vjp(rms_apply, residual, gain_two_wide)[1](d_normed_two)
    d_residual = d_resid_part + cotangent.astype(jnp.float32)
    d_branch = d_residual.astype(jnp.bfloat16)
    d_attended = dot(d_branch, out_full, 1, 1).astype(jnp.bfloat16)
    row_delta = jnp.sum(
        (d_attended.astype(jnp.float32) * attended_wide).reshape(
            2, SPAN, KVH, GROUP, HD
        ),
        axis=-1,
    )
    row_delta = row_delta.transpose(0, 2, 3, 1).reshape(2, KVH, 1, GROUP * SPAN)
    do_rows = pad_heads(split_rows(d_attended))
    do_pad = do_rows.transpose(0, 1, 3, 2)
    d_query_cols, d_kv_all = attend_back(
        span_order, mine, kv_all, q_pad, q_rows, do_pad, do_rows, lse, row_delta
    )
    d_kv = lax.psum_scatter(d_kv_all, CTX, scatter_dimension=0, tiled=True).astype(jnp.float32)

    def turn_back(grads):
        scaled = grads * sine
        middle = HD // 2
        back = jnp.concatenate([scaled[..., middle:], -scaled[..., :middle]], axis=-1)
        return grads * cosine + back

    d_query_raw = turn_back(join_rows(d_query_cols).reshape(token_count, QH, HD))
    d_key_raw = turn_back(d_kv[:, :k_cols].reshape(token_count, KVH, HD))
    d_mixed = jnp.concatenate(
        [
            d_query_raw.reshape(token_count, q_cols),
            d_key_raw.reshape(token_count, k_cols),
            d_kv[:, k_cols:],
        ],
        axis=1,
    ).astype(jnp.bfloat16)

    def my_columns(tokens):
        parts = tokens.reshape(token_count, slices, own_rows).transpose(1, 0, 2)
        moved = lax.all_to_all(parts, "dp", 0, 0, tiled=True)
        return moved.reshape(slices * token_count, own_rows)

    normed_one_mine = my_columns(normed_one)
    attended_mine = my_columns(attended_low)
    d_branch_all = lax.all_gather(d_branch, "dp", axis=0, tiled=True)
    out_grad = dot(attended_mine, d_branch_all, 0, 0).astype(jnp.bfloat16)
    d_mixed_all = lax.all_gather(d_mixed, "dp", axis=0, tiled=True)
    qkv_grad = dot(normed_one_mine, d_mixed_all, 0, 0).astype(jnp.bfloat16)
    bias_grad = jnp.sum(d_mixed.astype(jnp.float32), axis=0)
    d_normed_one = dot(d_mixed, qkv_full, 1, 1)
    d_input_part, gain_one_grad = jax.vjp(rms_apply, inputs_wide, gain_one_wide)[1](d_normed_one)
    input_grad = (d_input_part + d_residual).astype(jnp.bfloat16)

    out_grad, qkv_grad = lax.psum((out_grad, qkv_grad), CTX)
    vectors = lax.psum(
        jnp.concatenate([gain_one_grad, gain_two_grad, bias_grad]), ("dp",) + CTX
    )

    def owned(start, count):
        width = count // slices
        return lax.dynamic_slice_in_dim(vectors, start + dp * width, width)

    gate_up = jnp.stack([gate_grad, up_grad]).reshape(2, slices, own_rows, part)
    gate_up = lax.all_to_all(gate_up.transpose(1, 0, 2, 3), "dp", 0, 0, tiled=True)
    gate_up = lax.all_gather(gate_up, "core", axis=1)
    gate_up = gate_up.transpose(2, 3, 0, 1, 4).reshape(2, own_rows, FF).astype(jnp.float32)
    down_grad = lax.all_gather(down_grad, "core", axis=0, tiled=True)
    return (
        output,
        input_grad,
        owned(0, D),
        qkv_grad.astype(jnp.float32),
        owned(2 * D, q_cols + k_cols),
        owned(2 * D + q_cols + k_cols, k_cols),
        out_grad.astype(jnp.float32),
        owned(D, D),
        gate_up[0],
        gate_up[1],
        down_grad.astype(jnp.float32),
    )


def solution(mesh):
    grid = Mesh(mesh.devices.reshape(4, 4, 4, 2), ("dp", "z", "y", "core"))
    tokens = ("dp",) + CTX
    return jax.shard_map(
        body,
        mesh=grid,
        in_specs=(
            P(tokens, None),
            P(tokens, None),
            P(),
            P(tokens),
            P("dp"),
            P("dp", None),
            P("dp"),
            P("dp", None),
            P("dp"),
            P("dp", None),
            P("dp", None),
            P("dp", None),
        ),
        out_specs=(
            P(tokens, None),
            P(tokens, None),
            P("dp"),
            P("dp", None),
            P("dp"),
            P("dp"),
            P("dp", None),
            P("dp"),
            P("dp", None),
            P("dp", None),
            P("dp", None),
        ),
        check_vma=False,
    )
```

```python
import functools

import jax
import jax.numpy as jnp
from jax import lax
from jax.experimental import pallas as pl
from jax.experimental.pallas import tpu as pltpu
from jax.sharding import Mesh, PartitionSpec as P

QH = 14
KVH = 2
HD = 64
GROUP = QH // KVH
D = 896
FF = 4864
SPAN = 64
CHUNK = 256

norm_eps = 1e-06
rope_base = 1000000.0
masked_score = -1e30
CTX = ("z", "y", "core")
ROW = ("dp",)
PLANE = ("z", "y")

MESH = pl.DeviceIdType.MESH
SIZES = {"dp": 4, "z": 4, "y": 4}


def group_size(axes):
    size = 1
    for axis in axes:
        size *= SIZES[axis]
    return size


def group_index(axes):
    index = 0
    for axis in axes:
        index = index * SIZES[axis] + lax.axis_index(axis)
    return index


def member(axes, index):
    found = {}
    for axis in reversed(axes):
        found[axis] = index % SIZES[axis]
        index = index // SIZES[axis]
    return found


def remote(source, target, send, receive, device):
    return pltpu.make_async_remote_copy(
        src_ref=source,
        dst_ref=target,
        send_sem=send,
        recv_sem=receive,
        device_id=device,
        device_id_type=MESH,
    )


class Gather:
    def __init__(self, axes, array):
        self.axes, self.n = axes, group_size(axes)
        self.block, self.dtype = array.shape, array.dtype
        self.in_space = pl.ANY
        self.out = jax.ShapeDtypeStruct((self.n, 2) + self.block, self.dtype)
        self.out_space = pl.ANY
        self.scratch = [pltpu.SemaphoreType.DMA] + [pltpu.SemaphoreType.DMA((self.n,))] * 4

    def bind(self, source, target, scratch):
        self.x, self.o = source, target
        self.local, self.send, self.receive, self.f_send, self.f_receive = scratch
        self.me, self.core = group_index(self.axes), lax.axis_index("core")

    def mine(self):
        return pltpu.make_async_copy(self.x, self.o.at[self.me, self.core], self.local)

    def outward(self, k):
        device = member(self.axes, (self.me + k) % self.n)
        place = self.o.at[self.me, self.core]
        return remote(self.x, place, self.send.at[k], self.receive.at[k], device)

    def inward(self, k):
        device = member(self.axes, (self.me + k) % self.n)
        place = self.o.at[(self.me + self.n - k) % self.n, self.core]
        return remote(self.x, place, self.send.at[k], self.receive.at[k], device)

    def forward(self, k, core):
        place = self.o.at[(self.me + self.n - k) % self.n, core]
        source = self.x if k == 0 else place
        device = {"core": 1 - self.core}
        return remote(source, place, self.f_send.at[k], self.f_receive.at[k], device)

    def start(self):
        self.mine().start()
        for k in range(1, self.n):
            self.outward(k).start()
        self.forward(0, self.core).start()

    def middle(self):
        for k in range(1, self.n):
            self.inward(k).wait_recv()
            self.forward(k, self.core).start()

    def end(self):
        self.mine().wait()
        for k in range(self.n):
            if k:
                self.outward(k).wait_send()
            self.forward(k, self.core).wait_send()
            self.forward(k, 1 - self.core).wait_recv()


class Exchange:
    def __init__(self, axes, array):
        self.axes, self.n = axes, group_size(axes)
        self.in_space = pl.ANY
        self.out = jax.ShapeDtypeStruct(array.shape, array.dtype)
        self.out_space = pl.ANY
        self.scratch = [pltpu.SemaphoreType.DMA] + [pltpu.SemaphoreType.DMA((self.n,))] * 2

    def bind(self, source, target, scratch):
        self.x, self.o = source, target
        self.local, self.send, self.receive = scratch
        self.me = group_index(self.axes)

    def mine(self):
        return pltpu.make_async_copy(self.x.at[self.me], self.o.at[self.me], self.local)

    def outward(self, k, slot):
        to = (self.me + k) % self.n
        return remote(
            self.x.at[to],
            self.o.at[slot],
            self.send.at[k],
            self.receive.at[k],
            member(self.axes, to),
        )

    def start(self):
        self.mine().start()
        for k in range(1, self.n):
            self.outward(k, self.me).start()

    def middle(self):
        pass

    def end(self):
        self.mine().wait()
        for k in range(1, self.n):
            self.outward(k, self.me).wait_send()
            self.outward(k, (self.me + self.n - k) % self.n).wait_recv()


class Scatter:
    def __init__(self, axes, array):
        self.axes, self.n = axes, group_size(axes)
        self.block = array.shape[2:]
        self.in_space = pltpu.VMEM
        self.out = jax.ShapeDtypeStruct(self.block, jnp.float32)
        self.out_space = pltpu.VMEM
        buffer = pltpu.VMEM((self.n,) + self.block, array.dtype)
        self.scratch = [buffer] * 3 + [pltpu.SemaphoreType.DMA((self.n,))] * 4

    def bind(self, source, target, scratch):
        self.x, self.o = source, target
        self.half, self.summed, self.land = scratch[:3]
        self.s_one, self.r_one, self.s_two, self.r_two = scratch[3:]
        self.me, self.core = group_index(self.axes), lax.axis_index("core")

    def across(self, k):
        to = (self.me + k + 1) % self.n
        return remote(
            self.x.at[to, 1 - self.core],
            self.half.at[to],
            self.s_one.at[k],
            self.r_one.at[k],
            {"core": 1 - self.core},
        )

    def outward(self, k, slot):
        to = (self.me + k + 1) % self.n
        return remote(
            self.summed.at[to],
            self.land.at[slot],
            self.s_two.at[k],
            self.r_two.at[k],
            member(self.axes, to),
        )

    def start(self):
        for k in range(self.n):
            self.across(k).start()

    def middle(self):
        for k in range(self.n):
            to = (self.me + k + 1) % self.n
            self.across(k).wait_recv()
            both = self.x[to, self.core].astype(jnp.float32) + self.half[to].astype(jnp.float32)
            if k == self.n - 1:
                self.o[...] = both
            else:
                self.summed[to] = both.astype(self.summed.dtype)
                self.outward(k, self.me).start()

    def end(self):
        for k in range(self.n - 1):
            source = (self.me + self.n - k - 1) % self.n
            self.outward(k, source).wait_recv()
            self.o[...] += self.land[source].astype(jnp.float32)
        for k in range(self.n):
            self.across(k).wait_send()
            if k < self.n - 1:
                self.outward(k, self.me).wait_send()


class Total:
    def __init__(self, axes, array):
        self.axes, self.n = axes, group_size(axes)
        self.block = array.shape[1:]
        self.in_space = pltpu.VMEM
        own = jax.ShapeDtypeStruct(self.block, array.dtype)
        self.gather = Gather(axes, own)
        self.out, self.out_space = self.gather.out, self.gather.out_space
        self.scratch = [
            pltpu.VMEM((self.n,) + self.block, array.dtype),
            pltpu.VMEM(self.block, array.dtype),
            pltpu.SemaphoreType.DMA((self.n,)),
            pltpu.SemaphoreType.DMA((self.n,)),
        ] + self.gather.scratch

    def bind(self, source, target, scratch):
        self.x = source
        self.land, self.own, self.send, self.receive = scratch[:4]
        self.gather.bind(self.own, target, scratch[4:])
        self.me = self.gather.me

    def outward(self, k, slot):
        to = (self.me + k) % self.n
        return remote(
            self.x.at[to],
            self.land.at[slot],
            self.send.at[k],
            self.receive.at[k],
            member(self.axes, to),
        )

    def start(self):
        for k in range(1, self.n):
            self.outward(k, self.me).start()

    def middle(self):
        total = self.x[self.me].astype(jnp.float32)
        for k in range(1, self.n):
            source = (self.me + self.n - k) % self.n
            self.outward(k, source).wait_recv()
            total += self.land[source].astype(jnp.float32)
        self.own[...] = total.astype(self.own.dtype)
        self.gather.start()
        self.gather.middle()

    def end(self):
        self.gather.end()
        for k in range(1, self.n):
            self.outward(k, self.me).wait_send()


def communicate_kernel(ops, *refs):
    count = len(ops)
    scratch = list(refs[2 * count :])
    groups = []
    for index, op in enumerate(ops):
        used = [scratch.pop(0) for unused in op.scratch]
        op.bind(refs[index], refs[count + index], used)
        if op.axes not in groups:
            groups.append(op.axes)
    barrier = pltpu.get_barrier_semaphore()
    devices = [{"core": 1 - lax.axis_index("core")}]
    for axes in groups:
        n, me = group_size(axes), group_index(axes)
        devices += [member(axes, (me + k) % n) for k in range(1, n)]
    for device in devices:
        pl.semaphore_signal(barrier, inc=1, device_id=device, device_id_type=MESH)
    pl.semaphore_wait(barrier, len(devices))
    for op in ops:
        op.start()
    for op in ops:
        op.middle()
    for op in ops:
        op.end()


def communicate(name, identity, *requests):
    arrays = [array for kind, axes, array in requests]
    ops = [kind(axes, array) for kind, axes, array in requests]
    return pl.pallas_call(
        functools.partial(communicate_kernel, ops),
        out_shape=tuple(op.out for op in ops),
        in_specs=[pl.BlockSpec(memory_space=op.in_space) for op in ops],
        out_specs=tuple(pl.BlockSpec(memory_space=op.out_space) for op in ops),
        scratch_shapes=[item for op in ops for item in op.scratch],
        compiler_params=pltpu.CompilerParams(
            collective_id=identity,
            has_side_effects=True,
            vmem_limit_bytes=48 * 1024 * 1024,
        ),
        cost_estimate=pl.CostEstimate(flops=0, bytes_accessed=60_000_000, transcendentals=0),
        name=name,
    )(*arrays)


def rms_apply(values, gain):
    mean_square = jnp.mean(values * values, axis=-1, keepdims=True)
    return values * lax.rsqrt(mean_square + norm_eps) * gain


def half_turn(values):
    middle = values.shape[-1] // 2
    return jnp.concatenate([-values[..., middle:], values[..., :middle]], axis=-1)


def rotate(values, cosine, sine):
    return values * cosine + half_turn(values) * sine


def rope_tables(positions, head_dim):
    middle = head_dim // 2
    inverse = rope_base ** (-(jnp.arange(middle).astype(jnp.float32) * 2.0) / head_dim)
    angles = positions.astype(jnp.float32)[:, None] * inverse[None, :]
    angles = jnp.concatenate([angles, angles], axis=-1)
    return (jnp.cos(angles), jnp.sin(angles))


def swiglu(gate_in, up_in):
    return jax.nn.silu(gate_in) * up_in


def dot(a, b, ca=1, cb=0):
    return lax.dot_general(a, b, (((ca,), (cb,)), ((), ())), preferred_element_type=jnp.float32)


def causal_copy(order_ref, kv_ref, sorted_ref):
    def move(slot, unused):
        source = pl.multiple_of(slot * SPAN, SPAN)
        target = pl.multiple_of(order_ref[slot] * SPAN, SPAN)
        sorted_ref[pl.ds(target, SPAN), :] = kv_ref[pl.ds(source, SPAN), :]
        return unused

    lax.fori_loop(0, kv_ref.shape[0] // SPAN, move, 0)


def visible(start, place, rows):
    key_place = lax.broadcasted_iota(jnp.int32, (CHUNK, rows), 0) + start
    lane = lax.broadcasted_iota(jnp.int32, (CHUNK, rows), 1)
    return key_place <= place * SPAN + lane % SPAN


def attend_kernel(order_ref, mine_ref, kv_ref, q_ref, out_ref, lse_ref, sorted_ref):
    causal_copy(order_ref, kv_ref, sorted_ref)
    rows = q_ref.shape[-1]
    for half in range(2):
        place = mine_ref[half]
        last = place * SPAN // CHUNK

        def step(index, carry, masked, half=half, place=place):
            start = pl.multiple_of(index * CHUNK, CHUNK)
            keys = sorted_ref[pl.ds(start, CHUNK), :128]
            values = sorted_ref[pl.ds(start, CHUNK), 128:]
            result = []
            for head in range(KVH):
                top, total, mixed = carry[head]
                scores = dot(keys, q_ref[half, head])
                if masked:
                    scores = jnp.where(visible(start, place, rows), scores, masked_score)
                new_top = jnp.maximum(top, jnp.max(scores, axis=0, keepdims=True))
                shrink = jnp.exp(top - new_top)
                weights = jnp.exp(scores - new_top)
                total = total * shrink + jnp.sum(weights, axis=0, keepdims=True)
                mixed = mixed * shrink + dot(values, weights.astype(jnp.bfloat16), 0, 0)
                result.append((new_top, total, mixed))
            return tuple(result)

        empty = tuple(
            (
                jnp.full((1, rows), masked_score, jnp.float32),
                jnp.zeros((1, rows), jnp.float32),
                jnp.zeros((128, rows), jnp.float32),
            )
            for head in range(KVH)
        )
        carry = lax.fori_loop(0, last, functools.partial(step, masked=False), empty)
        carry = step(last, carry, True)
        for head in range(KVH):
            top, total, mixed = carry[head]
            out_ref[half, head] = mixed[head * HD : (head + 1) * HD] / total
            lse_ref[half, head] = top + jnp.log(total)


def attend(order, mine, kv_all, q_pad):
    halves, heads, unused, rows = q_pad.shape
    smem = pl.BlockSpec(memory_space=pltpu.SMEM)
    vmem = pl.BlockSpec(memory_space=pltpu.VMEM)
    return pl.pallas_call(
        attend_kernel,
        out_shape=(
            jax.ShapeDtypeStruct((halves, heads, HD, rows), jnp.float32),
            jax.ShapeDtypeStruct((halves, heads, 1, rows), jnp.float32),
        ),
        in_specs=[smem, smem, vmem, vmem],
        out_specs=(vmem, vmem),
        scratch_shapes=[pltpu.VMEM(kv_all.shape, kv_all.dtype)],
        compiler_params=pltpu.CompilerParams(vmem_limit_bytes=48 * 1024 * 1024),
        cost_estimate=pl.CostEstimate(
            flops=3_000_000_000, bytes_accessed=6_000_000, transcendentals=4_000_000
        ),
        name="attend",
    )(order, mine, kv_all, q_pad)


def attend_back_kernel(
    order_ref,
    mine_ref,
    kv_ref,
    q_ref,
    q_rows_ref,
    do_ref,
    do_rows_ref,
    lse_ref,
    delta_ref,
    dq_ref,
    dkv_ref,
    sorted_ref,
    sum_ref,
):
    causal_copy(order_ref, kv_ref, sorted_ref)
    sum_ref[...] = jnp.zeros_like(sum_ref)
    rows = q_ref.shape[-1]
    for half in range(2):
        place = mine_ref[half]
        last = place * SPAN // CHUNK

        def step(index, carry, masked, half=half, place=place):
            start = pl.multiple_of(index * CHUNK, CHUNK)
            keys = sorted_ref[pl.ds(start, CHUNK), :128]
            values = sorted_ref[pl.ds(start, CHUNK), 128:]
            d_keys = sum_ref[pl.ds(start, CHUNK), :128]
            d_values = sum_ref[pl.ds(start, CHUNK), 128:]
            result = []
            for head in range(KVH):
                scores = dot(keys, q_ref[half, head])
                probs = jnp.exp(scores - lse_ref[half, head])
                if masked:
                    probs = jnp.where(visible(start, place, rows), probs, 0.0)
                d_probs = dot(values, do_ref[half, head])
                d_scores = (probs * (d_probs - delta_ref[half, head])).astype(jnp.bfloat16)
                d_values += dot(probs.astype(jnp.bfloat16), do_rows_ref[half, head])
                d_keys += dot(d_scores, q_rows_ref[half, head])
                result.append(carry[head] + dot(keys, d_scores, 0, 0))
            sum_ref[pl.ds(start, CHUNK), :128] = d_keys
            sum_ref[pl.ds(start, CHUNK), 128:] = d_values
            return tuple(result)

        empty = tuple(jnp.zeros((128, rows), jnp.float32) for head in range(KVH))
        carry = lax.fori_loop(0, last, functools.partial(step, masked=False), empty)
        carry = step(last, carry, True)
        for head in range(KVH):
            dq_ref[half, head] = carry[head][head * HD : (head + 1) * HD] * (HD**-0.5)

    def move(slot, unused):
        target = pl.multiple_of(slot * SPAN, SPAN)
        source = pl.multiple_of(order_ref[slot] * SPAN, SPAN)
        dkv_ref[pl.ds(target, SPAN), :] = sum_ref[pl.ds(source, SPAN), :].astype(jnp.bfloat16)
        return unused

    lax.fori_loop(0, dkv_ref.shape[0] // SPAN, move, 0)


def attend_back(order, mine, kv_all, q_pad, q_rows, do_pad, do_rows, lse, delta):
    halves, heads, unused, rows = q_pad.shape
    smem = pl.BlockSpec(memory_space=pltpu.SMEM)
    vmem = pl.BlockSpec(memory_space=pltpu.VMEM)
    return pl.pallas_call(
        attend_back_kernel,
        out_shape=(
            jax.ShapeDtypeStruct((halves, heads, HD, rows), jnp.float32),
            jax.ShapeDtypeStruct(kv_all.shape, jnp.bfloat16),
        ),
        in_specs=[smem, smem] + [vmem] * 7,
        out_specs=(vmem, vmem),
        scratch_shapes=[
            pltpu.VMEM(kv_all.shape, kv_all.dtype),
            pltpu.VMEM(kv_all.shape, jnp.float32),
        ],
        compiler_params=pltpu.CompilerParams(vmem_limit_bytes=48 * 1024 * 1024),
        cost_estimate=pl.CostEstimate(
            flops=8_000_000_000, bytes_accessed=9_000_000, transcendentals=4_000_000
        ),
        name="attend_back",
    )(order, mine, kv_all, q_pad, q_rows, do_pad, do_rows, lse, delta)


def split_rows(tokens):
    parts = tokens.reshape(2, SPAN, KVH, GROUP, HD)
    return parts.transpose(0, 2, 3, 1, 4).reshape(2, KVH, GROUP * SPAN, HD)


def pad_heads(rows):
    return jnp.stack(
        [
            jnp.pad(rows[:, 0], ((0, 0), (0, 0), (0, HD))),
            jnp.pad(rows[:, 1], ((0, 0), (0, 0), (HD, 0))),
        ],
        axis=1,
    )


def join_rows(columns):
    parts = columns.reshape(2, KVH, HD, GROUP, SPAN)
    return parts.transpose(0, 4, 1, 3, 2).reshape(2 * SPAN, QH * HD)


def body(
    inputs,
    cotangent,
    span_order,
    positions,
    attn_gain,
    qkv_weight,
    qkv_bias,
    out_weight,
    mlp_gain,
    gate_weight,
    up_weight,
    down_weight,
):
    token_count = inputs.shape[0]
    q_cols = QH * HD
    k_cols = KVH * HD
    slices = lax.axis_size("dp")
    own_rows = D // slices
    part = FF // (slices * 2)
    dp = lax.axis_index("dp")
    core = lax.axis_index("core")
    slot = (lax.axis_index("z") * lax.axis_size("y") + lax.axis_index("y")) * 2 + core

    small = jnp.concatenate([attn_gain, mlp_gain, qkv_bias])
    small = jnp.pad(small, (0, 2048 - small.shape[0])).reshape(16, 128)
    qkv_half = lax.dynamic_slice_in_dim(qkv_weight, core * (own_rows // 2), own_rows // 2)
    qkv_full, small = communicate("qkv_in", 0, (Gather, ROW, qkv_half), (Gather, ROW, small))
    qkv_full = qkv_full.reshape(D, -1)
    small = small[:, 0].reshape(slices, -1)
    gain_one_wide = small[:, :own_rows].reshape(D).astype(jnp.float32)
    gain_two_wide = small[:, own_rows : 2 * own_rows].reshape(D).astype(jnp.float32)
    bias_full = small[:, 2 * own_rows : 2 * own_rows + qkv_bias.shape[0]]
    bias_full = bias_full.reshape(-1).astype(jnp.float32)
    out_full = lax.all_gather(out_weight, "dp", axis=0, tiled=True)

    def column_blocks(weight):
        parts = [weight[:, part * index : part * (index + 1)] for index in range(2 * slices)]
        return jnp.stack(
            [jnp.where(core == 0, parts[2 * p], parts[2 * p + 1]) for p in range(slices)]
        )

    down_part = lax.dynamic_slice_in_dim(down_weight, core * part, part, axis=0)
    cot_all = lax.all_gather(cotangent, ("dp", "core"), axis=0, tiled=True)

    inputs_wide = inputs.astype(jnp.float32)
    normed_one = rms_apply(inputs_wide, gain_one_wide).astype(jnp.bfloat16)
    mixed_proj = dot(normed_one, qkv_full) + bias_full
    cosine, sine = rope_tables(positions, HD)
    cosine = cosine[:, None, :]
    sine = sine[:, None, :]
    query_rot = rotate(
        mixed_proj[:, :q_cols].reshape(token_count, QH, HD), cosine, sine
    ).astype(jnp.bfloat16)
    key_rot = rotate(
        mixed_proj[:, q_cols : q_cols + k_cols].reshape(token_count, KVH, HD), cosine, sine
    )
    key_rot = key_rot.astype(jnp.bfloat16).reshape(token_count, k_cols)
    value_low = mixed_proj[:, q_cols + k_cols :].astype(jnp.bfloat16)
    kv_all, gate_part, up_part = communicate(
        "kv_in",
        1,
        (Gather, PLANE, jnp.concatenate([key_rot, value_low], axis=1)),
        (Exchange, ROW, column_blocks(gate_weight)),
        (Exchange, ROW, column_blocks(up_weight)),
    )
    kv_all = kv_all.reshape(-1, 2 * k_cols)
    gate_part = gate_part.reshape(D, part)
    up_part = up_part.reshape(D, part)
    mine = lax.dynamic_slice_in_dim(span_order, 2 * slot, 2)
    q_rows = pad_heads(split_rows(query_rot * jnp.bfloat16(HD**-0.5)))
    q_pad = q_rows.transpose(0, 1, 3, 2)
    attended_cols, lse = attend(span_order, mine, kv_all, q_pad)
    attended_wide = join_rows(attended_cols)
    attended_low = attended_wide.astype(jnp.bfloat16)
    residual = inputs_wide + dot(attended_low, out_full)
    normed_two = rms_apply(residual, gain_two_wide).astype(jnp.bfloat16)

    (normed_all,) = communicate("normed_in", 2, (Gather, ROW, normed_two))
    normed_all = normed_all.reshape(-1, D)
    gate_proj = dot(normed_all, gate_part)
    up_proj = dot(normed_all, up_part)
    hidden_low = swiglu(gate_proj, up_proj).astype(jnp.bfloat16)
    out_sum = dot(hidden_low, down_part).astype(jnp.bfloat16)
    d_hidden = dot(cot_all, down_part, 1, 1)
    d_gate, d_up = jax.vjp(swiglu, gate_proj, up_proj)[1](d_hidden)
    d_gate = d_gate.astype(jnp.bfloat16)
    d_up = d_up.astype(jnp.bfloat16)
    d_norm_sum = (dot(d_gate, gate_part, 1, 1) + dot(d_up, up_part, 1, 1)).astype(jnp.bfloat16)
    down_grad = dot(hidden_low, cot_all, 0, 0).astype(jnp.bfloat16)
    gate_grad = dot(normed_all, d_gate, 0, 0).astype(jnp.bfloat16)
    up_grad = dot(normed_all, d_up, 0, 0).astype(jnp.bfloat16)
    blocks = (slices, 2, token_count, D)
    (d_normed_two,) = communicate("d_normed_out", 3, (Scatter, ROW, d_norm_sum.reshape(blocks)))
    chips = group_size(PLANE)
    shards = (slices, chips, own_rows // chips, part)
    gate_up = jnp.stack([gate_grad, up_grad]).reshape((2,) + shards)
    gate_up = lax.psum_scatter(gate_up, PLANE, scatter_dimension=2)
    down_grad = lax.psum_scatter(down_grad, PLANE, scatter_dimension=0, tiled=True)

    d_resid_part, gain_two_grad = jax.vjp(rms_apply, residual, gain_two_wide)[1](d_normed_two)
    d_residual = d_resid_part + cotangent.astype(jnp.float32)
    d_branch = d_residual.astype(jnp.bfloat16)
    d_attended = dot(d_branch, out_full, 1, 1).astype(jnp.bfloat16)
    row_delta = jnp.sum(
        (d_attended.astype(jnp.float32) * attended_wide).reshape(
            2, SPAN, KVH, GROUP, HD
        ),
        axis=-1,
    )
    row_delta = row_delta.transpose(0, 2, 3, 1).reshape(2, KVH, 1, GROUP * SPAN)
    do_rows = pad_heads(split_rows(d_attended))
    do_pad = do_rows.transpose(0, 1, 3, 2)
    d_query_cols, d_kv_all = attend_back(
        span_order, mine, kv_all, q_pad, q_rows, do_pad, do_rows, lse, row_delta
    )
    def turn_back(grads):
        scaled = grads * sine
        middle = HD // 2
        back = jnp.concatenate([scaled[..., middle:], -scaled[..., :middle]], axis=-1)
        return grads * cosine + back

    d_query_raw = turn_back(join_rows(d_query_cols).reshape(token_count, QH, HD))
    d_query_low = d_query_raw.reshape(token_count, q_cols).astype(jnp.bfloat16)
    d_kv, out_rows, d_query_all = communicate(
        "d_kv_out",
        4,
        (Scatter, PLANE, d_kv_all.reshape(chips, 2, token_count, 2 * k_cols)),
        (Scatter, ROW, out_sum.reshape(blocks)),
        (Gather, ROW, d_query_low),
    )
    output = (residual + out_rows).astype(jnp.bfloat16)
    d_key_raw = turn_back(d_kv[:, :k_cols].reshape(token_count, KVH, HD))
    d_kv_low = jnp.concatenate(
        [d_key_raw.reshape(token_count, k_cols), d_kv[:, k_cols:]], axis=1
    ).astype(jnp.bfloat16)
    d_mixed = jnp.concatenate([d_query_low, d_kv_low], axis=1)
    d_normed_one = dot(d_mixed, qkv_full, 1, 1)
    d_input_part, gain_one_grad = jax.vjp(rms_apply, inputs_wide, gain_one_wide)[1](d_normed_one)
    input_grad = (d_input_part + d_residual).astype(jnp.bfloat16)
    gain_grads = jnp.concatenate([gain_one_grad, gain_two_grad])
    gain_grads = jnp.pad(gain_grads, (0, 2048 - 2 * D)).reshape(16, 128)
    rows = own_rows // chips
    gate_up = jnp.pad(gate_up.transpose(1, 0, 2, 3), ((0, 0), (0, 0), (0, 16 - rows), (0, 0)))
    d_kv_rows, gain_grads, gate_up = communicate(
        "d_kv_in",
        5,
        (Gather, ROW, d_kv_low),
        (Gather, ROW, gain_grads),
        (Exchange, ROW, gate_up),
    )
    d_mixed_all = jnp.concatenate(
        [d_query_all.reshape(-1, q_cols), d_kv_rows.reshape(-1, 2 * k_cols)], axis=1
    )
    gain_grads = jnp.sum(gain_grads.reshape(2 * slices, -1), axis=0)
    bias_grad = jnp.sum(d_mixed_all.astype(jnp.float32), axis=0)

    half_rows = own_rows // 2
    first = dp * own_rows + core * half_rows

    def my_columns(tokens):
        everyone = lax.all_gather(tokens, ("dp", "core"), axis=0, tiled=True)
        return lax.dynamic_slice_in_dim(everyone, first, half_rows, axis=1)

    d_branch_all = lax.all_gather(d_branch, ("dp", "core"), axis=0, tiled=True)
    out_grad = dot(my_columns(attended_low), d_branch_all, 0, 0)
    qkv_grad = dot(my_columns(normed_one), d_mixed_all, 0, 0)
    width = chips * 128
    sums = jnp.concatenate(
        [
            jnp.concatenate([qkv_grad, out_grad], axis=1),
            jnp.pad(bias_grad, (0, width - bias_grad.shape[0]))[None],
            jnp.pad(gain_grads, (0, width - gain_grads.shape[0]))[None],
            jnp.zeros((14, width), jnp.float32),
        ],
        axis=0,
    ).astype(jnp.bfloat16)
    sums = sums.reshape(128, chips, 128).transpose(1, 0, 2)
    down_rows = down_grad.shape[0]
    down_grad = jnp.pad(down_grad, ((0, 48 - down_rows), (0, 0)))
    sums, gate_up, down_grad = communicate(
        "grads",
        6,
        (Total, PLANE, sums),
        (Gather, PLANE, gate_up),
        (Gather, PLANE, down_grad),
    )
    sums = sums.transpose(1, 2, 0, 3).reshape(2, 128, width).astype(jnp.float32)
    proj_grads = sums[:, :half_rows].reshape(own_rows, width)
    bias_grad = sums[0, half_rows]
    gain_grads = sums[0, half_rows + 1]

    def owned(vector, start, count):
        width = count // slices
        return lax.dynamic_slice_in_dim(vector, start + dp * width, width)

    gate_up = gate_up[:, :, :, :, :rows].transpose(3, 0, 4, 2, 1, 5)
    gate_up = gate_up.reshape(2, own_rows, FF).astype(jnp.float32)
    down_grad = down_grad[:, :, :down_rows].transpose(1, 0, 2, 3).reshape(-1, D)
    mixed_cols = q_cols + 2 * k_cols
    return (
        output,
        input_grad,
        owned(gain_grads, 0, D),
        proj_grads[:, :mixed_cols],
        owned(bias_grad, 0, q_cols + k_cols),
        owned(bias_grad, q_cols + k_cols, k_cols),
        proj_grads[:, mixed_cols:],
        owned(gain_grads, D, D),
        gate_up[0],
        gate_up[1],
        down_grad.astype(jnp.float32),
    )


def solution(mesh):
    grid = Mesh(mesh.devices.reshape(4, 4, 4, 2), ("dp", "z", "y", "core"))
    tokens = ("dp",) + CTX
    return jax.shard_map(
        body,
        mesh=grid,
        in_specs=(
            P(tokens, None),
            P(tokens, None),
            P(),
            P(tokens),
            P("dp"),
            P("dp", None),
            P("dp"),
            P("dp", None),
            P("dp"),
            P("dp", None),
            P("dp", None),
            P("dp", None),
        ),
        out_specs=(
            P(tokens, None),
            P(tokens, None),
            P("dp"),
            P("dp", None),
            P("dp"),
            P("dp"),
            P("dp", None),
            P("dp"),
            P("dp", None),
            P("dp", None),
            P("dp", None),
        ),
        check_vma=False,
    )
```

```python
import functools

import jax
import jax.numpy as jnp
from jax import lax
from jax.experimental import pallas as pl
from jax.experimental.pallas import tpu as pltpu
from jax.sharding import Mesh, PartitionSpec as P

QH = 14
KVH = 2
HD = 64
GROUP = QH // KVH
D = 896
FF = 4864
SPAN = 64
CHUNK = 256

norm_eps = 1e-06
rope_base = 1000000.0
masked_score = -1e30
CTX = ("z", "y", "core")
ROW = ("dp",)
PLANE = ("z", "y")

MESH = pl.DeviceIdType.MESH
SIZES = {"dp": 4, "z": 4, "y": 4}


def group_size(axes):
    size = 1
    for axis in axes:
        size *= SIZES[axis]
    return size


def group_index(axes):
    index = 0
    for axis in axes:
        index = index * SIZES[axis] + lax.axis_index(axis)
    return index


def member(axes, index):
    found = {}
    for axis in reversed(axes):
        found[axis] = index % SIZES[axis]
        index = index // SIZES[axis]
    return found


def remote(source, target, send, receive, device):
    return pltpu.make_async_remote_copy(
        src_ref=source,
        dst_ref=target,
        send_sem=send,
        recv_sem=receive,
        device_id=device,
        device_id_type=MESH,
    )


class Gather:
    def __init__(self, axes, array):
        self.axes, self.n = axes, group_size(axes)
        self.block, self.dtype = array.shape, array.dtype
        self.in_space = pl.ANY
        self.out = jax.ShapeDtypeStruct((self.n, 2) + self.block, self.dtype)
        self.out_space = pl.ANY
        self.scratch = [pltpu.SemaphoreType.DMA] + [pltpu.SemaphoreType.DMA((self.n,))] * 4

    def bind(self, source, target, scratch):
        self.x, self.o = source, target
        self.local, self.send, self.receive, self.f_send, self.f_receive = scratch
        self.me, self.core = group_index(self.axes), lax.axis_index("core")

    def mine(self):
        return pltpu.make_async_copy(self.x, self.o.at[self.me, self.core], self.local)

    def outward(self, k):
        device = member(self.axes, (self.me + k) % self.n)
        place = self.o.at[self.me, self.core]
        return remote(self.x, place, self.send.at[k], self.receive.at[k], device)

    def inward(self, k):
        device = member(self.axes, (self.me + k) % self.n)
        place = self.o.at[(self.me + self.n - k) % self.n, self.core]
        return remote(self.x, place, self.send.at[k], self.receive.at[k], device)

    def forward(self, k, core):
        place = self.o.at[(self.me + self.n - k) % self.n, core]
        source = self.x if k == 0 else place
        device = {"core": 1 - self.core}
        return remote(source, place, self.f_send.at[k], self.f_receive.at[k], device)

    def start(self):
        self.mine().start()
        for k in range(1, self.n):
            self.outward(k).start()
        self.forward(0, self.core).start()

    def middle(self):
        for k in range(1, self.n):
            self.inward(k).wait_recv()
            self.forward(k, self.core).start()

    def end(self):
        self.mine().wait()
        for k in range(self.n):
            if k:
                self.outward(k).wait_send()
            self.forward(k, self.core).wait_send()
            self.forward(k, 1 - self.core).wait_recv()


def split_point(rows):
    return rows if rows < 32 else (rows // 2 + 15) // 16 * 16


class RingGather:
    def __init__(self, axes, array):
        self.axes, self.n = axes, group_size(axes)
        self.block, self.dtype = array.shape, array.dtype
        self.cut = split_point(self.block[0])
        self.in_space = pl.ANY
        self.out = jax.ShapeDtypeStruct((self.n, 2) + self.block, self.dtype)
        self.out_space = pl.ANY
        self.scratch = [pltpu.SemaphoreType.DMA] + [pltpu.SemaphoreType.DMA((4,))] * 4

    def bind(self, source, target, scratch):
        self.x, self.o = source, target
        self.local, self.send, self.receive, self.f_send, self.f_receive = scratch
        self.me, self.core = group_index(self.axes), lax.axis_index("core")

    def at(self, shift, core):
        return self.o.at[(self.me + shift) % 4, core]

    def mine(self):
        return pltpu.make_async_copy(self.x, self.at(0, self.core), self.local)

    def copy(self, step, to, source, target):
        device = member(self.axes, (self.me + to) % 4)
        return remote(source, target, self.send.at[step], self.receive.at[step], device)

    def piece(self, shift, low):
        ref = self.at(shift, self.core)
        rows = pl.ds(0, self.cut) if low else pl.ds(self.cut, self.block[0] - self.cut)
        return ref.at[rows]

    def sends(self):
        place = self.at(0, self.core)
        low, high = self.piece(3, True), None
        found = [self.copy(0, 1, self.x, place), self.copy(1, 3, self.x, place)]
        found.append(self.copy(2, 1, low, low))
        if self.cut < self.block[0]:
            high = self.piece(1, False)
            found.append(self.copy(3, 3, high, high))
        return found

    def receipts(self):
        found = [
            self.copy(0, 1, self.x, self.at(3, self.core)),
            self.copy(1, 3, self.x, self.at(1, self.core)),
        ]
        low = self.piece(2, True)
        found.append(self.copy(2, 1, low, low))
        if self.cut < self.block[0]:
            high = self.piece(2, False)
            found.append(self.copy(3, 3, high, high))
        return found

    def forward(self, step, core):
        place = self.at((0, 3, 1, 2)[step], core)
        source = self.x if step == 0 else place
        device = {"core": 1 - self.core}
        return remote(source, place, self.f_send.at[step], self.f_receive.at[step], device)

    def start(self):
        sends = self.sends()
        sends[0].start()
        sends[1].start()
        self.mine().start()
        self.forward(0, self.core).start()

    def middle(self):
        sends, receipts = self.sends(), self.receipts()
        for step in range(2):
            receipts[step].wait_recv()
            if step + 2 < len(sends):
                sends[step + 2].start()
            self.forward(step + 1, self.core).start()

    def late(self):
        for receipt in self.receipts()[2:]:
            receipt.wait_recv()
        self.forward(3, self.core).start()

    def end(self):
        self.mine().wait()
        for send in self.sends():
            send.wait_send()
        for step in range(4):
            self.forward(step, self.core).wait_send()
            self.forward(step, 1 - self.core).wait_recv()


class RingExchange:
    def __init__(self, axes, array, share=False):
        self.axes, self.share = axes, share
        self.block = array.shape[1:]
        self.cut = split_point(self.block[0])
        self.in_space = pl.ANY
        middle = (2,) if share else ()
        self.out = jax.ShapeDtypeStruct((4,) + middle + self.block, array.dtype)
        self.out_space = pl.ANY
        rows = (self.cut, self.block[0] - self.cut)
        self.scratch = [pltpu.VMEM((count,) + self.block[1:], array.dtype) for count in rows]
        self.scratch += [pltpu.SemaphoreType.DMA] + [pltpu.SemaphoreType.DMA((6,))] * 2
        if share:
            self.scratch += [pltpu.SemaphoreType.DMA((4,))] * 2

    def bind(self, source, target, scratch):
        self.x, self.o = source, target
        self.via, (self.local, self.send, self.receive) = scratch[:2], scratch[2:5]
        self.shared = scratch[5:]
        self.me, self.core = group_index(self.axes), lax.axis_index("core")
        self.halves = (pl.ds(0, self.cut), pl.ds(self.cut, self.block[0] - self.cut))

    def at(self, shift, core=None):
        ref = self.o.at[(self.me + shift) % 4]
        return ref.at[self.core if core is None else core] if self.share else ref

    def copy(self, step, to, source, target):
        device = member(self.axes, (self.me + to) % 4)
        return remote(source, target, self.send.at[step], self.receive.at[step], device)

    def block_to(self, shift):
        return self.x.at[(self.me + shift) % 4]

    def mine(self):
        return pltpu.make_async_copy(self.block_to(0), self.at(0), self.local)

    def sends(self):
        low, high = self.halves
        return [
            self.copy(0, 1, self.block_to(2).at[low], self.via[0]),
            self.copy(1, 3, self.block_to(2).at[high], self.via[1]),
            self.copy(2, 1, self.block_to(1), self.at(0)),
            self.copy(3, 3, self.block_to(3), self.at(0)),
            self.copy(4, 1, self.via[0], self.at(3).at[low]),
            self.copy(5, 3, self.via[1], self.at(1).at[high]),
        ]

    def receipts(self):
        low, high = self.halves
        return [
            self.copy(0, 1, self.via[0], self.via[0]),
            self.copy(1, 3, self.via[1], self.via[1]),
            self.copy(2, 1, self.block_to(1), self.at(3)),
            self.copy(3, 3, self.block_to(3), self.at(1)),
            self.copy(4, 1, self.via[0], self.at(2).at[low]),
            self.copy(5, 3, self.via[1], self.at(2).at[high]),
        ]

    def forward(self, step, core):
        place = self.at((0, 3, 1, 2)[step], core)
        source = self.block_to(0) if step == 0 else place
        f_send, f_receive = self.shared
        device = {"core": 1 - self.core}
        return remote(source, place, f_send.at[step], f_receive.at[step], device)

    def start(self):
        for send in self.sends()[:4]:
            send.start()
        self.mine().start()
        if self.share:
            self.forward(0, self.core).start()

    def middle(self):
        sends, receipts = self.sends(), self.receipts()
        for step in range(2):
            receipts[step].wait_recv()
            sends[step + 4].start()

    def late(self):
        receipts = self.receipts()
        for step in range(2):
            receipts[step + 2].wait_recv()
            if self.share:
                self.forward(step + 1, self.core).start()
        receipts[4].wait_recv()
        receipts[5].wait_recv()
        if self.share:
            self.forward(3, self.core).start()

    def end(self):
        self.mine().wait()
        for send in self.sends():
            send.wait_send()
        if self.share:
            for step in range(4):
                self.forward(step, self.core).wait_send()
                self.forward(step, 1 - self.core).wait_recv()


class Swap:
    def __init__(self, axes, array):
        self.axes = axes
        self.in_space = pl.ANY
        self.out = jax.ShapeDtypeStruct((2,) + array.shape, array.dtype)
        self.out_space = pl.ANY
        self.scratch = [pltpu.SemaphoreType.DMA] * 3

    def bind(self, source, target, scratch):
        self.x, self.o = source, target
        self.local, self.send, self.receive = scratch
        self.core = lax.axis_index("core")

    def mine(self):
        return pltpu.make_async_copy(self.x, self.o.at[self.core], self.local)

    def across(self, core):
        place = self.o.at[core]
        return remote(self.x, place, self.send, self.receive, {"core": 1 - self.core})

    def start(self):
        self.across(self.core).start()
        self.mine().start()

    def middle(self):
        pass

    def late(self):
        pass

    def end(self):
        self.mine().wait()
        self.across(self.core).wait_send()
        self.across(1 - self.core).wait_recv()


class RingScatter:
    def __init__(self, axes, array):
        self.axes = axes
        self.block = array.shape[2:]
        self.cut = split_point(self.block[0])
        self.in_space = pltpu.VMEM
        self.out = jax.ShapeDtypeStruct(self.block, jnp.float32)
        self.out_space = pltpu.VMEM
        rows = (self.cut, self.block[0] - self.cut)
        self.scratch = [pltpu.VMEM((4,) + self.block, array.dtype)] * 2
        self.scratch += [pltpu.VMEM((count,) + self.block[1:], array.dtype) for count in rows]
        self.scratch += [pltpu.VMEM((2,) + self.block, array.dtype)]
        self.scratch += [pltpu.SemaphoreType.DMA((4,))] * 4

    def bind(self, source, target, scratch):
        self.x, self.o = source, target
        self.half, self.summed = scratch[:2]
        self.via, self.land = scratch[2:4], scratch[4]
        self.s_one, self.r_one, self.send, self.receive = scratch[5:]
        self.me, self.core = group_index(self.axes), lax.axis_index("core")

    def across(self, shift):
        to = (self.me + shift) % 4
        return remote(
            self.x.at[to, 1 - self.core],
            self.half.at[to],
            self.s_one.at[shift],
            self.r_one.at[shift],
            {"core": 1 - self.core},
        )

    def copy(self, step, to, source, target):
        device = member(self.axes, (self.me + to) % 4)
        return remote(source, target, self.send.at[step], self.receive.at[step], device)

    def copies(self):
        far = self.summed.at[(self.me + 2) % 4]
        low, high = pl.ds(0, self.cut), pl.ds(self.cut, self.block[0] - self.cut)
        return [
            self.copy(0, 1, far.at[low], self.via[0]),
            self.copy(1, 3, far.at[high], self.via[1]),
            self.copy(2, 1, self.summed.at[(self.me + 1) % 4], self.land.at[0]),
            self.copy(3, 3, self.summed.at[(self.me + 3) % 4], self.land.at[1]),
        ]

    def both(self, shift):
        self.across(shift).wait_recv()
        to = (self.me + shift) % 4
        return self.x[to, self.core].astype(jnp.float32) + self.half[to].astype(jnp.float32)

    def start(self):
        for shift in (2, 1, 3, 0):
            self.across(shift).start()

    def middle(self):
        copies = self.copies()
        kind = self.summed.dtype
        self.summed[(self.me + 2) % 4] = self.both(2).astype(kind)
        copies[0].start()
        copies[1].start()
        near, back = self.both(1), self.both(3)
        cut = self.cut
        after, before = (self.me + 1) % 4, (self.me + 3) % 4
        copies[0].wait_recv()
        self.summed[after, :cut] = (near[:cut] + self.via[0][...].astype(jnp.float32)).astype(kind)
        self.summed[after, cut:] = near[cut:].astype(kind)
        copies[2].start()
        copies[1].wait_recv()
        self.summed[before, cut:] = (back[cut:] + self.via[1][...].astype(jnp.float32)).astype(kind)
        self.summed[before, :cut] = back[:cut].astype(kind)
        copies[3].start()
        self.o[...] = self.both(0)

    def late(self):
        pass

    def end(self):
        copies = self.copies()
        for step in range(2):
            copies[step + 2].wait_recv()
            self.o[...] += self.land[step].astype(jnp.float32)
        for shift in range(4):
            self.across(shift).wait_send()
            copies[shift].wait_send()


class Scatter:
    def __init__(self, axes, array):
        self.axes, self.n = axes, group_size(axes)
        self.block = array.shape[2:]
        self.in_space = pltpu.VMEM
        self.out = jax.ShapeDtypeStruct(self.block, jnp.float32)
        self.out_space = pltpu.VMEM
        buffer = pltpu.VMEM((self.n,) + self.block, array.dtype)
        self.scratch = [buffer] * 3 + [pltpu.SemaphoreType.DMA((self.n,))] * 4

    def bind(self, source, target, scratch):
        self.x, self.o = source, target
        self.half, self.summed, self.land = scratch[:3]
        self.s_one, self.r_one, self.s_two, self.r_two = scratch[3:]
        self.me, self.core = group_index(self.axes), lax.axis_index("core")

    def across(self, k):
        to = (self.me + k + 1) % self.n
        return remote(
            self.x.at[to, 1 - self.core],
            self.half.at[to],
            self.s_one.at[k],
            self.r_one.at[k],
            {"core": 1 - self.core},
        )

    def outward(self, k, slot):
        to = (self.me + k + 1) % self.n
        return remote(
            self.summed.at[to],
            self.land.at[slot],
            self.s_two.at[k],
            self.r_two.at[k],
            member(self.axes, to),
        )

    def start(self):
        for k in range(self.n):
            self.across(k).start()

    def middle(self):
        for k in range(self.n):
            to = (self.me + k + 1) % self.n
            self.across(k).wait_recv()
            both = self.x[to, self.core].astype(jnp.float32) + self.half[to].astype(jnp.float32)
            if k == self.n - 1:
                self.o[...] = both
            else:
                self.summed[to] = both.astype(self.summed.dtype)
                self.outward(k, self.me).start()

    def end(self):
        for k in range(self.n - 1):
            source = (self.me + self.n - k - 1) % self.n
            self.outward(k, source).wait_recv()
            self.o[...] += self.land[source].astype(jnp.float32)
        for k in range(self.n):
            self.across(k).wait_send()
            if k < self.n - 1:
                self.outward(k, self.me).wait_send()


class Total:
    def __init__(self, axes, array):
        self.axes, self.n = axes, group_size(axes)
        self.block = array.shape[1:]
        self.in_space = pltpu.VMEM
        own = jax.ShapeDtypeStruct(self.block, array.dtype)
        self.gather = Gather(axes, own)
        self.out, self.out_space = self.gather.out, self.gather.out_space
        self.scratch = [
            pltpu.VMEM((self.n,) + self.block, array.dtype),
            pltpu.VMEM(self.block, array.dtype),
            pltpu.SemaphoreType.DMA((self.n,)),
            pltpu.SemaphoreType.DMA((self.n,)),
        ] + self.gather.scratch

    def bind(self, source, target, scratch):
        self.x = source
        self.land, self.own, self.send, self.receive = scratch[:4]
        self.gather.bind(self.own, target, scratch[4:])
        self.me = self.gather.me

    def outward(self, k, slot):
        to = (self.me + k) % self.n
        return remote(
            self.x.at[to],
            self.land.at[slot],
            self.send.at[k],
            self.receive.at[k],
            member(self.axes, to),
        )

    def start(self):
        for k in range(1, self.n):
            self.outward(k, self.me).start()

    def middle(self):
        total = self.x[self.me].astype(jnp.float32)
        for k in range(1, self.n):
            source = (self.me + self.n - k) % self.n
            self.outward(k, source).wait_recv()
            total += self.land[source].astype(jnp.float32)
        self.own[...] = total.astype(self.own.dtype)
        self.gather.start()
        self.gather.middle()

    def end(self):
        self.gather.end()
        for k in range(1, self.n):
            self.outward(k, self.me).wait_send()


def communicate_kernel(ops, compute, inputs, outputs, *refs):
    count = len(ops)
    extra = refs[count : count + inputs]
    refs = refs[:count] + refs[count + inputs :]
    extra += refs[2 * count : 2 * count + outputs]
    scratch = list(refs[2 * count + outputs :])
    groups = []
    for index, op in enumerate(ops):
        used = [scratch.pop(0) for unused in op.scratch]
        op.bind(refs[index], refs[count + index], used)
        if op.axes not in groups:
            groups.append(op.axes)
    barrier = pltpu.get_barrier_semaphore()
    devices = [{"core": 1 - lax.axis_index("core")}]
    for axes in groups:
        n, me = group_size(axes), group_index(axes)
        devices += [member(axes, (me + k) % n) for k in range(1, n)]
    for device in devices:
        pl.semaphore_signal(barrier, inc=1, device_id=device, device_id_type=MESH)
    pl.semaphore_wait(barrier, len(devices))
    for op in ops:
        op.start()
    for op in ops:
        op.middle()
    if compute is not None:
        compute(*extra)
    for op in ops:
        if hasattr(op, "late"):
            op.late()
    for op in ops:
        op.end()


def communicate(name, identity, *requests, compute=None, inputs=(), outputs=()):
    arrays = [array for kind, axes, array in requests]
    ops = [kind(axes, array) for kind, axes, array in requests]
    vmem = pl.BlockSpec(memory_space=pltpu.VMEM)
    return pl.pallas_call(
        functools.partial(communicate_kernel, ops, compute, len(inputs), len(outputs)),
        out_shape=tuple(op.out for op in ops) + tuple(outputs),
        in_specs=[pl.BlockSpec(memory_space=op.in_space) for op in ops] + [vmem] * len(inputs),
        out_specs=tuple(pl.BlockSpec(memory_space=op.out_space) for op in ops)
        + (vmem,) * len(outputs),
        scratch_shapes=[item for op in ops for item in op.scratch],
        compiler_params=pltpu.CompilerParams(
            collective_id=identity,
            has_side_effects=True,
            vmem_limit_bytes=56 * 1024 * 1024,
        ),
        cost_estimate=pl.CostEstimate(flops=0, bytes_accessed=60_000_000, transcendentals=0),
        name=name,
    )(*arrays, *inputs)


def weight_grads(normed_ref, cot_ref, hidden_ref, d_gate_ref, d_up_ref, gate_ref, up_ref, down_ref):
    def step(index, unused):
        place = pl.ds(pl.multiple_of(index * 128, 128), 128)
        normed = normed_ref[:, place]
        gate_ref[place, :] = dot(normed, d_gate_ref[...], 0, 0).astype(jnp.bfloat16)
        up_ref[place, :] = dot(normed, d_up_ref[...], 0, 0).astype(jnp.bfloat16)
        down = dot(cot_ref[:, place], hidden_ref[...], 0, 0)
        down_ref[:, place] = down.T.astype(jnp.bfloat16)
        return unused

    lax.fori_loop(0, D // 128, step, 0)


def widen_kernel(gate_ref, up_ref, gate_out_ref, up_out_ref):
    part = gate_ref.shape[-1]
    for source, target in ((gate_ref, gate_out_ref), (up_ref, up_out_ref)):
        for index in range(gate_ref.shape[0]):
            target[:, part * index : part * (index + 1)] = source[index].astype(jnp.float32)


def widen(gate, up):
    count, rows, part = gate.shape
    step = 32
    source = pl.BlockSpec((count, step, part), lambda index: (0, index, 0))
    target = pl.BlockSpec((step, count * part), lambda index: (index, 0))
    wide = jax.ShapeDtypeStruct((rows, count * part), jnp.float32)
    return pl.pallas_call(
        widen_kernel,
        grid=(rows // step,),
        out_shape=(wide, wide),
        in_specs=[source, source],
        out_specs=(target, target),
        name="widen",
    )(gate, up)


def rms_apply(values, gain):
    mean_square = jnp.mean(values * values, axis=-1, keepdims=True)
    return values * lax.rsqrt(mean_square + norm_eps) * gain


def half_turn(values):
    middle = values.shape[-1] // 2
    return jnp.concatenate([-values[..., middle:], values[..., :middle]], axis=-1)


def rotate(values, cosine, sine):
    return values * cosine + half_turn(values) * sine


def rope_tables(positions, head_dim):
    middle = head_dim // 2
    inverse = rope_base ** (-(jnp.arange(middle).astype(jnp.float32) * 2.0) / head_dim)
    angles = positions.astype(jnp.float32)[:, None] * inverse[None, :]
    angles = jnp.concatenate([angles, angles], axis=-1)
    return (jnp.cos(angles), jnp.sin(angles))


def swiglu(gate_in, up_in):
    return jax.nn.silu(gate_in) * up_in


def dot(a, b, ca=1, cb=0):
    return lax.dot_general(a, b, (((ca,), (cb,)), ((), ())), preferred_element_type=jnp.float32)


def causal_copy(order_ref, kv_ref, sorted_ref):
    def move(slot, unused):
        source = pl.multiple_of(slot * SPAN, SPAN)
        target = pl.multiple_of(order_ref[slot] * SPAN, SPAN)
        sorted_ref[pl.ds(target, SPAN), :] = kv_ref[pl.ds(source, SPAN), :]
        return unused

    lax.fori_loop(0, kv_ref.shape[0] // SPAN, move, 0)


def visible(start, place, rows):
    key_place = lax.broadcasted_iota(jnp.int32, (CHUNK, rows), 0) + start
    lane = lax.broadcasted_iota(jnp.int32, (CHUNK, rows), 1)
    return key_place <= place * SPAN + lane % SPAN


def attend_kernel(order_ref, mine_ref, kv_ref, q_ref, out_ref, lse_ref, sorted_ref):
    causal_copy(order_ref, kv_ref, sorted_ref)
    rows = q_ref.shape[-1]
    for half in range(2):
        place = mine_ref[half]
        last = place * SPAN // CHUNK

        def step(index, carry, masked, half=half, place=place):
            start = pl.multiple_of(index * CHUNK, CHUNK)
            keys = sorted_ref[pl.ds(start, CHUNK), :128]
            values = sorted_ref[pl.ds(start, CHUNK), 128:]
            result = []
            for head in range(KVH):
                top, total, mixed = carry[head]
                scores = dot(keys, q_ref[half, head])
                if masked:
                    scores = jnp.where(visible(start, place, rows), scores, masked_score)
                new_top = jnp.maximum(top, jnp.max(scores, axis=0, keepdims=True))
                shrink = jnp.exp(top - new_top)
                weights = jnp.exp(scores - new_top)
                total = total * shrink + jnp.sum(weights, axis=0, keepdims=True)
                mixed = mixed * shrink + dot(values, weights.astype(jnp.bfloat16), 0, 0)
                result.append((new_top, total, mixed))
            return tuple(result)

        empty = tuple(
            (
                jnp.full((1, rows), masked_score, jnp.float32),
                jnp.zeros((1, rows), jnp.float32),
                jnp.zeros((128, rows), jnp.float32),
            )
            for head in range(KVH)
        )
        carry = lax.fori_loop(0, last, functools.partial(step, masked=False), empty)
        carry = step(last, carry, True)
        for head in range(KVH):
            top, total, mixed = carry[head]
            out_ref[half, head] = mixed[head * HD : (head + 1) * HD] / total
            lse_ref[half, head] = top + jnp.log(total)


def attend(order, mine, kv_all, q_pad):
    halves, heads, unused, rows = q_pad.shape
    smem = pl.BlockSpec(memory_space=pltpu.SMEM)
    vmem = pl.BlockSpec(memory_space=pltpu.VMEM)
    return pl.pallas_call(
        attend_kernel,
        out_shape=(
            jax.ShapeDtypeStruct((halves, heads, HD, rows), jnp.float32),
            jax.ShapeDtypeStruct((halves, heads, 1, rows), jnp.float32),
        ),
        in_specs=[smem, smem, vmem, vmem],
        out_specs=(vmem, vmem),
        scratch_shapes=[pltpu.VMEM(kv_all.shape, kv_all.dtype)],
        compiler_params=pltpu.CompilerParams(vmem_limit_bytes=48 * 1024 * 1024),
        cost_estimate=pl.CostEstimate(
            flops=3_000_000_000, bytes_accessed=6_000_000, transcendentals=4_000_000
        ),
        name="attend",
    )(order, mine, kv_all, q_pad)


def attend_back_kernel(
    order_ref,
    mine_ref,
    kv_ref,
    q_ref,
    q_rows_ref,
    do_ref,
    do_rows_ref,
    lse_ref,
    delta_ref,
    dq_ref,
    dkv_ref,
    sorted_ref,
    sum_ref,
):
    causal_copy(order_ref, kv_ref, sorted_ref)
    sum_ref[...] = jnp.zeros_like(sum_ref)
    rows = q_ref.shape[-1]
    for half in range(2):
        place = mine_ref[half]
        last = place * SPAN // CHUNK

        def step(index, carry, masked, half=half, place=place):
            start = pl.multiple_of(index * CHUNK, CHUNK)
            keys = sorted_ref[pl.ds(start, CHUNK), :128]
            values = sorted_ref[pl.ds(start, CHUNK), 128:]
            d_keys = sum_ref[pl.ds(start, CHUNK), :128]
            d_values = sum_ref[pl.ds(start, CHUNK), 128:]
            result = []
            for head in range(KVH):
                scores = dot(keys, q_ref[half, head])
                probs = jnp.exp(scores - lse_ref[half, head])
                if masked:
                    probs = jnp.where(visible(start, place, rows), probs, 0.0)
                d_probs = dot(values, do_ref[half, head])
                d_scores = (probs * (d_probs - delta_ref[half, head])).astype(jnp.bfloat16)
                d_values += dot(probs.astype(jnp.bfloat16), do_rows_ref[half, head])
                d_keys += dot(d_scores, q_rows_ref[half, head])
                result.append(carry[head] + dot(keys, d_scores, 0, 0))
            sum_ref[pl.ds(start, CHUNK), :128] = d_keys
            sum_ref[pl.ds(start, CHUNK), 128:] = d_values
            return tuple(result)

        empty = tuple(jnp.zeros((128, rows), jnp.float32) for head in range(KVH))
        carry = lax.fori_loop(0, last, functools.partial(step, masked=False), empty)
        carry = step(last, carry, True)
        for head in range(KVH):
            dq_ref[half, head] = carry[head][head * HD : (head + 1) * HD] * (HD**-0.5)

    def move(slot, unused):
        target = pl.multiple_of(slot * SPAN, SPAN)
        source = pl.multiple_of(order_ref[slot] * SPAN, SPAN)
        dkv_ref[pl.ds(target, SPAN), :] = sum_ref[pl.ds(source, SPAN), :].astype(jnp.bfloat16)
        return unused

    lax.fori_loop(0, dkv_ref.shape[0] // SPAN, move, 0)


def attend_back(order, mine, kv_all, q_pad, q_rows, do_pad, do_rows, lse, delta):
    halves, heads, unused, rows = q_pad.shape
    smem = pl.BlockSpec(memory_space=pltpu.SMEM)
    vmem = pl.BlockSpec(memory_space=pltpu.VMEM)
    return pl.pallas_call(
        attend_back_kernel,
        out_shape=(
            jax.ShapeDtypeStruct((halves, heads, HD, rows), jnp.float32),
            jax.ShapeDtypeStruct(kv_all.shape, jnp.bfloat16),
        ),
        in_specs=[smem, smem] + [vmem] * 7,
        out_specs=(vmem, vmem),
        scratch_shapes=[
            pltpu.VMEM(kv_all.shape, kv_all.dtype),
            pltpu.VMEM(kv_all.shape, jnp.float32),
        ],
        compiler_params=pltpu.CompilerParams(vmem_limit_bytes=48 * 1024 * 1024),
        cost_estimate=pl.CostEstimate(
            flops=8_000_000_000, bytes_accessed=9_000_000, transcendentals=4_000_000
        ),
        name="attend_back",
    )(order, mine, kv_all, q_pad, q_rows, do_pad, do_rows, lse, delta)


def split_rows(tokens):
    parts = tokens.reshape(2, SPAN, KVH, GROUP, HD)
    return parts.transpose(0, 2, 3, 1, 4).reshape(2, KVH, GROUP * SPAN, HD)


def pad_heads(rows):
    return jnp.stack(
        [
            jnp.pad(rows[:, 0], ((0, 0), (0, 0), (0, HD))),
            jnp.pad(rows[:, 1], ((0, 0), (0, 0), (HD, 0))),
        ],
        axis=1,
    )


def join_rows(columns):
    parts = columns.reshape(2, KVH, HD, GROUP, SPAN)
    return parts.transpose(0, 4, 1, 3, 2).reshape(2 * SPAN, QH * HD)


def body(
    inputs,
    cotangent,
    span_order,
    positions,
    attn_gain,
    qkv_weight,
    qkv_bias,
    out_weight,
    mlp_gain,
    gate_weight,
    up_weight,
    down_weight,
):
    token_count = inputs.shape[0]
    q_cols = QH * HD
    k_cols = KVH * HD
    slices = lax.axis_size("dp")
    own_rows = D // slices
    part = FF // (slices * 2)
    dp = lax.axis_index("dp")
    core = lax.axis_index("core")
    slot = (lax.axis_index("z") * lax.axis_size("y") + lax.axis_index("y")) * 2 + core

    small = jnp.concatenate([attn_gain, mlp_gain, qkv_bias])
    small = jnp.pad(small, (0, 2048 - small.shape[0])).reshape(16, 128)
    qkv_half = lax.dynamic_slice_in_dim(qkv_weight, core * (own_rows // 2), own_rows // 2)
    qkv_full, small = communicate(
        "qkv_in", 0, (RingGather, ROW, qkv_half), (RingGather, ROW, small)
    )
    qkv_full = qkv_full.reshape(D, -1)
    small = small[:, 0].reshape(slices, -1)
    gain_one_wide = small[:, :own_rows].reshape(D).astype(jnp.float32)
    gain_two_wide = small[:, own_rows : 2 * own_rows].reshape(D).astype(jnp.float32)
    bias_full = small[:, 2 * own_rows : 2 * own_rows + qkv_bias.shape[0]]
    bias_full = bias_full.reshape(-1).astype(jnp.float32)
    out_full = lax.all_gather(out_weight, "dp", axis=0, tiled=True)

    def column_blocks(weight):
        parts = [weight[:, part * index : part * (index + 1)] for index in range(2 * slices)]
        return jnp.stack(
            [jnp.where(core == 0, parts[2 * p], parts[2 * p + 1]) for p in range(slices)]
        )

    down_part = lax.dynamic_slice_in_dim(down_weight, core * part, part, axis=0)
    cot_all = lax.all_gather(cotangent, ("dp", "core"), axis=0, tiled=True)

    inputs_wide = inputs.astype(jnp.float32)
    normed_one = rms_apply(inputs_wide, gain_one_wide).astype(jnp.bfloat16)
    normed_one_all = lax.all_gather(normed_one, ("dp", "core"), axis=0, tiled=True)
    mixed_proj = dot(normed_one, qkv_full) + bias_full
    cosine, sine = rope_tables(positions, HD)
    cosine = cosine[:, None, :]
    sine = sine[:, None, :]
    query_rot = rotate(
        mixed_proj[:, :q_cols].reshape(token_count, QH, HD), cosine, sine
    ).astype(jnp.bfloat16)
    key_rot = rotate(
        mixed_proj[:, q_cols : q_cols + k_cols].reshape(token_count, KVH, HD), cosine, sine
    )
    key_rot = key_rot.astype(jnp.bfloat16).reshape(token_count, k_cols)
    value_low = mixed_proj[:, q_cols + k_cols :].astype(jnp.bfloat16)
    kv_all, gate_part, up_part = communicate(
        "kv_in",
        1,
        (Gather, PLANE, jnp.concatenate([key_rot, value_low], axis=1)),
        (RingExchange, ROW, column_blocks(gate_weight)),
        (RingExchange, ROW, column_blocks(up_weight)),
    )
    kv_all = kv_all.reshape(-1, 2 * k_cols)
    gate_part = gate_part.reshape(D, part)
    up_part = up_part.reshape(D, part)
    mine = lax.dynamic_slice_in_dim(span_order, 2 * slot, 2)
    q_rows = pad_heads(split_rows(query_rot * jnp.bfloat16(HD**-0.5)))
    q_pad = q_rows.transpose(0, 1, 3, 2)
    attended_cols, lse = attend(span_order, mine, kv_all, q_pad)
    attended_wide = join_rows(attended_cols)
    attended_low = attended_wide.astype(jnp.bfloat16)
    attended_all = lax.all_gather(attended_low, ("dp", "core"), axis=0, tiled=True)
    residual = inputs_wide + dot(attended_low, out_full)
    normed_two = rms_apply(residual, gain_two_wide).astype(jnp.bfloat16)

    (normed_two, normed_one_all) = lax.optimization_barrier((normed_two, normed_one_all))
    (normed_all,) = communicate("normed_in", 2, (RingGather, ROW, normed_two))
    normed_all = normed_all.reshape(-1, D)
    gate_proj = dot(normed_all, gate_part)
    up_proj = dot(normed_all, up_part)
    hidden_low = swiglu(gate_proj, up_proj).astype(jnp.bfloat16)
    out_sum = dot(hidden_low, down_part).astype(jnp.bfloat16)
    d_hidden = dot(cot_all, down_part, 1, 1)
    d_gate, d_up = jax.vjp(swiglu, gate_proj, up_proj)[1](d_hidden)
    d_gate = d_gate.astype(jnp.bfloat16)
    d_up = d_up.astype(jnp.bfloat16)
    d_norm_sum = (dot(d_gate, gate_part, 1, 1) + dot(d_up, up_part, 1, 1)).astype(jnp.bfloat16)
    blocks = (slices, 2, token_count, D)
    low = functools.partial(jax.ShapeDtypeStruct, dtype=jnp.bfloat16)
    d_normed_two, out_rows, gate_grad, up_grad, down_grad = communicate(
        "d_normed_out",
        3,
        (RingScatter, ROW, d_norm_sum.reshape(blocks)),
        (RingScatter, ROW, out_sum.reshape(blocks)),
        compute=weight_grads,
        inputs=(normed_all, cot_all, hidden_low, d_gate, d_up),
        outputs=(low((D, part)), low((D, part)), low((part, D))),
    )
    output = (residual + out_rows).astype(jnp.bfloat16)
    chips = group_size(PLANE)
    gate_grad, up_grad, down_grad = lax.psum((gate_grad, up_grad, down_grad), PLANE)

    d_resid_part, gain_two_grad = jax.vjp(rms_apply, residual, gain_two_wide)[1](d_normed_two)
    d_residual = d_resid_part + cotangent.astype(jnp.float32)
    d_branch = d_residual.astype(jnp.bfloat16)
    d_attended = dot(d_branch, out_full, 1, 1).astype(jnp.bfloat16)
    d_attended, attended_all = lax.optimization_barrier((d_attended, attended_all))
    row_delta = jnp.sum(
        (d_attended.astype(jnp.float32) * attended_wide).reshape(
            2, SPAN, KVH, GROUP, HD
        ),
        axis=-1,
    )
    row_delta = row_delta.transpose(0, 2, 3, 1).reshape(2, KVH, 1, GROUP * SPAN)
    do_rows = pad_heads(split_rows(d_attended))
    do_pad = do_rows.transpose(0, 1, 3, 2)
    d_query_cols, d_kv_all = attend_back(
        span_order, mine, kv_all, q_pad, q_rows, do_pad, do_rows, lse, row_delta
    )
    def turn_back(grads):
        scaled = grads * sine
        middle = HD // 2
        back = jnp.concatenate([scaled[..., middle:], -scaled[..., :middle]], axis=-1)
        return grads * cosine + back

    d_query_raw = turn_back(join_rows(d_query_cols).reshape(token_count, QH, HD))
    d_query_low = d_query_raw.reshape(token_count, q_cols).astype(jnp.bfloat16)
    d_kv, d_query_all, d_branch_all = communicate(
        "d_kv_out",
        4,
        (Scatter, PLANE, d_kv_all.reshape(chips, 2, token_count, 2 * k_cols)),
        (RingGather, ROW, d_query_low),
        (RingGather, ROW, d_branch),
    )
    d_key_raw = turn_back(d_kv[:, :k_cols].reshape(token_count, KVH, HD))
    d_kv_low = jnp.concatenate(
        [d_key_raw.reshape(token_count, k_cols), d_kv[:, k_cols:]], axis=1
    ).astype(jnp.bfloat16)
    d_mixed = jnp.concatenate([d_query_low, d_kv_low], axis=1)
    d_normed_one = dot(d_mixed, qkv_full, 1, 1)
    d_input_part, gain_one_grad = jax.vjp(rms_apply, inputs_wide, gain_one_wide)[1](d_normed_one)
    input_grad = (d_input_part + d_residual).astype(jnp.bfloat16)
    gain_grads = jnp.concatenate([gain_one_grad, gain_two_grad])
    gain_grads = jnp.pad(gain_grads, (0, 2048 - 2 * D)).reshape(16, 128)
    d_kv_rows, gain_grads = communicate(
        "d_kv_in", 5, (RingGather, ROW, d_kv_low), (RingGather, ROW, gain_grads)
    )
    d_mixed_all = jnp.concatenate(
        [d_query_all.reshape(-1, q_cols), d_kv_rows.reshape(-1, 2 * k_cols)], axis=1
    )
    gain_grads = jnp.sum(gain_grads.reshape(2 * slices, -1), axis=0)
    bias_grad = jnp.sum(d_mixed_all.astype(jnp.float32), axis=0)

    half_rows = own_rows // 2
    first = dp * own_rows + core * half_rows

    def my_columns(tokens):
        return lax.dynamic_slice_in_dim(tokens, first, half_rows, axis=1)

    out_grad = dot(my_columns(attended_all), d_branch_all.reshape(-1, D), 0, 0)
    qkv_grad = dot(my_columns(normed_one_all), d_mixed_all, 0, 0)
    width = chips * 128
    sums = jnp.concatenate(
        [
            jnp.concatenate([qkv_grad, out_grad], axis=1),
            jnp.pad(bias_grad, (0, width - bias_grad.shape[0]))[None],
            jnp.pad(gain_grads, (0, width - gain_grads.shape[0]))[None],
            jnp.zeros((14, width), jnp.float32),
        ],
        axis=0,
    ).astype(jnp.bfloat16)
    sums = sums.reshape(128, chips, 128).transpose(1, 0, 2)
    shared = functools.partial(RingExchange, share=True)
    row_blocks = (slices, own_rows, part)
    gate_grad, up_grad, sums, down_grad = communicate(
        "grads",
        6,
        (shared, ROW, gate_grad.reshape(row_blocks)),
        (shared, ROW, up_grad.reshape(row_blocks)),
        (Total, PLANE, sums),
        (Swap, ROW, down_grad),
    )
    sums = sums.transpose(1, 2, 0, 3).reshape(2, 128, width).astype(jnp.float32)
    proj_grads = sums[:, :half_rows].reshape(own_rows, width)
    bias_grad = sums[0, half_rows]
    gain_grads = sums[0, half_rows + 1]

    def owned(vector, start, count):
        width = count // slices
        return lax.dynamic_slice_in_dim(vector, start + dp * width, width)

    gate_grad, up_grad = widen(
        gate_grad.reshape(-1, own_rows, part), up_grad.reshape(-1, own_rows, part)
    )
    down_grad = down_grad.reshape(-1, D)
    mixed_cols = q_cols + 2 * k_cols
    return (
        output,
        input_grad,
        owned(gain_grads, 0, D),
        proj_grads[:, :mixed_cols],
        owned(bias_grad, 0, q_cols + k_cols),
        owned(bias_grad, q_cols + k_cols, k_cols),
        proj_grads[:, mixed_cols:],
        owned(gain_grads, D, D),
        gate_grad,
        up_grad,
        down_grad.astype(jnp.float32),
    )


def solution(mesh):
    grid = Mesh(mesh.devices.reshape(4, 4, 4, 2), ("dp", "z", "y", "core"))
    tokens = ("dp",) + CTX
    return jax.shard_map(
        body,
        mesh=grid,
        in_specs=(
            P(tokens, None),
            P(tokens, None),
            P(),
            P(tokens),
            P("dp"),
            P("dp", None),
            P("dp"),
            P("dp", None),
            P("dp"),
            P("dp", None),
            P("dp", None),
            P("dp", None),
        ),
        out_specs=(
            P(tokens, None),
            P(tokens, None),
            P("dp"),
            P("dp", None),
            P("dp"),
            P("dp"),
            P("dp", None),
            P("dp"),
            P("dp", None),
            P("dp", None),
            P("dp", None),
        ),
        check_vma=False,
    )
```

```python
import functools

import jax
import jax.numpy as jnp
from jax import lax
from jax.experimental import pallas as pl
from jax.experimental.pallas import tpu as pltpu
from jax.sharding import Mesh, PartitionSpec as P

QH = 14
KVH = 2
HD = 64
GROUP = QH // KVH
D = 896
FF = 4864
SPAN = 64
CHUNK = 256

norm_eps = 1e-06
rope_base = 1000000.0
masked_score = -1e30
CTX = ("z", "y", "core")
ROW = ("dp",)
PLANE = ("z", "y")
ENALP = ("y", "z")

MESH = pl.DeviceIdType.MESH
SIZES = {"dp": 4, "z": 4, "y": 4}


def group_size(axes):
    size = 1
    for axis in axes:
        size *= SIZES[axis]
    return size


def group_index(axes):
    index = 0
    for axis in axes:
        index = index * SIZES[axis] + lax.axis_index(axis)
    return index


def member(axes, index):
    found = {}
    for axis in reversed(axes):
        found[axis] = index % SIZES[axis]
        index = index // SIZES[axis]
    return found


def remote(source, target, send, receive, device):
    return pltpu.make_async_remote_copy(
        src_ref=source,
        dst_ref=target,
        send_sem=send,
        recv_sem=receive,
        device_id=device,
        device_id_type=MESH,
    )


class Exchange:
    def __init__(self, axes, array):
        self.axes, self.n = axes, group_size(axes)
        self.in_space = pltpu.VMEM
        self.out = jax.ShapeDtypeStruct(array.shape, array.dtype)
        self.out_space = pl.ANY
        self.scratch = [pltpu.SemaphoreType.DMA] + [pltpu.SemaphoreType.DMA((self.n,))] * 2

    def bind(self, source, target, scratch):
        self.x, self.o = source, target
        self.local, self.send, self.receive = scratch
        self.me = group_index(self.axes)
        self.stages = [self.start, self.end]

    def mine(self):
        return pltpu.make_async_copy(self.x.at[self.me], self.o.at[self.me], self.local)

    def outward(self, k, slot):
        to = (self.me + k) % self.n
        device = member(self.axes, to)
        send, receive = self.send.at[k], self.receive.at[k]
        return remote(self.x.at[to], self.o.at[slot], send, receive, device)

    def start(self):
        self.mine().start()
        for k in range(1, self.n):
            self.outward(k, self.me).start()

    def end(self):
        self.mine().wait()
        for k in range(1, self.n):
            self.outward(k, self.me).wait_send()
            self.outward(k, (self.me + self.n - k) % self.n).wait_recv()


class PlaneGather:
    def __init__(self, axes, array):
        self.axes = axes
        self.in_space = pltpu.VMEM
        self.out = jax.ShapeDtypeStruct((2, 4, 4) + array.shape, array.dtype)
        self.out_space = pl.ANY
        self.scratch = [pltpu.SemaphoreType.DMA] + [pltpu.SemaphoreType.DMA((4,))] * 6

    def bind(self, source, target, scratch):
        self.x, self.o, self.local = source, target, scratch[0]
        self.s_one, self.r_one, self.s_two, self.r_two, self.s_core, self.r_core = scratch[1:]
        self.one, self.two = (lax.axis_index(axis) for axis in self.axes)
        self.core = lax.axis_index("core")
        self.stages = [self.start, self.middle, self.late, self.end]

    def mine(self):
        place = self.o.at[self.core, self.one, self.two]
        return pltpu.make_async_copy(self.x, place, self.local)

    def first(self, k, slot):
        device = {self.axes[1]: (self.two + k) % 4}
        place = self.o.at[self.core, self.one, slot]
        return remote(self.x, place, self.s_one.at[k], self.r_one.at[k], device)

    def second(self, k, row):
        device = {self.axes[0]: (self.one + k) % 4}
        place = self.o.at[self.core, row]
        return remote(place, place, self.s_two.at[k], self.r_two.at[k], device)

    def across(self, k, core):
        place = self.o.at[core, (self.one + 4 - k) % 4]
        device = {"core": 1 - self.core}
        return remote(place, place, self.s_core.at[k], self.r_core.at[k], device)

    def start(self):
        for k in (2, 1, 3):
            self.first(k, self.two).start()
        self.mine().start()

    def middle(self):
        self.mine().wait()
        for k in range(1, 4):
            self.first(k, (self.two + 4 - k) % 4).wait_recv()
        for k in (2, 1, 3):
            self.second(k, self.one).start()
        self.across(0, self.core).start()

    def late(self):
        for k in (1, 3, 2):
            self.second(k, (self.one + 4 - k) % 4).wait_recv()
            self.across(k, self.core).start()

    def end(self):
        for k in range(4):
            if k:
                self.first(k, self.two).wait_send()
                self.second(k, self.one).wait_send()
            self.across(k, self.core).wait_send()
            self.across(k, 1 - self.core).wait_recv()


class PlaneScatter:
    def __init__(self, axes, array, pair=False, kind=jnp.float32):
        self.axes, self.pair = axes, pair
        self.block = array.shape[3 if pair else 2 :]
        self.in_space = pltpu.VMEM
        self.out = jax.ShapeDtypeStruct(self.block, kind)
        self.out_space = pltpu.VMEM
        self.kind = array.dtype
        row = (4,) + self.block
        self.scratch = [
            pltpu.VMEM((4,) + row, self.kind),
            pltpu.VMEM(row, jnp.float32),
            pltpu.VMEM(row, self.kind),
            pltpu.VMEM(row, self.kind),
        ]
        if pair:
            self.scratch += [pltpu.VMEM((4,) + row, self.kind)] * 2
            self.scratch += [pltpu.SemaphoreType.DMA((4,))] * 2
        self.scratch += [pltpu.SemaphoreType.DMA((4,))] * 4

    def bind(self, source, target, scratch):
        self.x, self.o = source, target
        self.land, self.total, self.low, self.last = scratch[:4]
        if self.pair:
            self.half, self.summed, self.s_core, self.r_core = scratch[4:8]
        self.s_one, self.r_one, self.s_two, self.r_two = scratch[-4:]
        self.one, self.two = (lax.axis_index(axis) for axis in self.axes)
        self.core = lax.axis_index("core")
        self.stages = [self.start, self.middle, self.late, self.end]

    def across(self, k):
        to = (self.one + k) % 4
        source = self.x.at[to, :, 1 - self.core]
        device = {"core": 1 - self.core}
        return remote(source, self.half.at[to], self.s_core.at[k], self.r_core.at[k], device)

    def first(self, k, slot):
        to = (self.one + k) % 4
        source = self.summed if self.pair else self.x
        send, receive = self.s_one.at[k], self.r_one.at[k]
        return remote(source.at[to], self.land.at[slot], send, receive, {self.axes[0]: to})

    def second(self, k, slot):
        to = (self.two + k) % 4
        send, receive = self.s_two.at[k], self.r_two.at[k]
        return remote(self.low.at[to], self.last.at[slot], send, receive, {self.axes[1]: to})

    def start(self):
        for k in (2, 1, 3):
            if self.pair:
                self.across(k).start()
            else:
                self.first(k, self.one).start()
        if self.pair:
            self.across(0).start()

    def middle(self):
        if self.pair:
            for k in (2, 1, 3, 0):
                to = (self.one + k) % 4
                self.across(k).wait_recv()
                for item in range(4):
                    both = self.x[to, item, self.core].astype(jnp.float32)
                    both += self.half[to, item].astype(jnp.float32)
                    if k:
                        self.summed[to, item] = both.astype(self.kind)
                    else:
                        self.total[item] = both
                if k:
                    self.first(k, self.one).start()

    def late(self):
        slots = [(self.one + 4 - k) % 4 for k in range(4)]
        for k in range(1, 4):
            self.first(k, slots[k]).wait_recv()
        for item in range(4):
            if self.pair:
                total = self.total[item]
            else:
                total = self.x[self.one, item].astype(jnp.float32)
            for k in range(1, 4):
                total += self.land[slots[k], item].astype(jnp.float32)
            self.total[item] = total
            self.low[item] = total.astype(self.kind)
        for k in (2, 1, 3):
            self.second(k, self.two).start()

    def end(self):
        total = self.total[self.two]
        for k in range(1, 4):
            slot = (self.two + 4 - k) % 4
            self.second(k, slot).wait_recv()
            total += self.last[slot].astype(jnp.float32)
        self.o[...] = total.astype(self.o.dtype)
        for k in range(4):
            if k:
                self.first(k, self.one).wait_send()
                self.second(k, self.two).wait_send()
            if self.pair:
                self.across(k).wait_send()


class PlaneTotal:
    def __init__(self, axes, array):
        self.axes = axes
        self.scatter = PlaneScatter(axes, array, kind=array.dtype)
        self.gather = PlaneGather(axes, self.scatter.out)
        self.in_space = pltpu.VMEM
        self.out, self.out_space = self.gather.out, pl.ANY
        own = pltpu.VMEM(self.scatter.block, array.dtype)
        self.scratch = [own] + self.scatter.scratch + self.gather.scratch

    def bind(self, source, target, scratch):
        count = 1 + len(self.scatter.scratch)
        self.scatter.bind(source, scratch[0], scratch[1:count])
        self.gather.bind(scratch[0], target, scratch[count:])
        self.stages = self.scatter.stages + self.gather.stages


def split_point(rows):
    return rows if rows < 32 else (rows // 2 + 15) // 16 * 16


class RingGather:
    def __init__(self, axes, array):
        self.axes, self.n = axes, group_size(axes)
        self.block, self.dtype = array.shape, array.dtype
        self.cut = split_point(self.block[0])
        self.in_space = pltpu.VMEM
        self.out = jax.ShapeDtypeStruct((self.n, 2) + self.block, self.dtype)
        self.out_space = pl.ANY
        self.scratch = [pltpu.SemaphoreType.DMA] + [pltpu.SemaphoreType.DMA((4,))] * 4

    def bind(self, source, target, scratch):
        self.x, self.o = source, target
        self.local, self.send, self.receive, self.f_send, self.f_receive = scratch
        self.me, self.core = group_index(self.axes), lax.axis_index("core")
        self.stages = [self.start, self.middle, self.late, self.end]

    def at(self, shift, core):
        return self.o.at[(self.me + shift) % 4, core]

    def mine(self):
        return pltpu.make_async_copy(self.x, self.at(0, self.core), self.local)

    def copy(self, step, to, source, target):
        device = member(self.axes, (self.me + to) % 4)
        return remote(source, target, self.send.at[step], self.receive.at[step], device)

    def piece(self, shift, low):
        ref = self.at(shift, self.core)
        rows = pl.ds(0, self.cut) if low else pl.ds(self.cut, self.block[0] - self.cut)
        return ref.at[rows]

    def sends(self):
        place = self.at(0, self.core)
        low, high = self.piece(3, True), None
        found = [self.copy(0, 1, self.x, place), self.copy(1, 3, self.x, place)]
        found.append(self.copy(2, 1, low, low))
        if self.cut < self.block[0]:
            high = self.piece(1, False)
            found.append(self.copy(3, 3, high, high))
        return found

    def receipts(self):
        found = [
            self.copy(0, 1, self.x, self.at(3, self.core)),
            self.copy(1, 3, self.x, self.at(1, self.core)),
        ]
        low = self.piece(2, True)
        found.append(self.copy(2, 1, low, low))
        if self.cut < self.block[0]:
            high = self.piece(2, False)
            found.append(self.copy(3, 3, high, high))
        return found

    def forward(self, step, core):
        place = self.at((0, 3, 1, 2)[step], core)
        source = self.x if step == 0 else place
        device = {"core": 1 - self.core}
        return remote(source, place, self.f_send.at[step], self.f_receive.at[step], device)

    def start(self):
        sends = self.sends()
        sends[0].start()
        sends[1].start()
        self.mine().start()
        self.forward(0, self.core).start()

    def middle(self):
        sends, receipts = self.sends(), self.receipts()
        for step in range(2):
            receipts[step].wait_recv()
            if step + 2 < len(sends):
                sends[step + 2].start()
            self.forward(step + 1, self.core).start()

    def late(self):
        for receipt in self.receipts()[2:]:
            receipt.wait_recv()
        self.forward(3, self.core).start()

    def end(self):
        self.mine().wait()
        for send in self.sends():
            send.wait_send()
        for step in range(4):
            self.forward(step, self.core).wait_send()
            self.forward(step, 1 - self.core).wait_recv()


class RingScatter:
    def __init__(self, axes, array):
        self.axes = axes
        self.block = array.shape[2:]
        self.cut = split_point(self.block[0])
        self.in_space = pltpu.VMEM
        self.out = jax.ShapeDtypeStruct(self.block, jnp.float32)
        self.out_space = pltpu.VMEM
        rows = (self.cut, self.block[0] - self.cut)
        self.scratch = [pltpu.VMEM((4,) + self.block, array.dtype)] * 2
        self.scratch += [pltpu.VMEM((count,) + self.block[1:], array.dtype) for count in rows]
        self.scratch += [pltpu.VMEM((2,) + self.block, array.dtype)]
        self.scratch += [pltpu.SemaphoreType.DMA((4,))] * 4

    def bind(self, source, target, scratch):
        self.x, self.o = source, target
        self.half, self.summed = scratch[:2]
        self.via, self.land = scratch[2:4], scratch[4]
        self.s_one, self.r_one, self.send, self.receive = scratch[5:]
        self.me, self.core = group_index(self.axes), lax.axis_index("core")
        self.stages = [self.start, self.middle, self.late, self.end]

    def across(self, shift):
        to = (self.me + shift) % 4
        return remote(
            self.x.at[to, 1 - self.core],
            self.half.at[to],
            self.s_one.at[shift],
            self.r_one.at[shift],
            {"core": 1 - self.core},
        )

    def copy(self, step, to, source, target):
        device = member(self.axes, (self.me + to) % 4)
        return remote(source, target, self.send.at[step], self.receive.at[step], device)

    def copies(self):
        far = self.summed.at[(self.me + 2) % 4]
        low, high = pl.ds(0, self.cut), pl.ds(self.cut, self.block[0] - self.cut)
        return [
            self.copy(0, 1, far.at[low], self.via[0]),
            self.copy(1, 3, far.at[high], self.via[1]),
            self.copy(2, 1, self.summed.at[(self.me + 1) % 4], self.land.at[0]),
            self.copy(3, 3, self.summed.at[(self.me + 3) % 4], self.land.at[1]),
        ]

    def both(self, shift):
        self.across(shift).wait_recv()
        to = (self.me + shift) % 4
        return self.x[to, self.core].astype(jnp.float32) + self.half[to].astype(jnp.float32)

    def start(self):
        for shift in (2, 1, 3, 0):
            self.across(shift).start()

    def middle(self):
        copies = self.copies()
        kind = self.summed.dtype
        self.summed[(self.me + 2) % 4] = self.both(2).astype(kind)
        copies[0].start()
        copies[1].start()
        near, back = self.both(1), self.both(3)
        cut = self.cut
        after, before = (self.me + 1) % 4, (self.me + 3) % 4
        copies[0].wait_recv()
        self.summed[after, :cut] = (near[:cut] + self.via[0][...].astype(jnp.float32)).astype(kind)
        self.summed[after, cut:] = near[cut:].astype(kind)
        copies[2].start()
        copies[1].wait_recv()
        self.summed[before, cut:] = (back[cut:] + self.via[1][...].astype(jnp.float32)).astype(kind)
        self.summed[before, :cut] = back[:cut].astype(kind)
        copies[3].start()
        self.o[...] = self.both(0)

    def late(self):
        pass

    def end(self):
        copies = self.copies()
        for step in range(2):
            copies[step + 2].wait_recv()
            self.o[...] += self.land[step].astype(jnp.float32)
        for shift in range(4):
            self.across(shift).wait_send()
            copies[shift].wait_send()


def run_stages(ops, final):
    longest = max(len(op.stages) for op in ops)
    for index in range(longest - 1):
        for op in ops:
            if index < len(op.stages) - 1:
                op.stages[index]()
    if final:
        for op in ops:
            op.stages[-1]()


def communicate_kernel(ops, after, compute, inputs, *refs):
    refs = list(refs)
    count, more = len(ops), len(after)
    sources, extra = refs[:count], refs[count : count + inputs]
    refs = refs[count + inputs :]
    targets, late_targets = refs[:count], refs[count : count + more]
    scratch = refs[count + more :]
    late_sources = [scratch.pop(0) for unused in after]
    axes = []
    for op, source, target in zip(ops + after, sources + late_sources, targets + late_targets):
        op.bind(source, target, [scratch.pop(0) for unused in op.scratch])
        axes += [axis for axis in op.axes if axis not in axes]
    barrier = pltpu.get_barrier_semaphore()
    devices = [{"core": 1 - lax.axis_index("core")}]
    for axis in axes:
        devices += [{axis: (lax.axis_index(axis) + k) % 4} for k in range(1, 4)]
    for device in devices:
        pl.semaphore_signal(barrier, inc=1, device_id=device, device_id_type=MESH)
    pl.semaphore_wait(barrier, len(devices))
    if compute is None:
        run_stages(ops, True)
    else:
        for stage in (0, 1):
            for op in ops:
                op.stages[stage]()
        compute(*extra, *late_sources)
        run_stages(after, True)
        for stage in (2, 3):
            for op in ops:
                op.stages[stage]()


def communicate(name, identity, *requests, compute=None, inputs=(), after=()):
    arrays = [array for kind, axes, array in requests]
    ops = [kind(axes, array) for kind, axes, array in requests]
    late = [kind(axes, array) for kind, axes, array in after]
    held = [pltpu.VMEM(array.shape, array.dtype) for kind, axes, array in after]
    vmem = pl.BlockSpec(memory_space=pltpu.VMEM)
    return pl.pallas_call(
        functools.partial(communicate_kernel, ops, late, compute, len(inputs)),
        out_shape=tuple(op.out for op in ops + late),
        in_specs=[pl.BlockSpec(memory_space=op.in_space) for op in ops] + [vmem] * len(inputs),
        out_specs=tuple(pl.BlockSpec(memory_space=op.out_space) for op in ops + late),
        scratch_shapes=held + [item for op in ops + late for item in op.scratch],
        compiler_params=pltpu.CompilerParams(
            collective_id=identity,
            has_side_effects=True,
            vmem_limit_bytes=56 * 1024 * 1024,
        ),
        cost_estimate=pl.CostEstimate(flops=0, bytes_accessed=1_000_000, transcendentals=0),
        name=name,
    )(*arrays, *inputs)


ROWS = 16
GROUPS = 14
DOWN_ROWS = 48
DOWN_CUT = 512


def weight_grads(
    normed_ref, cot_ref, hidden_ref, d_gate_ref, d_up_ref, gate_ref, up_ref, down_ref, rest_ref
):
    part = hidden_ref.shape[1]
    for chip in range(GROUPS, 16):
        z, y = chip // 4, chip % 4
        gate_ref[z, y] = jnp.zeros(gate_ref.shape[2:], gate_ref.dtype)
        up_ref[y, z] = jnp.zeros(up_ref.shape[2:], up_ref.dtype)
    for chip in range(part // DOWN_ROWS, 16):
        z, y = chip // 4, chip % 4
        down_ref[z, y] = jnp.zeros(down_ref.shape[2:], down_ref.dtype)
        rest_ref[y, z] = jnp.zeros(rest_ref.shape[2:], rest_ref.dtype)

    def step(index, target, swapped, start):
        place = pl.ds(pl.multiple_of(index * 128, 128), 128)
        normed = normed_ref[:, place]
        gate = dot(normed, d_gate_ref[...], 0, 0).astype(jnp.bfloat16)
        up = dot(normed, d_up_ref[...], 0, 0).astype(jnp.bfloat16)
        for item in range(128 // ROWS):
            group = index * (128 // ROWS) + item
            owner, chip = group // GROUPS, group % GROUPS
            piece = slice(item * ROWS, (item + 1) * ROWS)
            gate_ref[chip // 4, chip % 4, owner] = gate[piece]
            up_ref[chip % 4, chip // 4, owner] = up[piece]
        down = dot(cot_ref[:, place], hidden_ref[...], 0, 0).T.astype(jnp.bfloat16)
        columns = pl.ds(pl.multiple_of(index * 128 - start, 128), 128)
        for chip in range(-(-part // DOWN_ROWS)):
            first = chip * DOWN_ROWS
            rows = min(DOWN_ROWS, part - first)
            z, y = chip // 4, chip % 4
            spot = (y, z) if swapped else (z, y)
            target[spot + (pl.ds(0, rows), columns)] = down[first : first + rows]

    def low_step(index, unused):
        step(index, down_ref, False, 0)
        return unused

    def high_step(index, unused):
        step(index, rest_ref, True, DOWN_CUT)
        return unused

    lax.fori_loop(0, DOWN_CUT // 128, low_step, 0)
    lax.fori_loop(DOWN_CUT // 128, D // 128, high_step, 0)


def widen_kernel(gate_ref, up_ref, gate_out_ref, up_out_ref):
    part = gate_ref.shape[-1]
    for source, target in ((gate_ref, gate_out_ref), (up_ref, up_out_ref)):
        for index in range(4):
            for core in range(2):
                first = (2 * index + core) * part
                value = source[core, 0, 0, index].astype(jnp.float32)
                target[:, first : first + part] = value


def widen(gate, up):
    part = gate.shape[-1]
    block = (2, 1, 1, 4, ROWS, part)
    target = pl.BlockSpec((ROWS, 8 * part), lambda index: (index, 0))
    wide = jax.ShapeDtypeStruct((ROWS * GROUPS, 8 * part), jnp.float32)
    return pl.pallas_call(
        widen_kernel,
        grid=(GROUPS,),
        out_shape=(wide, wide),
        in_specs=[
            pl.BlockSpec(block, lambda index: (0, index // 4, index % 4, 0, 0, 0)),
            pl.BlockSpec(block, lambda index: (0, index % 4, index // 4, 0, 0, 0)),
        ],
        out_specs=(target, target),
        name="widen",
    )(gate, up)


def widen_down_kernel(low_ref, high_ref, out_ref):
    part = out_ref.shape[0] // 2
    for core in range(2):
        for chip in range(-(-part // DOWN_ROWS)):
            first = chip * DOWN_ROWS
            rows = min(DOWN_ROWS, part - first)
            z, y = chip // 4, chip % 4
            place = pl.ds(core * part + first, rows)
            out_ref[place, :DOWN_CUT] = low_ref[core, z, y, :rows].astype(jnp.float32)
            out_ref[place, DOWN_CUT:] = high_ref[core, y, z, :rows].astype(jnp.float32)


def widen_down(low, high, part):
    vmem = pl.BlockSpec(memory_space=pltpu.VMEM)
    return pl.pallas_call(
        widen_down_kernel,
        out_shape=jax.ShapeDtypeStruct((2 * part, D), jnp.float32),
        in_specs=[vmem, vmem],
        out_specs=vmem,
        compiler_params=pltpu.CompilerParams(vmem_limit_bytes=32 * 1024 * 1024),
        name="widen_down",
    )(low, high)


def split_sums_kernel(rows, sums_ref, qkv_ref, out_ref, vectors_ref):
    first = qkv_ref.shape[1] // 128
    for chip in range(16):
        target = qkv_ref if chip < first else out_ref
        place = (chip if chip < first else chip - first) * 128
        for core in range(2):
            block = sums_ref[core, chip // 4, chip % 4].astype(jnp.float32)
            target[core * rows : (core + 1) * rows, place : place + 128] = block[:rows]
        vectors_ref[:, chip * 128 : (chip + 1) * 128] = block[rows : rows + 8]


def split_sums(sums, rows, columns):
    chips = 16
    vmem = pl.BlockSpec(memory_space=pltpu.VMEM)
    shapes = ((2 * rows, columns), (2 * rows, chips * 128 - columns), (8, chips * 128))
    return pl.pallas_call(
        functools.partial(split_sums_kernel, rows),
        out_shape=tuple(jax.ShapeDtypeStruct(shape, jnp.float32) for shape in shapes),
        in_specs=[vmem],
        out_specs=(vmem,) * 3,
        name="split_sums",
    )(sums)


def rms_apply(values, gain):
    mean_square = jnp.mean(values * values, axis=-1, keepdims=True)
    return values * lax.rsqrt(mean_square + norm_eps) * gain


def half_turn(values):
    middle = values.shape[-1] // 2
    return jnp.concatenate([-values[..., middle:], values[..., :middle]], axis=-1)


def rotate(values, cosine, sine):
    return values * cosine + half_turn(values) * sine


def rope_tables(positions, head_dim):
    middle = head_dim // 2
    inverse = rope_base ** (-(jnp.arange(middle).astype(jnp.float32) * 2.0) / head_dim)
    angles = positions.astype(jnp.float32)[:, None] * inverse[None, :]
    angles = jnp.concatenate([angles, angles], axis=-1)
    return (jnp.cos(angles), jnp.sin(angles))


def swiglu(gate_in, up_in):
    return jax.nn.silu(gate_in) * up_in


def dot(a, b, ca=1, cb=0):
    return lax.dot_general(a, b, (((ca,), (cb,)), ((), ())), preferred_element_type=jnp.float32)


def causal_copy(order_ref, k_ref, v_ref, sorted_ref):
    def move(slot, unused):
        half, core, y, z = slot % 2, slot // 2 % 2, slot // 4 % 4, slot // 16
        k_place = pl.multiple_of((((core * 4 + z) * 4 + y) * 2 + half) * SPAN, SPAN)
        v_place = pl.multiple_of((((core * 4 + y) * 4 + z) * 2 + half) * SPAN, SPAN)
        target = pl.ds(pl.multiple_of(order_ref[slot] * SPAN, SPAN), SPAN)
        sorted_ref[target, :128] = k_ref[pl.ds(k_place, SPAN), :]
        sorted_ref[target, 128:] = v_ref[pl.ds(v_place, SPAN), :]
        return unused

    lax.fori_loop(0, k_ref.shape[0] // SPAN, move, 0)


def visible(start, place, rows):
    key_place = lax.broadcasted_iota(jnp.int32, (CHUNK, rows), 0) + start
    lane = lax.broadcasted_iota(jnp.int32, (CHUNK, rows), 1)
    return key_place <= place * SPAN + lane % SPAN


def attend_kernel(order_ref, mine_ref, k_ref, v_ref, q_ref, out_ref, lse_ref, sorted_ref):
    causal_copy(order_ref, k_ref, v_ref, sorted_ref)
    rows = q_ref.shape[-1]
    for half in range(2):
        place = mine_ref[half]
        last = place * SPAN // CHUNK

        def step(index, carry, masked, half=half, place=place):
            start = pl.multiple_of(index * CHUNK, CHUNK)
            keys = sorted_ref[pl.ds(start, CHUNK), :128]
            values = sorted_ref[pl.ds(start, CHUNK), 128:]
            result = []
            for head in range(KVH):
                top, total, mixed = carry[head]
                scores = dot(keys, q_ref[half, head])
                if masked:
                    scores = jnp.where(visible(start, place, rows), scores, masked_score)
                new_top = jnp.maximum(top, jnp.max(scores, axis=0, keepdims=True))
                shrink = jnp.exp(top - new_top)
                weights = jnp.exp(scores - new_top)
                total = total * shrink + jnp.sum(weights, axis=0, keepdims=True)
                mixed = mixed * shrink + dot(values, weights.astype(jnp.bfloat16), 0, 0)
                result.append((new_top, total, mixed))
            return tuple(result)

        empty = tuple(
            (
                jnp.full((1, rows), masked_score, jnp.float32),
                jnp.zeros((1, rows), jnp.float32),
                jnp.zeros((128, rows), jnp.float32),
            )
            for head in range(KVH)
        )
        carry = lax.fori_loop(0, last, functools.partial(step, masked=False), empty)
        carry = step(last, carry, True)
        for head in range(KVH):
            top, total, mixed = carry[head]
            out_ref[half, head] = mixed[head * HD : (head + 1) * HD] / total
            lse_ref[half, head] = top + jnp.log(total)


def attend(order, mine, k_all, v_all, q_pad):
    halves, heads, unused, rows = q_pad.shape
    smem = pl.BlockSpec(memory_space=pltpu.SMEM)
    vmem = pl.BlockSpec(memory_space=pltpu.VMEM)
    return pl.pallas_call(
        attend_kernel,
        out_shape=(
            jax.ShapeDtypeStruct((halves, heads, HD, rows), jnp.float32),
            jax.ShapeDtypeStruct((halves, heads, 1, rows), jnp.float32),
        ),
        in_specs=[smem, smem, vmem, vmem, vmem],
        out_specs=(vmem, vmem),
        scratch_shapes=[pltpu.VMEM((k_all.shape[0], 256), k_all.dtype)],
        compiler_params=pltpu.CompilerParams(vmem_limit_bytes=48 * 1024 * 1024),
        cost_estimate=pl.CostEstimate(
            flops=0, bytes_accessed=1_000_000, transcendentals=0
        ),
        name="attend",
    )(order, mine, k_all, v_all, q_pad)


def attend_back_kernel(
    order_ref,
    mine_ref,
    k_ref,
    v_ref,
    q_ref,
    q_rows_ref,
    do_ref,
    do_rows_ref,
    lse_ref,
    delta_ref,
    dq_ref,
    dk_ref,
    dv_ref,
    sorted_ref,
    sum_ref,
):
    causal_copy(order_ref, k_ref, v_ref, sorted_ref)
    sum_ref[...] = jnp.zeros_like(sum_ref)
    rows = q_ref.shape[-1]
    for half in range(2):
        place = mine_ref[half]
        last = place * SPAN // CHUNK

        def step(index, carry, masked, half=half, place=place):
            start = pl.multiple_of(index * CHUNK, CHUNK)
            keys = sorted_ref[pl.ds(start, CHUNK), :128]
            values = sorted_ref[pl.ds(start, CHUNK), 128:]
            d_keys = sum_ref[pl.ds(start, CHUNK), :128]
            d_values = sum_ref[pl.ds(start, CHUNK), 128:]
            result = []
            for head in range(KVH):
                scores = dot(keys, q_ref[half, head])
                probs = jnp.exp(scores - lse_ref[half, head])
                if masked:
                    probs = jnp.where(visible(start, place, rows), probs, 0.0)
                d_probs = dot(values, do_ref[half, head])
                d_scores = (probs * (d_probs - delta_ref[half, head])).astype(jnp.bfloat16)
                d_values += dot(probs.astype(jnp.bfloat16), do_rows_ref[half, head])
                d_keys += dot(d_scores, q_rows_ref[half, head])
                result.append(carry[head] + dot(keys, d_scores, 0, 0))
            sum_ref[pl.ds(start, CHUNK), :128] = d_keys
            sum_ref[pl.ds(start, CHUNK), 128:] = d_values
            return tuple(result)

        empty = tuple(jnp.zeros((128, rows), jnp.float32) for head in range(KVH))
        carry = lax.fori_loop(0, last, functools.partial(step, masked=False), empty)
        carry = step(last, carry, True)
        for head in range(KVH):
            dq_ref[half, head] = carry[head][head * HD : (head + 1) * HD] * (HD**-0.5)

    def move(slot, unused):
        rest, y, z = slot % 4, slot // 4 % 4, slot // 16
        k_place = pl.multiple_of(slot * SPAN, SPAN)
        v_place = pl.multiple_of(((y * 4 + z) * 4 + rest) * SPAN, SPAN)
        source = pl.ds(pl.multiple_of(order_ref[slot] * SPAN, SPAN), SPAN)
        dk_ref[pl.ds(k_place, SPAN), :] = sum_ref[source, :128].astype(jnp.bfloat16)
        dv_ref[pl.ds(v_place, SPAN), :] = sum_ref[source, 128:].astype(jnp.bfloat16)
        return unused

    lax.fori_loop(0, dk_ref.shape[0] // SPAN, move, 0)


def attend_back(order, mine, k_all, v_all, q_pad, q_rows, do_pad, do_rows, lse, delta):
    halves, heads, unused, rows = q_pad.shape
    smem = pl.BlockSpec(memory_space=pltpu.SMEM)
    vmem = pl.BlockSpec(memory_space=pltpu.VMEM)
    return pl.pallas_call(
        attend_back_kernel,
        out_shape=(
            jax.ShapeDtypeStruct((halves, heads, HD, rows), jnp.float32),
            jax.ShapeDtypeStruct(k_all.shape, jnp.bfloat16),
            jax.ShapeDtypeStruct(v_all.shape, jnp.bfloat16),
        ),
        in_specs=[smem, smem] + [vmem] * 8,
        out_specs=(vmem, vmem, vmem),
        scratch_shapes=[
            pltpu.VMEM((k_all.shape[0], 256), k_all.dtype),
            pltpu.VMEM((k_all.shape[0], 256), jnp.float32),
        ],
        compiler_params=pltpu.CompilerParams(vmem_limit_bytes=48 * 1024 * 1024),
        cost_estimate=pl.CostEstimate(
            flops=0, bytes_accessed=1_000_000, transcendentals=0
        ),
        name="attend_back",
    )(order, mine, k_all, v_all, q_pad, q_rows, do_pad, do_rows, lse, delta)


def split_rows(tokens):
    parts = tokens.reshape(2, SPAN, KVH, GROUP, HD)
    return parts.transpose(0, 2, 3, 1, 4).reshape(2, KVH, GROUP * SPAN, HD)


def pad_heads(rows):
    return jnp.stack(
        [
            jnp.pad(rows[:, 0], ((0, 0), (0, 0), (0, HD))),
            jnp.pad(rows[:, 1], ((0, 0), (0, 0), (HD, 0))),
        ],
        axis=1,
    )


def join_rows(columns):
    parts = columns.reshape(2, KVH, HD, GROUP, SPAN)
    return parts.transpose(0, 4, 1, 3, 2).reshape(2 * SPAN, QH * HD)


def body(
    inputs,
    cotangent,
    span_order,
    positions,
    attn_gain,
    qkv_weight,
    qkv_bias,
    out_weight,
    mlp_gain,
    gate_weight,
    up_weight,
    down_weight,
):
    token_count = inputs.shape[0]
    q_cols = QH * HD
    k_cols = KVH * HD
    slices = lax.axis_size("dp")
    own_rows = D // slices
    part = FF // (slices * 2)
    dp = lax.axis_index("dp")
    core = lax.axis_index("core")
    slot = (lax.axis_index("z") * lax.axis_size("y") + lax.axis_index("y")) * 2 + core

    small = jnp.concatenate([attn_gain, mlp_gain, qkv_bias])
    small = jnp.pad(small, (0, 2048 - small.shape[0])).reshape(16, 128)
    qkv_half = lax.dynamic_slice_in_dim(qkv_weight, core * (own_rows // 2), own_rows // 2)
    qkv_full, small = communicate(
        "qkv_in", 0, (RingGather, ROW, qkv_half), (RingGather, ROW, small)
    )
    qkv_full = qkv_full.reshape(D, -1)
    small = small[:, 0].reshape(slices, -1)
    gain_one_wide = small[:, :own_rows].reshape(D).astype(jnp.float32)
    gain_two_wide = small[:, own_rows : 2 * own_rows].reshape(D).astype(jnp.float32)
    bias_full = small[:, 2 * own_rows : 2 * own_rows + qkv_bias.shape[0]]
    bias_full = bias_full.reshape(-1).astype(jnp.float32)
    out_full = lax.all_gather(out_weight, "dp", axis=0, tiled=True)

    def column_blocks(weight):
        parts = [weight[:, part * index : part * (index + 1)] for index in range(2 * slices)]
        return [jnp.where(core == 0, parts[2 * p], parts[2 * p + 1]) for p in range(slices)]

    gate_blocks, up_blocks = column_blocks(gate_weight), column_blocks(up_weight)
    gate_up = jnp.stack(
        [jnp.concatenate([gate_blocks[p], up_blocks[p]], axis=0) for p in range(slices)]
    )
    gate_up = lax.all_to_all(gate_up, "dp", 0, 0, tiled=True)
    gate_part = gate_up[:, :own_rows].reshape(D, part)
    up_part = gate_up[:, own_rows:].reshape(D, part)
    down_part = lax.dynamic_slice_in_dim(down_weight, core * part, part, axis=0)
    cot_all = lax.all_gather(cotangent, ("dp", "core"), axis=0, tiled=True)

    inputs_wide = inputs.astype(jnp.float32)
    normed_one = rms_apply(inputs_wide, gain_one_wide).astype(jnp.bfloat16)
    normed_one_all = lax.all_gather(normed_one, ("dp", "core"), axis=0, tiled=True)
    mixed_proj = dot(normed_one, qkv_full) + bias_full
    cosine, sine = rope_tables(positions, HD)
    cosine = cosine[:, None, :]
    sine = sine[:, None, :]
    query_rot = rotate(
        mixed_proj[:, :q_cols].reshape(token_count, QH, HD), cosine, sine
    ).astype(jnp.bfloat16)
    key_rot = rotate(
        mixed_proj[:, q_cols : q_cols + k_cols].reshape(token_count, KVH, HD), cosine, sine
    )
    key_rot = key_rot.astype(jnp.bfloat16).reshape(token_count, k_cols)
    value_low = mixed_proj[:, q_cols + k_cols :].astype(jnp.bfloat16)
    k_all, v_all = communicate(
        "kv_in", 1, (PlaneGather, PLANE, key_rot), (PlaneGather, ENALP, value_low)
    )
    k_all = k_all.reshape(-1, k_cols)
    v_all = v_all.reshape(-1, k_cols)
    mine = lax.dynamic_slice_in_dim(span_order, 2 * slot, 2)
    q_rows = pad_heads(split_rows(query_rot * jnp.bfloat16(HD**-0.5)))
    q_pad = q_rows.transpose(0, 1, 3, 2)
    attended_cols, lse = attend(span_order, mine, k_all, v_all, q_pad)
    attended_wide = join_rows(attended_cols)
    attended_low = attended_wide.astype(jnp.bfloat16)
    attended_all = lax.all_gather(attended_low, ("dp", "core"), axis=0, tiled=True)
    residual = inputs_wide + dot(attended_low, out_full)
    normed_two = rms_apply(residual, gain_two_wide).astype(jnp.bfloat16)

    (normed_two, normed_one_all) = lax.optimization_barrier((normed_two, normed_one_all))
    (normed_all,) = communicate("normed_in", 2, (RingGather, ROW, normed_two))
    normed_all = normed_all.reshape(-1, D)
    gate_proj = dot(normed_all, gate_part)
    up_proj = dot(normed_all, up_part)
    hidden_low = swiglu(gate_proj, up_proj).astype(jnp.bfloat16)
    out_sum = dot(hidden_low, down_part).astype(jnp.bfloat16)
    d_hidden = dot(cot_all, down_part, 1, 1)
    d_gate, d_up = jax.vjp(swiglu, gate_proj, up_proj)[1](d_hidden)
    d_gate = d_gate.astype(jnp.bfloat16)
    d_up = d_up.astype(jnp.bfloat16)
    d_norm_sum = (dot(d_gate, gate_part, 1, 1) + dot(d_up, up_part, 1, 1)).astype(jnp.bfloat16)
    blocks = (slices, 2, token_count, D)
    low = functools.partial(jax.ShapeDtypeStruct, dtype=jnp.bfloat16)
    scatter = functools.partial(PlaneScatter, kind=jnp.bfloat16)
    columns = low((4, 4, slices, ROWS, part))
    d_normed_two, out_rows, gate_grad, up_grad, down_low, down_high = communicate(
        "d_normed_out",
        3,
        (RingScatter, ROW, d_norm_sum.reshape(blocks)),
        (RingScatter, ROW, out_sum.reshape(blocks)),
        compute=weight_grads,
        inputs=(normed_all, cot_all, hidden_low, d_gate, d_up),
        after=(
            (scatter, PLANE, columns),
            (scatter, ENALP, columns),
            (scatter, PLANE, low((4, 4, DOWN_ROWS, DOWN_CUT))),
            (scatter, ENALP, low((4, 4, DOWN_ROWS, D - DOWN_CUT))),
        ),
    )
    output = (residual + out_rows).astype(jnp.bfloat16)

    d_resid_part, gain_two_grad = jax.vjp(rms_apply, residual, gain_two_wide)[1](d_normed_two)
    d_residual = d_resid_part + cotangent.astype(jnp.float32)
    d_branch = d_residual.astype(jnp.bfloat16)
    d_attended = dot(d_branch, out_full, 1, 1).astype(jnp.bfloat16)
    d_attended, attended_all = lax.optimization_barrier((d_attended, attended_all))
    row_delta = jnp.sum(
        (d_attended.astype(jnp.float32) * attended_wide).reshape(
            2, SPAN, KVH, GROUP, HD
        ),
        axis=-1,
    )
    row_delta = row_delta.transpose(0, 2, 3, 1).reshape(2, KVH, 1, GROUP * SPAN)
    do_rows = pad_heads(split_rows(d_attended))
    do_pad = do_rows.transpose(0, 1, 3, 2)
    d_query_cols, d_k_all, d_v_all = attend_back(
        span_order, mine, k_all, v_all, q_pad, q_rows, do_pad, do_rows, lse, row_delta
    )
    def turn_back(grads):
        scaled = grads * sine
        middle = HD // 2
        back = jnp.concatenate([scaled[..., middle:], -scaled[..., :middle]], axis=-1)
        return grads * cosine + back

    d_query_raw = turn_back(join_rows(d_query_cols).reshape(token_count, QH, HD))
    d_query_low = d_query_raw.reshape(token_count, q_cols).astype(jnp.bfloat16)
    paired = functools.partial(PlaneScatter, pair=True)
    pairs = (4, 4, 2, token_count, k_cols)
    d_k, d_v, d_query_all, d_branch_all, gate_grad, up_grad = communicate(
        "d_kv_out",
        4,
        (paired, PLANE, d_k_all.reshape(pairs)),
        (paired, ENALP, d_v_all.reshape(pairs)),
        (RingGather, ROW, d_query_low),
        (RingGather, ROW, d_branch),
        (Exchange, ROW, gate_grad),
        (Exchange, ROW, up_grad),
    )
    d_key_raw = turn_back(d_k.reshape(token_count, KVH, HD))
    d_kv_low = jnp.concatenate(
        [d_key_raw.reshape(token_count, k_cols), d_v], axis=1
    ).astype(jnp.bfloat16)
    d_mixed = jnp.concatenate([d_query_low, d_kv_low], axis=1)
    d_normed_one = dot(d_mixed, qkv_full, 1, 1)
    d_input_part, gain_one_grad = jax.vjp(rms_apply, inputs_wide, gain_one_wide)[1](d_normed_one)
    input_grad = (d_input_part + d_residual).astype(jnp.bfloat16)
    gain_grads = jnp.concatenate([gain_one_grad, gain_two_grad])
    gain_grads = jnp.pad(gain_grads, (0, 2048 - 2 * D)).reshape(16, 128)
    d_kv_rows, gain_grads, gate_grad, up_grad, down_low, down_high = communicate(
        "d_kv_in",
        5,
        (RingGather, ROW, d_kv_low),
        (RingGather, ROW, gain_grads),
        (PlaneGather, PLANE, gate_grad),
        (PlaneGather, ENALP, up_grad),
        (PlaneGather, PLANE, down_low),
        (PlaneGather, ENALP, down_high),
    )
    d_mixed_all = jnp.concatenate(
        [d_query_all.reshape(-1, q_cols), d_kv_rows.reshape(-1, 2 * k_cols)], axis=1
    )
    gain_grads = jnp.sum(gain_grads.reshape(2 * slices, -1), axis=0)
    bias_grad = jnp.sum(d_mixed_all.astype(jnp.float32), axis=0)

    half_rows = own_rows // 2
    first = dp * own_rows + core * half_rows

    def my_columns(tokens):
        return lax.dynamic_slice_in_dim(tokens, first, half_rows, axis=1)

    out_grad = dot(my_columns(attended_all), d_branch_all.reshape(-1, D), 0, 0)
    qkv_grad = dot(my_columns(normed_one_all), d_mixed_all, 0, 0)
    chips = 16
    width = chips * 128
    sums = jnp.concatenate(
        [
            jnp.concatenate([qkv_grad, out_grad], axis=1),
            jnp.pad(bias_grad, (0, width - bias_grad.shape[0]))[None],
            jnp.pad(gain_grads, (0, width - gain_grads.shape[0]))[None],
            jnp.zeros((14, width), jnp.float32),
        ],
        axis=0,
    ).astype(jnp.bfloat16)
    sums = sums.reshape(128, 4, 4, 128).transpose(1, 2, 0, 3)
    (sums,) = communicate("grads", 6, (PlaneTotal, PLANE, sums))
    qkv_grad, out_grad, vectors = split_sums(sums, half_rows, q_cols + 2 * k_cols)
    bias_grad, gain_grads = vectors[0], vectors[1]

    def owned(vector, start, count):
        width = count // slices
        return lax.dynamic_slice_in_dim(vector, start + dp * width, width)

    gate_grad, up_grad = widen(gate_grad, up_grad)
    down_grad = widen_down(down_low, down_high, part)
    return (
        output,
        input_grad,
        owned(gain_grads, 0, D),
        qkv_grad,
        owned(bias_grad, 0, q_cols + k_cols),
        owned(bias_grad, q_cols + k_cols, k_cols),
        out_grad,
        owned(gain_grads, D, D),
        gate_grad,
        up_grad,
        down_grad,
    )


def solution(mesh):
    grid = Mesh(mesh.devices.reshape(4, 4, 4, 2), ("dp", "z", "y", "core"))
    tokens = ("dp",) + CTX
    return jax.shard_map(
        body,
        mesh=grid,
        in_specs=(
            P(tokens, None),
            P(tokens, None),
            P(),
            P(tokens),
            P("dp"),
            P("dp", None),
            P("dp"),
            P("dp", None),
            P("dp"),
            P("dp", None),
            P("dp", None),
            P("dp", None),
        ),
        out_specs=(
            P(tokens, None),
            P(tokens, None),
            P("dp"),
            P("dp", None),
            P("dp"),
            P("dp"),
            P("dp", None),
            P("dp"),
            P("dp", None),
            P("dp", None),
            P("dp", None),
        ),
        check_vma=False,
    )
```

```python
import functools

import jax
import jax.numpy as jnp
from jax import lax
from jax.experimental import pallas as pl
from jax.experimental.pallas import tpu as pltpu
from jax.sharding import Mesh, PartitionSpec as P

QH = 14
KVH = 2
HD = 64
GROUP = QH // KVH
D = 896
FF = 4864
SPAN = 64
CHUNK = 256

norm_eps = 1e-06
rope_base = 1000000.0
masked_score = -1e30
CTX = ("z", "y", "core")
ROW = ("dp",)
PLANE = ("z", "y")
ENALP = ("y", "z")

MESH = pl.DeviceIdType.MESH
SIZES = {"dp": 4, "z": 4, "y": 4}


def group_size(axes):
    size = 1
    for axis in axes:
        size *= SIZES[axis]
    return size


def group_index(axes):
    index = 0
    for axis in axes:
        index = index * SIZES[axis] + lax.axis_index(axis)
    return index


def member(axes, index):
    found = {}
    for axis in reversed(axes):
        found[axis] = index % SIZES[axis]
        index = index // SIZES[axis]
    return found


def remote(source, target, send, receive, device):
    return pltpu.make_async_remote_copy(
        src_ref=source,
        dst_ref=target,
        send_sem=send,
        recv_sem=receive,
        device_id=device,
        device_id_type=MESH,
    )


class Exchange:
    def __init__(self, axes, array):
        self.axes, self.n = axes, group_size(axes)
        self.in_space = pltpu.VMEM
        self.out = jax.ShapeDtypeStruct(array.shape, array.dtype)
        self.out_space = pl.ANY
        self.scratch = [pltpu.SemaphoreType.DMA] + [pltpu.SemaphoreType.DMA((self.n,))] * 2

    def bind(self, source, target, scratch):
        self.x, self.o = source, target
        self.local, self.send, self.receive = scratch
        self.me = group_index(self.axes)
        self.stages = [self.start, self.end]

    def mine(self):
        return pltpu.make_async_copy(self.x.at[self.me], self.o.at[self.me], self.local)

    def outward(self, k, slot):
        to = (self.me + k) % self.n
        device = member(self.axes, to)
        send, receive = self.send.at[k], self.receive.at[k]
        return remote(self.x.at[to], self.o.at[slot], send, receive, device)

    def start(self):
        self.mine().start()
        for k in range(1, self.n):
            self.outward(k, self.me).start()

    def end(self):
        self.mine().wait()
        for k in range(1, self.n):
            self.outward(k, self.me).wait_send()
            self.outward(k, (self.me + self.n - k) % self.n).wait_recv()


class PlaneGather:
    def __init__(self, axes, array):
        self.axes = axes
        self.in_space = pltpu.VMEM
        self.out = jax.ShapeDtypeStruct((2, 4, 4) + array.shape, array.dtype)
        self.out_space = pl.ANY
        self.scratch = [pltpu.SemaphoreType.DMA] + [pltpu.SemaphoreType.DMA((4,))] * 6

    def bind(self, source, target, scratch):
        self.x, self.o, self.local = source, target, scratch[0]
        self.s_one, self.r_one, self.s_two, self.r_two, self.s_core, self.r_core = scratch[1:]
        self.one, self.two = (lax.axis_index(axis) for axis in self.axes)
        self.core = lax.axis_index("core")
        self.stages = [self.start, self.middle, self.late, self.end]

    def mine(self):
        place = self.o.at[self.core, self.one, self.two]
        return pltpu.make_async_copy(self.x, place, self.local)

    def first(self, k, slot):
        device = {self.axes[1]: (self.two + k) % 4}
        place = self.o.at[self.core, self.one, slot]
        return remote(self.x, place, self.s_one.at[k], self.r_one.at[k], device)

    def second(self, k, row):
        device = {self.axes[0]: (self.one + k) % 4}
        place = self.o.at[self.core, row]
        return remote(place, place, self.s_two.at[k], self.r_two.at[k], device)

    def across(self, k, core):
        place = self.o.at[core, (self.one + 4 - k) % 4]
        device = {"core": 1 - self.core}
        return remote(place, place, self.s_core.at[k], self.r_core.at[k], device)

    def start(self):
        for k in (2, 1, 3):
            self.first(k, self.two).start()
        self.mine().start()

    def middle(self):
        self.mine().wait()
        for k in range(1, 4):
            self.first(k, (self.two + 4 - k) % 4).wait_recv()
        for k in (2, 1, 3):
            self.second(k, self.one).start()
        self.across(0, self.core).start()

    def late(self):
        for k in (1, 3, 2):
            self.second(k, (self.one + 4 - k) % 4).wait_recv()
            self.across(k, self.core).start()

    def end(self):
        for k in range(4):
            if k:
                self.first(k, self.two).wait_send()
                self.second(k, self.one).wait_send()
            self.across(k, self.core).wait_send()
            self.across(k, 1 - self.core).wait_recv()


class PlaneScatter:
    def __init__(self, axes, array, pair=False, kind=jnp.float32):
        self.axes, self.pair = axes, pair
        self.block = array.shape[3 if pair else 2 :]
        self.in_space = pltpu.VMEM
        self.out = jax.ShapeDtypeStruct(self.block, kind)
        self.out_space = pltpu.VMEM
        self.kind = array.dtype
        row = (4,) + self.block
        self.scratch = [
            pltpu.VMEM((4,) + row, self.kind),
            pltpu.VMEM(row, jnp.float32),
            pltpu.VMEM(row, self.kind),
            pltpu.VMEM(row, self.kind),
        ]
        if pair:
            self.scratch += [pltpu.VMEM((4,) + row, self.kind)] * 2
            self.scratch += [pltpu.SemaphoreType.DMA((4,))] * 2
        self.scratch += [pltpu.SemaphoreType.DMA((4,))] * 4

    def bind(self, source, target, scratch):
        self.x, self.o = source, target
        self.land, self.total, self.low, self.last = scratch[:4]
        if self.pair:
            self.half, self.summed, self.s_core, self.r_core = scratch[4:8]
        self.s_one, self.r_one, self.s_two, self.r_two = scratch[-4:]
        self.one, self.two = (lax.axis_index(axis) for axis in self.axes)
        self.core = lax.axis_index("core")
        self.stages = [self.start, self.middle, self.late, self.end]

    def across(self, k):
        to = (self.one + k) % 4
        source = self.x.at[to, :, 1 - self.core]
        device = {"core": 1 - self.core}
        return remote(source, self.half.at[to], self.s_core.at[k], self.r_core.at[k], device)

    def first(self, k, slot):
        to = (self.one + k) % 4
        source = self.summed if self.pair else self.x
        send, receive = self.s_one.at[k], self.r_one.at[k]
        return remote(source.at[to], self.land.at[slot], send, receive, {self.axes[0]: to})

    def second(self, k, slot):
        to = (self.two + k) % 4
        send, receive = self.s_two.at[k], self.r_two.at[k]
        return remote(self.low.at[to], self.last.at[slot], send, receive, {self.axes[1]: to})

    def start(self):
        for k in (2, 1, 3):
            if self.pair:
                self.across(k).start()
            else:
                self.first(k, self.one).start()
        if self.pair:
            self.across(0).start()

    def middle(self):
        if self.pair:
            for k in (2, 1, 3, 0):
                to = (self.one + k) % 4
                self.across(k).wait_recv()
                for item in range(4):
                    both = self.x[to, item, self.core].astype(jnp.float32)
                    both += self.half[to, item].astype(jnp.float32)
                    if k:
                        self.summed[to, item] = both.astype(self.kind)
                    else:
                        self.total[item] = both
                if k:
                    self.first(k, self.one).start()

    def late(self):
        slots = [(self.one + 4 - k) % 4 for k in range(4)]
        for k in range(1, 4):
            self.first(k, slots[k]).wait_recv()
        for item in range(4):
            if self.pair:
                total = self.total[item]
            else:
                total = self.x[self.one, item].astype(jnp.float32)
            for k in range(1, 4):
                total += self.land[slots[k], item].astype(jnp.float32)
            self.total[item] = total
            self.low[item] = total.astype(self.kind)
        for k in (2, 1, 3):
            self.second(k, self.two).start()

    def end(self):
        total = self.total[self.two]
        for k in range(1, 4):
            slot = (self.two + 4 - k) % 4
            self.second(k, slot).wait_recv()
            total += self.last[slot].astype(jnp.float32)
        self.o[...] = total.astype(self.o.dtype)
        for k in range(4):
            if k:
                self.first(k, self.one).wait_send()
                self.second(k, self.two).wait_send()
            if self.pair:
                self.across(k).wait_send()


class PlaneTotal:
    def __init__(self, axes, array):
        self.axes = axes
        self.scatter = PlaneScatter(axes, array, kind=array.dtype)
        self.gather = PlaneGather(axes, self.scatter.out)
        self.in_space = pltpu.VMEM
        self.out, self.out_space = self.gather.out, pl.ANY
        own = pltpu.VMEM(self.scatter.block, array.dtype)
        self.scratch = [own] + self.scatter.scratch + self.gather.scratch

    def bind(self, source, target, scratch):
        count = 1 + len(self.scatter.scratch)
        self.scatter.bind(source, scratch[0], scratch[1:count])
        self.gather.bind(scratch[0], target, scratch[count:])
        self.stages = self.scatter.stages + self.gather.stages


def split_point(rows):
    return rows if rows < 32 else (rows // 2 + 15) // 16 * 16


class RingGather:
    def __init__(self, axes, array):
        self.axes, self.n = axes, group_size(axes)
        self.block, self.dtype = array.shape, array.dtype
        self.cut = split_point(self.block[0])
        self.in_space = pltpu.VMEM
        self.out = jax.ShapeDtypeStruct((self.n, 2) + self.block, self.dtype)
        self.out_space = pl.ANY
        self.scratch = [pltpu.SemaphoreType.DMA] + [pltpu.SemaphoreType.DMA((4,))] * 4

    def bind(self, source, target, scratch):
        self.x, self.o = source, target
        self.local, self.send, self.receive, self.f_send, self.f_receive = scratch
        self.me, self.core = group_index(self.axes), lax.axis_index("core")
        self.stages = [self.start, self.middle, self.late, self.end]

    def at(self, shift, core):
        return self.o.at[(self.me + shift) % 4, core]

    def mine(self):
        return pltpu.make_async_copy(self.x, self.at(0, self.core), self.local)

    def copy(self, step, to, source, target):
        device = member(self.axes, (self.me + to) % 4)
        return remote(source, target, self.send.at[step], self.receive.at[step], device)

    def piece(self, shift, low):
        ref = self.at(shift, self.core)
        rows = pl.ds(0, self.cut) if low else pl.ds(self.cut, self.block[0] - self.cut)
        return ref.at[rows]

    def sends(self):
        place = self.at(0, self.core)
        low, high = self.piece(3, True), None
        found = [self.copy(0, 1, self.x, place), self.copy(1, 3, self.x, place)]
        found.append(self.copy(2, 1, low, low))
        if self.cut < self.block[0]:
            high = self.piece(1, False)
            found.append(self.copy(3, 3, high, high))
        return found

    def receipts(self):
        found = [
            self.copy(0, 1, self.x, self.at(3, self.core)),
            self.copy(1, 3, self.x, self.at(1, self.core)),
        ]
        low = self.piece(2, True)
        found.append(self.copy(2, 1, low, low))
        if self.cut < self.block[0]:
            high = self.piece(2, False)
            found.append(self.copy(3, 3, high, high))
        return found

    def forward(self, step, core):
        place = self.at((0, 3, 1, 2)[step], core)
        source = self.x if step == 0 else place
        device = {"core": 1 - self.core}
        return remote(source, place, self.f_send.at[step], self.f_receive.at[step], device)

    def start(self):
        sends = self.sends()
        sends[0].start()
        sends[1].start()
        self.mine().start()
        self.forward(0, self.core).start()

    def middle(self):
        sends, receipts = self.sends(), self.receipts()
        for step in range(2):
            receipts[step].wait_recv()
            if step + 2 < len(sends):
                sends[step + 2].start()
            self.forward(step + 1, self.core).start()

    def late(self):
        for receipt in self.receipts()[2:]:
            receipt.wait_recv()
        self.forward(3, self.core).start()

    def end(self):
        self.mine().wait()
        for send in self.sends():
            send.wait_send()
        for step in range(4):
            self.forward(step, self.core).wait_send()
            self.forward(step, 1 - self.core).wait_recv()


class RingScatter:
    def __init__(self, axes, array):
        self.axes = axes
        self.block = array.shape[2:]
        self.cut = split_point(self.block[0])
        self.in_space = pltpu.VMEM
        self.out = jax.ShapeDtypeStruct(self.block, jnp.float32)
        self.out_space = pltpu.VMEM
        rows = (self.cut, self.block[0] - self.cut)
        self.scratch = [pltpu.VMEM((4,) + self.block, array.dtype)] * 2
        self.scratch += [pltpu.VMEM((count,) + self.block[1:], array.dtype) for count in rows]
        self.scratch += [pltpu.VMEM((2,) + self.block, array.dtype)]
        self.scratch += [pltpu.SemaphoreType.DMA((4,))] * 4

    def bind(self, source, target, scratch):
        self.x, self.o = source, target
        self.half, self.summed = scratch[:2]
        self.via, self.land = scratch[2:4], scratch[4]
        self.s_one, self.r_one, self.send, self.receive = scratch[5:]
        self.me, self.core = group_index(self.axes), lax.axis_index("core")
        self.stages = [self.start, self.middle, self.late, self.end]

    def across(self, shift):
        to = (self.me + shift) % 4
        return remote(
            self.x.at[to, 1 - self.core],
            self.half.at[to],
            self.s_one.at[shift],
            self.r_one.at[shift],
            {"core": 1 - self.core},
        )

    def copy(self, step, to, source, target):
        device = member(self.axes, (self.me + to) % 4)
        return remote(source, target, self.send.at[step], self.receive.at[step], device)

    def copies(self):
        far = self.summed.at[(self.me + 2) % 4]
        low, high = pl.ds(0, self.cut), pl.ds(self.cut, self.block[0] - self.cut)
        return [
            self.copy(0, 1, far.at[low], self.via[0]),
            self.copy(1, 3, far.at[high], self.via[1]),
            self.copy(2, 1, self.summed.at[(self.me + 1) % 4], self.land.at[0]),
            self.copy(3, 3, self.summed.at[(self.me + 3) % 4], self.land.at[1]),
        ]

    def both(self, shift):
        self.across(shift).wait_recv()
        to = (self.me + shift) % 4
        return self.x[to, self.core].astype(jnp.float32) + self.half[to].astype(jnp.float32)

    def start(self):
        for shift in (2, 1, 3, 0):
            self.across(shift).start()

    def middle(self):
        copies = self.copies()
        kind = self.summed.dtype
        self.summed[(self.me + 2) % 4] = self.both(2).astype(kind)
        copies[0].start()
        copies[1].start()
        near, back = self.both(1), self.both(3)
        cut = self.cut
        after, before = (self.me + 1) % 4, (self.me + 3) % 4
        copies[0].wait_recv()
        self.summed[after, :cut] = (near[:cut] + self.via[0][...].astype(jnp.float32)).astype(kind)
        self.summed[after, cut:] = near[cut:].astype(kind)
        copies[2].start()
        copies[1].wait_recv()
        self.summed[before, cut:] = (back[cut:] + self.via[1][...].astype(jnp.float32)).astype(kind)
        self.summed[before, :cut] = back[:cut].astype(kind)
        copies[3].start()
        self.o[...] = self.both(0)

    def late(self):
        pass

    def end(self):
        copies = self.copies()
        for step in range(2):
            copies[step + 2].wait_recv()
            self.o[...] += self.land[step].astype(jnp.float32)
        for shift in range(4):
            self.across(shift).wait_send()
            copies[shift].wait_send()


class AxisScatter:
    def __init__(self, axes, array):
        self.axes = axes
        self.block, self.kind = array.shape[1:], array.dtype
        self.in_space = pltpu.VMEM
        self.out = jax.ShapeDtypeStruct(self.block, self.kind)
        self.out_space = pltpu.VMEM
        self.scratch = [pltpu.VMEM(array.shape, self.kind)] + [pltpu.SemaphoreType.DMA((4,))] * 2

    def bind(self, source, target, scratch):
        self.x, self.o = source, target
        self.land, self.send, self.receive = scratch
        self.me = lax.axis_index(self.axes[0])
        self.stages = [self.start, self.end]

    def outward(self, k, slot):
        to = (self.me + k) % 4
        send, receive = self.send.at[k], self.receive.at[k]
        return remote(self.x.at[to], self.land.at[slot], send, receive, {self.axes[0]: to})

    def start(self):
        for k in (2, 1, 3):
            self.outward(k, self.me).start()

    def end(self):
        slots = [(self.me + 4 - k) % 4 for k in range(4)]
        for k in range(1, 4):
            self.outward(k, slots[k]).wait_recv()
        for item in range(self.block[0] if len(self.block) > 2 else 1):
            at = (item,) if len(self.block) > 2 else ()
            total = self.x[(self.me,) + at].astype(jnp.float32)
            for k in range(1, 4):
                total += self.land[(slots[k],) + at].astype(jnp.float32)
            if at:
                self.o[item] = total.astype(self.kind)
            else:
                self.o[...] = total.astype(self.kind)
        for k in range(1, 4):
            self.outward(k, self.me).wait_send()


class AxisGather:
    def __init__(self, axes, array, share=False):
        self.axes, self.share = axes, share
        self.in_space = pltpu.VMEM
        lead = (2, 4) if share else (4,)
        self.out = jax.ShapeDtypeStruct(lead + array.shape, array.dtype)
        self.out_space = pl.ANY
        self.scratch = [pltpu.SemaphoreType.DMA] + [pltpu.SemaphoreType.DMA((4,))] * 4

    def bind(self, source, target, scratch):
        self.x, self.o, self.local = source, target, scratch[0]
        self.send, self.receive, self.f_send, self.f_receive = scratch[1:]
        self.me, self.core = lax.axis_index(self.axes[0]), lax.axis_index("core")
        self.stages = [self.start, self.late, self.end] if self.share else [self.start, self.end]

    def at(self, slot, core):
        return self.o.at[core, slot] if self.share else self.o.at[slot]

    def mine(self):
        return pltpu.make_async_copy(self.x, self.at(self.me, self.core), self.local)

    def outward(self, k, slot):
        send, receive = self.send.at[k], self.receive.at[k]
        device = {self.axes[0]: (self.me + k) % 4}
        return remote(self.x, self.at(slot, self.core), send, receive, device)

    def forward(self, k, core):
        place = self.at((self.me + 4 - k) % 4, core)
        send, receive = self.f_send.at[k], self.f_receive.at[k]
        source = place if k else self.x
        return remote(source, place, send, receive, {"core": 1 - self.core})

    def start(self):
        for k in (2, 1, 3):
            self.outward(k, self.me).start()
        self.mine().start()
        if self.share:
            self.forward(0, self.core).start()

    def late(self):
        for k in (1, 3, 2):
            self.outward(k, (self.me + 4 - k) % 4).wait_recv()
            self.forward(k, self.core).start()

    def end(self):
        self.mine().wait()
        for k in range(4):
            if k:
                self.outward(k, self.me).wait_send()
                if not self.share:
                    self.outward(k, (self.me + 4 - k) % 4).wait_recv()
            if self.share:
                self.forward(k, self.core).wait_send()
                self.forward(k, 1 - self.core).wait_recv()


class Deal:
    def __init__(self, axes, array):
        self.axes = axes + ROW
        self.scatter = AxisScatter(axes, array)
        self.exchange = Exchange(ROW, self.scatter.out)
        self.in_space = pltpu.VMEM
        self.out, self.out_space = self.exchange.out, pl.ANY
        own = pltpu.VMEM(self.scatter.block, array.dtype)
        self.scratch = [own] + self.scatter.scratch + self.exchange.scratch

    def bind(self, source, target, scratch):
        count = 1 + len(self.scatter.scratch)
        self.scatter.bind(source, scratch[0], scratch[1:count])
        self.exchange.bind(scratch[0], target, scratch[count:])
        self.stages = self.scatter.stages + self.exchange.stages


def run_stages(ops):
    longest = max(len(op.stages) for op in ops)
    for index in range(longest - 1):
        for op in ops:
            if index < len(op.stages) - 1:
                op.stages[index]()
    for op in ops:
        op.stages[-1]()


def communicate_kernel(ops, after, compute, inputs, *refs):
    refs = list(refs)
    count, more, waiting = len(ops), len(after), after
    sources, extra = refs[:count], refs[count : count + inputs]
    refs = refs[count + inputs :]
    targets, late_targets = refs[:count], refs[count : count + more]
    scratch = refs[count + more :]
    late_sources = [scratch.pop(0) for unused in after]
    axes = []
    for op, source, target in zip(ops + after, sources + late_sources, targets + late_targets):
        op.bind(source, target, [scratch.pop(0) for unused in op.scratch])
        axes += [axis for axis in op.axes if axis not in axes]
    barrier = pltpu.get_barrier_semaphore()
    devices = [{"core": 1 - lax.axis_index("core")}]
    for axis in axes:
        devices += [{axis: (lax.axis_index(axis) + k) % 4} for k in range(1, 4)]
    for device in devices:
        pl.semaphore_signal(barrier, inc=1, device_id=device, device_id_type=MESH)
    pl.semaphore_wait(barrier, len(devices))
    if compute is None:
        run_stages(ops)
    else:
        for op in ops:
            op.stages[0]()
        for index, (function, count) in enumerate(compute):
            function(*extra, *late_sources)
            for op in after[:count]:
                op.stages[0]()
            after = after[count:]
            if index == 0:
                for op in ops:
                    op.stages[1]()
        for stage in (2, 3):
            for op in ops:
                op.stages[stage]()
        for op in waiting:
            op.stages[1]()


def communicate(name, identity, *requests, compute=None, inputs=(), after=()):
    arrays = [array for kind, axes, array in requests]
    ops = [kind(axes, array) for kind, axes, array in requests]
    late = [kind(axes, array) for kind, axes, array in after]
    held = [pltpu.VMEM(array.shape, array.dtype) for kind, axes, array in after]
    vmem = pl.BlockSpec(memory_space=pltpu.VMEM)
    return pl.pallas_call(
        functools.partial(communicate_kernel, ops, late, compute, len(inputs)),
        out_shape=tuple(op.out for op in ops + late),
        in_specs=[pl.BlockSpec(memory_space=op.in_space) for op in ops] + [vmem] * len(inputs),
        out_specs=tuple(pl.BlockSpec(memory_space=op.out_space) for op in ops + late),
        scratch_shapes=held + [item for op in ops + late for item in op.scratch],
        compiler_params=pltpu.CompilerParams(
            collective_id=identity,
            has_side_effects=True,
            vmem_limit_bytes=56 * 1024 * 1024,
        ),
        cost_estimate=pl.CostEstimate(flops=0, bytes_accessed=1_000_000, transcendentals=0),
        name=name,
    )(*arrays, *inputs)


ROWS = 16
GROUPS = 14
DOWN_ROWS = 48
DOWN_CUT = 512


def store_groups(index, value, target, swapped):
    for item in range(128 // ROWS):
        group = index * (128 // ROWS) + item
        owner, chip = group // GROUPS, group % GROUPS
        z, y = chip // 4, chip % 4
        spot = (y, z) if swapped else (z, y)
        target[spot + (owner,)] = value[item * ROWS : (item + 1) * ROWS]


def gate_or_up_grads(normed_ref, d_ref, target, swapped):
    for chip in range(GROUPS, 16):
        z, y = chip // 4, chip % 4
        target[(y, z) if swapped else (z, y)] = jnp.zeros(target.shape[2:], target.dtype)

    def step(index, unused):
        place = pl.ds(pl.multiple_of(index * 128, 128), 128)
        value = dot(normed_ref[:, place], d_ref[...], 0, 0).astype(jnp.bfloat16)
        store_groups(index, value, target, swapped)
        return unused

    lax.fori_loop(0, D // 128, step, 0)


def gate_grads(normed, cot, hidden, d_gate, d_up, gate, up, down, rest):
    gate_or_up_grads(normed, d_gate, gate, False)


def up_grads(normed, cot, hidden, d_gate, d_up, gate, up, down, rest):
    gate_or_up_grads(normed, d_up, up, True)


def down_grads(normed, cot_ref, hidden_ref, d_gate, d_up, gate, up, down_ref, rest_ref):
    part = hidden_ref.shape[1]
    for chip in range(part // DOWN_ROWS, 16):
        z, y = chip // 4, chip % 4
        down_ref[z, y] = jnp.zeros(down_ref.shape[2:], down_ref.dtype)
        rest_ref[y, z] = jnp.zeros(rest_ref.shape[2:], rest_ref.dtype)

    def step(index, target, swapped, start):
        place = pl.ds(pl.multiple_of(index * 128, 128), 128)
        down = dot(cot_ref[:, place], hidden_ref[...], 0, 0).T.astype(jnp.bfloat16)
        columns = pl.ds(pl.multiple_of(index * 128 - start, 128), 128)
        for chip in range(-(-part // DOWN_ROWS)):
            first = chip * DOWN_ROWS
            rows = min(DOWN_ROWS, part - first)
            z, y = chip // 4, chip % 4
            spot = (y, z) if swapped else (z, y)
            target[spot + (pl.ds(0, rows), columns)] = down[first : first + rows]

    def low_step(index, unused):
        step(index, down_ref, False, 0)
        return unused

    def high_step(index, unused):
        step(index, rest_ref, True, DOWN_CUT)
        return unused

    lax.fori_loop(0, DOWN_CUT // 128, low_step, 0)
    lax.fori_loop(DOWN_CUT // 128, D // 128, high_step, 0)


def widen_kernel(gate_ref, up_ref, gate_out_ref, up_out_ref):
    part = gate_ref.shape[-1]
    for source, target in ((gate_ref, gate_out_ref), (up_ref, up_out_ref)):
        for index in range(4):
            for core in range(2):
                first = (2 * index + core) * part
                value = source[core, 0, 0, index].astype(jnp.float32)
                target[:, first : first + part] = value


def widen(gate, up):
    part = gate.shape[-1]
    block = (2, 1, 1, 4, ROWS, part)
    target = pl.BlockSpec((ROWS, 8 * part), lambda index: (index, 0))
    wide = jax.ShapeDtypeStruct((ROWS * GROUPS, 8 * part), jnp.float32)
    return pl.pallas_call(
        widen_kernel,
        grid=(GROUPS,),
        out_shape=(wide, wide),
        in_specs=[
            pl.BlockSpec(block, lambda index: (0, index // 4, index % 4, 0, 0, 0)),
            pl.BlockSpec(block, lambda index: (0, index % 4, index // 4, 0, 0, 0)),
        ],
        out_specs=(target, target),
        name="widen",
    )(gate, up)


def widen_down_kernel(low_ref, high_ref, out_ref):
    part = out_ref.shape[0] // 2
    for core in range(2):
        for chip in range(-(-part // DOWN_ROWS)):
            first = chip * DOWN_ROWS
            rows = min(DOWN_ROWS, part - first)
            z, y = chip // 4, chip % 4
            place = pl.ds(core * part + first, rows)
            out_ref[place, :DOWN_CUT] = low_ref[core, z, y, :rows].astype(jnp.float32)
            out_ref[place, DOWN_CUT:] = high_ref[core, y, z, :rows].astype(jnp.float32)


def widen_down(low, high, part):
    vmem = pl.BlockSpec(memory_space=pltpu.VMEM)
    return pl.pallas_call(
        widen_down_kernel,
        out_shape=jax.ShapeDtypeStruct((2 * part, D), jnp.float32),
        in_specs=[vmem, vmem],
        out_specs=vmem,
        compiler_params=pltpu.CompilerParams(vmem_limit_bytes=32 * 1024 * 1024),
        name="widen_down",
    )(low, high)


def split_sums_kernel(rows, top_ref, end_ref, qkv_ref, out_ref, vectors_ref):
    first = qkv_ref.shape[1] // 128
    for chip in range(16):
        target = qkv_ref if chip < first else out_ref
        place = (chip if chip < first else chip - first) * 128
        for core in range(2):
            z, y = chip // 4, chip % 4
            top = top_ref[core, z, y].astype(jnp.float32)
            end = end_ref[core, y, z].astype(jnp.float32)
            start, cut = core * rows, top.shape[0]
            target[start : start + cut, place : place + 128] = top
            target[start + cut : start + rows, place : place + 128] = end[: rows - cut]
        vectors_ref[:, chip * 128 : (chip + 1) * 128] = end[rows - cut : rows - cut + 8]


def split_sums(top, end, rows, columns):
    chips = 16
    vmem = pl.BlockSpec(memory_space=pltpu.VMEM)
    shapes = ((2 * rows, columns), (2 * rows, chips * 128 - columns), (8, chips * 128))
    return pl.pallas_call(
        functools.partial(split_sums_kernel, rows),
        out_shape=tuple(jax.ShapeDtypeStruct(shape, jnp.float32) for shape in shapes),
        in_specs=[vmem, vmem],
        out_specs=(vmem,) * 3,
        name="split_sums",
    )(top, end)


def rms_apply(values, gain):
    mean_square = jnp.mean(values * values, axis=-1, keepdims=True)
    return values * lax.rsqrt(mean_square + norm_eps) * gain


def half_turn(values):
    middle = values.shape[-1] // 2
    return jnp.concatenate([-values[..., middle:], values[..., :middle]], axis=-1)


def rotate(values, cosine, sine):
    return values * cosine + half_turn(values) * sine


def rope_tables(positions, head_dim):
    middle = head_dim // 2
    inverse = rope_base ** (-(jnp.arange(middle).astype(jnp.float32) * 2.0) / head_dim)
    angles = positions.astype(jnp.float32)[:, None] * inverse[None, :]
    angles = jnp.concatenate([angles, angles], axis=-1)
    return (jnp.cos(angles), jnp.sin(angles))


def swiglu(gate_in, up_in):
    return jax.nn.silu(gate_in) * up_in


def dot(a, b, ca=1, cb=0):
    return lax.dot_general(a, b, (((ca,), (cb,)), ((), ())), preferred_element_type=jnp.float32)


def causal_copy(order_ref, k_ref, v_ref, sorted_ref):
    def move(slot, unused):
        half, core, y, z = slot % 2, slot // 2 % 2, slot // 4 % 4, slot // 16
        k_place = pl.multiple_of((((core * 4 + z) * 4 + y) * 2 + half) * SPAN, SPAN)
        v_place = pl.multiple_of((((core * 4 + y) * 4 + z) * 2 + half) * SPAN, SPAN)
        target = pl.ds(pl.multiple_of(order_ref[slot] * SPAN, SPAN), SPAN)
        sorted_ref[target, :128] = k_ref[pl.ds(k_place, SPAN), :]
        sorted_ref[target, 128:] = v_ref[pl.ds(v_place, SPAN), :]
        return unused

    lax.fori_loop(0, k_ref.shape[0] // SPAN, move, 0)


def visible(start, place, rows):
    key_place = lax.broadcasted_iota(jnp.int32, (CHUNK, rows), 0) + start
    lane = lax.broadcasted_iota(jnp.int32, (CHUNK, rows), 1)
    return key_place <= place * SPAN + lane % SPAN


def head_tile(heads, half, group):
    lanes = slice(half * SPAN, (half + 1) * SPAN)
    first = group * GROUP
    return jnp.concatenate([heads[first + item][:, lanes] for item in range(GROUP)], axis=1)


def padded(tile, group):
    empty = jnp.zeros_like(tile)
    return jnp.concatenate([tile, empty] if group == 0 else [empty, tile], axis=0)


def token_rows(tiles):
    blocks = []
    for tile in tiles:
        turned = tile.T
        blocks += [turned[item * SPAN : (item + 1) * SPAN] for item in range(GROUP)]
    pairs = [
        jnp.concatenate([blocks[2 * item], blocks[2 * item + 1]], axis=1) for item in range(GROUP)
    ]
    return jnp.concatenate(pairs, axis=1)


def prepare_kernel(
    x_ref,
    gain_ref,
    weight_ref,
    bias_ref,
    cos_ref,
    sin_ref,
    normed_ref,
    q_ref,
    q_rows_ref,
    k_ref,
    v_ref,
):
    wide = x_ref[...].astype(jnp.float32)
    scale = lax.rsqrt(jnp.mean(wide * wide, axis=-1, keepdims=True) + norm_eps)
    normed = (wide * scale * gain_ref[...]).astype(jnp.bfloat16)
    normed_ref[...] = normed
    mixed = dot(normed, weight_ref[...]) + bias_ref[...]
    count = QH + KVH
    v_ref[...] = mixed[:, count * HD :].astype(jnp.bfloat16)
    turned = mixed[:, : count * HD].T
    cosine, sine = cos_ref[...], sin_ref[...]
    heads = []
    for head in range(count):
        first = turned[head * HD : head * HD + HD // 2]
        second = turned[head * HD + HD // 2 : (head + 1) * HD]
        rotated = [first * cosine - second * sine, second * cosine + first * sine]
        heads.append(jnp.concatenate(rotated, axis=0))
    k_ref[...] = jnp.concatenate(heads[QH:], axis=0).T.astype(jnp.bfloat16)
    for half in range(2):
        for group in range(KVH):
            tile = padded(head_tile(heads, half, group) * HD**-0.5, group)
            q_ref[half, group] = tile.astype(jnp.bfloat16)
            q_rows_ref[half, group] = tile.T.astype(jnp.bfloat16)


def prepare(inputs, gain, weight, bias, cosine, sine):
    tokens = inputs.shape[0]
    rows = GROUP * SPAN
    vmem = pl.BlockSpec(memory_space=pltpu.VMEM)
    low = functools.partial(jax.ShapeDtypeStruct, dtype=jnp.bfloat16)
    return pl.pallas_call(
        prepare_kernel,
        out_shape=(
            low((tokens, D)),
            low((2, KVH, 128, rows)),
            low((2, KVH, rows, 128)),
            low((tokens, KVH * HD)),
            low((tokens, KVH * HD)),
        ),
        in_specs=[vmem] * 6,
        out_specs=(vmem,) * 5,
        compiler_params=pltpu.CompilerParams(vmem_limit_bytes=32 * 1024 * 1024),
        cost_estimate=pl.CostEstimate(flops=0, bytes_accessed=1_000_000, transcendentals=0),
        name="prepare",
    )(inputs, gain, weight, bias, cosine, sine)


def attend_kernel(
    order_ref,
    mine_ref,
    k_ref,
    v_ref,
    q_ref,
    x_ref,
    weight_ref,
    gain_ref,
    out_ref,
    lse_ref,
    attended_ref,
    residual_ref,
    normed_ref,
    sorted_ref,
):
    causal_copy(order_ref, k_ref, v_ref, sorted_ref)
    rows = q_ref.shape[-1]
    for half in range(2):
        place = mine_ref[half]
        last = place * SPAN // CHUNK

        def step(index, carry, masked, half=half, place=place):
            start = pl.multiple_of(index * CHUNK, CHUNK)
            keys = sorted_ref[pl.ds(start, CHUNK), :128]
            values = sorted_ref[pl.ds(start, CHUNK), 128:]
            result = []
            for head in range(KVH):
                top, total, mixed = carry[head]
                scores = dot(keys, q_ref[half, head])
                if masked:
                    scores = jnp.where(visible(start, place, rows), scores, masked_score)
                new_top = jnp.maximum(top, jnp.max(scores, axis=0, keepdims=True))
                shrink = jnp.exp(top - new_top)
                weights = jnp.exp(scores - new_top)
                total = total * shrink + jnp.sum(weights, axis=0, keepdims=True)
                mixed = mixed * shrink + dot(values, weights.astype(jnp.bfloat16), 0, 0)
                result.append((new_top, total, mixed))
            return tuple(result)

        empty = tuple(
            (
                jnp.full((1, rows), masked_score, jnp.float32),
                jnp.zeros((1, rows), jnp.float32),
                jnp.zeros((128, rows), jnp.float32),
            )
            for head in range(KVH)
        )
        carry = lax.fori_loop(0, last, functools.partial(step, masked=False), empty)
        carry = step(last, carry, True)
        tiles = []
        for head in range(KVH):
            top, total, mixed = carry[head]
            tiles.append(mixed[head * HD : (head + 1) * HD] / total)
            out_ref[half, head] = tiles[head]
            lse_ref[half, head] = top + jnp.log(total)
        place = pl.ds(half * SPAN, SPAN)
        attended_ref[place, :] = token_rows(tiles).astype(jnp.bfloat16)
    residual = x_ref[...].astype(jnp.float32) + dot(attended_ref[...], weight_ref[...])
    residual_ref[...] = residual
    scale = lax.rsqrt(jnp.mean(residual * residual, axis=-1, keepdims=True) + norm_eps)
    normed_ref[...] = (residual * scale * gain_ref[...]).astype(jnp.bfloat16)


def attend(order, mine, k_all, v_all, q_pad, inputs, weight, gain):
    halves, heads, unused, rows = q_pad.shape
    smem = pl.BlockSpec(memory_space=pltpu.SMEM)
    vmem = pl.BlockSpec(memory_space=pltpu.VMEM)
    return pl.pallas_call(
        attend_kernel,
        out_shape=(
            jax.ShapeDtypeStruct((halves, heads, HD, rows), jnp.float32),
            jax.ShapeDtypeStruct((halves, heads, 1, rows), jnp.float32),
            jax.ShapeDtypeStruct(inputs.shape, jnp.bfloat16),
            jax.ShapeDtypeStruct(inputs.shape, jnp.float32),
            jax.ShapeDtypeStruct(inputs.shape, jnp.bfloat16),
        ),
        in_specs=[smem, smem] + [vmem] * 6,
        out_specs=(vmem,) * 5,
        scratch_shapes=[pltpu.VMEM((k_all.shape[0], 256), k_all.dtype)],
        compiler_params=pltpu.CompilerParams(vmem_limit_bytes=48 * 1024 * 1024),
        cost_estimate=pl.CostEstimate(
            flops=0, bytes_accessed=1_000_000, transcendentals=0
        ),
        name="attend",
    )(order, mine, k_all, v_all, q_pad, inputs, weight, gain)


def attend_back_kernel(
    order_ref,
    mine_ref,
    k_ref,
    v_ref,
    q_ref,
    q_rows_ref,
    out_ref,
    lse_ref,
    d_normed_ref,
    residual_ref,
    cot_ref,
    gain_ref,
    weight_ref,
    cos_ref,
    sin_ref,
    dq_ref,
    dk_ref,
    dv_ref,
    d_residual_ref,
    d_branch_ref,
    gain_grad_ref,
    sorted_ref,
    sum_ref,
    do_ref,
    do_rows_ref,
    delta_ref,
):
    residual, d_normed = residual_ref[...], d_normed_ref[...]
    scale = lax.rsqrt(jnp.mean(residual * residual, axis=-1, keepdims=True) + norm_eps)
    unit = residual * scale
    gain_grad_ref[...] = jnp.sum(d_normed * unit, axis=0, keepdims=True)
    weighted = d_normed * gain_ref[...]
    inner = jnp.mean(weighted * unit, axis=-1, keepdims=True)
    d_residual = cot_ref[...].astype(jnp.float32) + scale * (weighted - unit * inner)
    d_residual_ref[...] = d_residual
    d_branch = d_residual.astype(jnp.bfloat16)
    d_branch_ref[...] = d_branch
    d_attended = dot(d_branch, weight_ref[...], 1, 1).astype(jnp.bfloat16).astype(jnp.float32)
    turned = d_attended.T
    heads = [turned[head * HD : (head + 1) * HD] for head in range(QH)]
    for half in range(2):
        for group in range(KVH):
            tile = head_tile(heads, half, group)
            product = tile * out_ref[half, group]
            delta_ref[half, group] = jnp.sum(product, axis=0, keepdims=True)
            tile = padded(tile, group)
            do_ref[half, group] = tile.astype(jnp.bfloat16)
            do_rows_ref[half, group] = tile.T.astype(jnp.bfloat16)
    causal_copy(order_ref, k_ref, v_ref, sorted_ref)
    sum_ref[...] = jnp.zeros_like(sum_ref)
    rows = q_ref.shape[-1]
    for half in range(2):
        place = mine_ref[half]
        last = place * SPAN // CHUNK

        def step(index, carry, masked, half=half, place=place):
            start = pl.multiple_of(index * CHUNK, CHUNK)
            keys = sorted_ref[pl.ds(start, CHUNK), :128]
            values = sorted_ref[pl.ds(start, CHUNK), 128:]
            d_keys = sum_ref[pl.ds(start, CHUNK), :128]
            d_values = sum_ref[pl.ds(start, CHUNK), 128:]
            result = []
            for head in range(KVH):
                scores = dot(keys, q_ref[half, head])
                probs = jnp.exp(scores - lse_ref[half, head])
                if masked:
                    probs = jnp.where(visible(start, place, rows), probs, 0.0)
                d_probs = dot(values, do_ref[half, head])
                d_scores = (probs * (d_probs - delta_ref[half, head])).astype(jnp.bfloat16)
                d_values += dot(probs.astype(jnp.bfloat16), do_rows_ref[half, head])
                d_keys += dot(d_scores, q_rows_ref[half, head])
                result.append(carry[head] + dot(keys, d_scores, 0, 0))
            sum_ref[pl.ds(start, CHUNK), :128] = d_keys
            sum_ref[pl.ds(start, CHUNK), 128:] = d_values
            return tuple(result)

        empty = tuple(jnp.zeros((128, rows), jnp.float32) for head in range(KVH))
        carry = lax.fori_loop(0, last, functools.partial(step, masked=False), empty)
        carry = step(last, carry, True)
        lanes = slice(half * SPAN, (half + 1) * SPAN)
        cosine = jnp.concatenate([cos_ref[:, lanes]] * GROUP, axis=1)
        sine = jnp.concatenate([sin_ref[:, lanes]] * GROUP, axis=1)
        tiles = []
        for head in range(KVH):
            middle = head * HD + HD // 2
            first = carry[head][head * HD : middle] * (HD**-0.5)
            second = carry[head][middle : (head + 1) * HD] * (HD**-0.5)
            turned = [first * cosine + second * sine, second * cosine - first * sine]
            tiles.append(jnp.concatenate(turned, axis=0))
        dq_ref[pl.ds(half * SPAN, SPAN), :] = token_rows(tiles).astype(jnp.bfloat16)

    def move(slot, unused):
        rest, y, z = slot % 4, slot // 4 % 4, slot // 16
        k_place = pl.multiple_of(slot * SPAN, SPAN)
        v_place = pl.multiple_of(((y * 4 + z) * 4 + rest) * SPAN, SPAN)
        source = pl.ds(pl.multiple_of(order_ref[slot] * SPAN, SPAN), SPAN)
        dk_ref[pl.ds(k_place, SPAN), :] = sum_ref[source, :128].astype(jnp.bfloat16)
        dv_ref[pl.ds(v_place, SPAN), :] = sum_ref[source, 128:].astype(jnp.bfloat16)
        return unused

    lax.fori_loop(0, dk_ref.shape[0] // SPAN, move, 0)


def attend_back(order, mine, k_all, v_all, q_pad, *rest):
    halves, heads, unused, rows = q_pad.shape
    tokens = 2 * SPAN
    smem = pl.BlockSpec(memory_space=pltpu.SMEM)
    vmem = pl.BlockSpec(memory_space=pltpu.VMEM)
    return pl.pallas_call(
        attend_back_kernel,
        out_shape=(
            jax.ShapeDtypeStruct((tokens, D), jnp.bfloat16),
            jax.ShapeDtypeStruct(k_all.shape, jnp.bfloat16),
            jax.ShapeDtypeStruct(v_all.shape, jnp.bfloat16),
            jax.ShapeDtypeStruct((tokens, D), jnp.float32),
            jax.ShapeDtypeStruct((tokens, D), jnp.bfloat16),
            jax.ShapeDtypeStruct((1, D), jnp.float32),
        ),
        in_specs=[smem, smem] + [vmem] * (3 + len(rest)),
        out_specs=(vmem,) * 6,
        scratch_shapes=[
            pltpu.VMEM((k_all.shape[0], 256), k_all.dtype),
            pltpu.VMEM((k_all.shape[0], 256), jnp.float32),
            pltpu.VMEM((halves, heads, 128, rows), jnp.bfloat16),
            pltpu.VMEM((halves, heads, rows, 128), jnp.bfloat16),
            pltpu.VMEM((halves, heads, 1, rows), jnp.float32),
        ],
        compiler_params=pltpu.CompilerParams(vmem_limit_bytes=48 * 1024 * 1024),
        cost_estimate=pl.CostEstimate(flops=0, bytes_accessed=1_000_000, transcendentals=0),
        name="attend_back",
    )(order, mine, k_all, v_all, q_pad, *rest)


def body(
    inputs,
    cotangent,
    span_order,
    positions,
    attn_gain,
    qkv_weight,
    qkv_bias,
    out_weight,
    mlp_gain,
    gate_weight,
    up_weight,
    down_weight,
):
    token_count = inputs.shape[0]
    q_cols = QH * HD
    k_cols = KVH * HD
    slices = lax.axis_size("dp")
    own_rows = D // slices
    part = FF // (slices * 2)
    dp = lax.axis_index("dp")
    core = lax.axis_index("core")
    slot = (lax.axis_index("z") * lax.axis_size("y") + lax.axis_index("y")) * 2 + core

    small = jnp.concatenate([attn_gain, mlp_gain, qkv_bias])
    small = jnp.pad(small, (0, 2048 - small.shape[0])).reshape(16, 128)
    qkv_half = lax.dynamic_slice_in_dim(qkv_weight, core * (own_rows // 2), own_rows // 2)
    qkv_full, small = communicate(
        "qkv_in", 0, (RingGather, ROW, qkv_half), (RingGather, ROW, small)
    )
    qkv_full = qkv_full.reshape(D, -1)
    small = small[:, 0].reshape(slices, -1)
    gain_one_wide = small[:, :own_rows].reshape(D).astype(jnp.float32)
    gain_two_wide = small[:, own_rows : 2 * own_rows].reshape(D).astype(jnp.float32)
    bias_full = small[:, 2 * own_rows : 2 * own_rows + qkv_bias.shape[0]]
    bias_full = bias_full.reshape(-1).astype(jnp.float32)
    out_full = lax.all_gather(out_weight, "dp", axis=0, tiled=True)

    def column_blocks(weight):
        parts = [weight[:, part * index : part * (index + 1)] for index in range(2 * slices)]
        return [jnp.where(core == 0, parts[2 * p], parts[2 * p + 1]) for p in range(slices)]

    gate_blocks, up_blocks = column_blocks(gate_weight), column_blocks(up_weight)
    gate_up = jnp.stack(
        [jnp.concatenate([gate_blocks[p], up_blocks[p]], axis=0) for p in range(slices)]
    )
    gate_up = lax.all_to_all(gate_up, "dp", 0, 0, tiled=True)
    gate_part = gate_up[:, :own_rows].reshape(D, part)
    up_part = gate_up[:, own_rows:].reshape(D, part)
    down_part = lax.dynamic_slice_in_dim(down_weight, core * part, part, axis=0)
    cot_all = lax.all_gather(cotangent, ("dp", "core"), axis=0, tiled=True)

    inputs_wide = inputs.astype(jnp.float32)
    cosine, sine = rope_tables(positions, HD)
    cos_turned, sin_turned = cosine[:, : HD // 2].T, sine[:, : HD // 2].T
    cosine = cosine[:, None, :]
    sine = sine[:, None, :]
    normed_one, q_pad, q_rows, key_rot, value_low = prepare(
        inputs, gain_one_wide[None], qkv_full, bias_full[None], cos_turned, sin_turned
    )
    normed_one_all = lax.all_gather(normed_one, ("dp", "core"), axis=0, tiled=True)
    k_all, v_all = communicate(
        "kv_in", 1, (PlaneGather, PLANE, key_rot), (PlaneGather, ENALP, value_low)
    )
    k_all = k_all.reshape(-1, k_cols)
    v_all = v_all.reshape(-1, k_cols)
    mine = lax.dynamic_slice_in_dim(span_order, 2 * slot, 2)
    attended_cols, lse, attended_low, residual, normed_two = attend(
        span_order, mine, k_all, v_all, q_pad, inputs, out_full, gain_two_wide[None]
    )
    attended_all = lax.all_gather(attended_low, ("dp", "core"), axis=0, tiled=True)
    (normed_two, normed_one_all) = lax.optimization_barrier((normed_two, normed_one_all))
    (normed_all,) = communicate("normed_in", 2, (RingGather, ROW, normed_two))
    normed_all = normed_all.reshape(-1, D)
    gate_proj = dot(normed_all, gate_part)
    up_proj = dot(normed_all, up_part)
    hidden_low = swiglu(gate_proj, up_proj).astype(jnp.bfloat16)
    out_sum = dot(hidden_low, down_part).astype(jnp.bfloat16)
    d_hidden = dot(cot_all, down_part, 1, 1)
    d_gate, d_up = jax.vjp(swiglu, gate_proj, up_proj)[1](d_hidden)
    d_gate = d_gate.astype(jnp.bfloat16)
    d_up = d_up.astype(jnp.bfloat16)
    d_norm_sum = (dot(d_gate, gate_part, 1, 1) + dot(d_up, up_part, 1, 1)).astype(jnp.bfloat16)
    blocks = (slices, 2, token_count, D)
    low = functools.partial(jax.ShapeDtypeStruct, dtype=jnp.bfloat16)
    columns = low((4, 4, slices, ROWS, part))
    d_normed_two, out_rows, gate_grad, up_grad, down_low, down_high = communicate(
        "d_normed_out",
        3,
        (RingScatter, ROW, d_norm_sum.reshape(blocks)),
        (RingScatter, ROW, out_sum.reshape(blocks)),
        compute=((gate_grads, 1), (up_grads, 1), (down_grads, 2)),
        inputs=(normed_all, cot_all, hidden_low, d_gate, d_up),
        after=(
            (AxisScatter, ("z",), columns),
            (AxisScatter, ("y",), columns),
            (AxisScatter, ("z",), low((4, 4, DOWN_ROWS, DOWN_CUT))),
            (AxisScatter, ("y",), low((4, 4, DOWN_ROWS, D - DOWN_CUT))),
        ),
    )
    output = (residual + out_rows).astype(jnp.bfloat16)

    d_normed_two, attended_all = lax.optimization_barrier((d_normed_two, attended_all))
    d_query_low, d_k_all, d_v_all, d_residual, d_branch, gain_two_grad = attend_back(
        span_order,
        mine,
        k_all,
        v_all,
        q_pad,
        q_rows,
        attended_cols,
        lse,
        d_normed_two,
        residual,
        cotangent,
        gain_two_wide[None],
        out_full,
        cos_turned,
        sin_turned,
    )

    def turn_back(grads):
        scaled = grads * sine
        middle = HD // 2
        back = jnp.concatenate([scaled[..., middle:], -scaled[..., :middle]], axis=-1)
        return grads * cosine + back

    paired = functools.partial(PlaneScatter, pair=True)
    pairs = (4, 4, 2, token_count, k_cols)
    d_k, d_v, d_query_all, d_branch_all, gate_grad, up_grad, down_low, down_high = communicate(
        "d_kv_out",
        4,
        (paired, PLANE, d_k_all.reshape(pairs)),
        (paired, ENALP, d_v_all.reshape(pairs)),
        (RingGather, ROW, d_query_low),
        (RingGather, ROW, d_branch),
        (Deal, ("y",), gate_grad),
        (Deal, ("z",), up_grad),
        (AxisScatter, ("y",), down_low),
        (AxisScatter, ("z",), down_high),
    )
    d_key_raw = turn_back(d_k.reshape(token_count, KVH, HD))
    d_kv_low = jnp.concatenate(
        [d_key_raw.reshape(token_count, k_cols), d_v], axis=1
    ).astype(jnp.bfloat16)
    d_mixed = jnp.concatenate([d_query_low, d_kv_low], axis=1)
    d_normed_one = dot(d_mixed, qkv_full, 1, 1)
    d_input_part, gain_one_grad = jax.vjp(rms_apply, inputs_wide, gain_one_wide)[1](d_normed_one)
    input_grad = (d_input_part + d_residual).astype(jnp.bfloat16)
    gain_grads = jnp.concatenate([gain_one_grad, gain_two_grad[0]])
    gain_grads = jnp.pad(gain_grads, (0, 2048 - 2 * D)).reshape(16, 128)
    d_kv_rows, gain_grads, gate_grad, up_grad, down_low, down_high = communicate(
        "d_kv_in",
        5,
        (RingGather, ROW, d_kv_low),
        (RingGather, ROW, gain_grads),
        (AxisGather, ("y",), gate_grad),
        (AxisGather, ("z",), up_grad),
        (PlaneGather, PLANE, down_low),
        (PlaneGather, ENALP, down_high),
    )
    d_mixed_all = jnp.concatenate(
        [d_query_all.reshape(-1, q_cols), d_kv_rows.reshape(-1, 2 * k_cols)], axis=1
    )
    gain_grads = jnp.sum(gain_grads.reshape(2 * slices, -1), axis=0)
    bias_grad = jnp.sum(d_mixed_all.astype(jnp.float32), axis=0)

    half_rows = own_rows // 2
    first = dp * own_rows + core * half_rows

    def my_columns(tokens):
        return lax.dynamic_slice_in_dim(tokens, first, half_rows, axis=1)

    out_grad = dot(my_columns(attended_all), d_branch_all.reshape(-1, D), 0, 0)
    qkv_grad = dot(my_columns(normed_one_all), d_mixed_all, 0, 0)
    chips = 16
    width = chips * 128
    sums = jnp.concatenate(
        [
            jnp.concatenate([qkv_grad, out_grad], axis=1),
            jnp.pad(bias_grad, (0, width - bias_grad.shape[0]))[None],
            jnp.pad(gain_grads, (0, width - gain_grads.shape[0]))[None],
            jnp.zeros((14, width), jnp.float32),
        ],
        axis=0,
    ).astype(jnp.bfloat16)
    sums = sums.reshape(128, 4, 4, 128).transpose(1, 2, 0, 3)
    shared = functools.partial(AxisGather, share=True)
    sums_top, sums_end, gate_grad, up_grad = communicate(
        "grads",
        6,
        (PlaneTotal, PLANE, sums[:, :, :64]),
        (PlaneTotal, ENALP, sums[:, :, 64:].transpose(1, 0, 2, 3)),
        (shared, ("z",), gate_grad),
        (shared, ("y",), up_grad),
    )
    qkv_grad, out_grad, vectors = split_sums(
        sums_top, sums_end, half_rows, q_cols + 2 * k_cols
    )
    bias_grad, gain_grads = vectors[0], vectors[1]

    def owned(vector, start, count):
        width = count // slices
        return lax.dynamic_slice_in_dim(vector, start + dp * width, width)

    gate_grad, up_grad = widen(gate_grad, up_grad)
    down_grad = widen_down(down_low, down_high, part)
    return (
        output,
        input_grad,
        owned(gain_grads, 0, D),
        qkv_grad,
        owned(bias_grad, 0, q_cols + k_cols),
        owned(bias_grad, q_cols + k_cols, k_cols),
        out_grad,
        owned(gain_grads, D, D),
        gate_grad,
        up_grad,
        down_grad,
    )


def solution(mesh):
    grid = Mesh(mesh.devices.reshape(4, 4, 4, 2), ("dp", "z", "y", "core"))
    tokens = ("dp",) + CTX
    return jax.shard_map(
        body,
        mesh=grid,
        in_specs=(
            P(tokens, None),
            P(tokens, None),
            P(),
            P(tokens),
            P("dp"),
            P("dp", None),
            P("dp"),
            P("dp", None),
            P("dp"),
            P("dp", None),
            P("dp", None),
            P("dp", None),
        ),
        out_specs=(
            P(tokens, None),
            P(tokens, None),
            P("dp"),
            P("dp", None),
            P("dp"),
            P("dp"),
            P("dp", None),
            P("dp"),
            P("dp", None),
            P("dp", None),
            P("dp", None),
        ),
        check_vma=False,
    )
```

```python
import functools

import jax
import jax.numpy as jnp
from jax import lax
from jax.experimental import pallas as pl
from jax.experimental.pallas import tpu as pltpu
from jax.sharding import Mesh, PartitionSpec as P

QH = 14
KVH = 2
HD = 64
GROUP = QH // KVH
D = 896
FF = 4864
SPAN = 64
CHUNK = 512

norm_eps = 1e-06
rope_base = 1000000.0
masked_score = -1e30
CTX = ("z", "y", "core")
ROW = ("dp",)
PLANE = ("z", "y")
ENALP = ("y", "z")

MESH = pl.DeviceIdType.MESH
SIZES = {"dp": 4, "z": 4, "y": 4}


def group_size(axes):
    size = 1
    for axis in axes:
        size *= SIZES[axis]
    return size


def group_index(axes):
    index = 0
    for axis in axes:
        index = index * SIZES[axis] + lax.axis_index(axis)
    return index


def member(axes, index):
    found = {}
    for axis in reversed(axes):
        found[axis] = index % SIZES[axis]
        index = index // SIZES[axis]
    return found


def remote(source, target, send, receive, device):
    return pltpu.make_async_remote_copy(
        src_ref=source,
        dst_ref=target,
        send_sem=send,
        recv_sem=receive,
        device_id=device,
        device_id_type=MESH,
    )


class Exchange:
    def __init__(self, axes, array):
        self.axes, self.n = axes, group_size(axes)
        self.in_space = pltpu.VMEM
        self.out = jax.ShapeDtypeStruct(array.shape, array.dtype)
        self.out_space = pl.ANY
        self.scratch = [pltpu.SemaphoreType.DMA] + [pltpu.SemaphoreType.DMA((self.n,))] * 2

    def bind(self, source, target, scratch):
        self.x, self.o = source, target
        self.local, self.send, self.receive = scratch
        self.me = group_index(self.axes)
        self.stages = [self.start, self.end]

    def mine(self):
        return pltpu.make_async_copy(self.x.at[self.me], self.o.at[self.me], self.local)

    def outward(self, k, slot):
        to = (self.me + k) % self.n
        device = member(self.axes, to)
        send, receive = self.send.at[k], self.receive.at[k]
        return remote(self.x.at[to], self.o.at[slot], send, receive, device)

    def start(self):
        self.mine().start()
        for k in range(1, self.n):
            self.outward(k, self.me).start()

    def end(self):
        self.mine().wait()
        for k in range(1, self.n):
            self.outward(k, self.me).wait_send()
            self.outward(k, (self.me + self.n - k) % self.n).wait_recv()


class PlaneGather:
    def __init__(self, axes, array):
        self.axes = axes
        self.in_space = pltpu.VMEM
        self.out = jax.ShapeDtypeStruct((2, 4, 4) + array.shape, array.dtype)
        self.out_space = pl.ANY
        self.scratch = [pltpu.SemaphoreType.DMA] + [pltpu.SemaphoreType.DMA((4,))] * 6

    def bind(self, source, target, scratch):
        self.x, self.o, self.local = source, target, scratch[0]
        self.s_one, self.r_one, self.s_two, self.r_two, self.s_core, self.r_core = scratch[1:]
        self.one, self.two = (lax.axis_index(axis) for axis in self.axes)
        self.core = lax.axis_index("core")
        self.stages = [self.start, self.middle, self.late, self.end]

    def mine(self):
        place = self.o.at[self.core, self.one, self.two]
        return pltpu.make_async_copy(self.x, place, self.local)

    def first(self, k, slot):
        device = {self.axes[1]: (self.two + k) % 4}
        place = self.o.at[self.core, self.one, slot]
        return remote(self.x, place, self.s_one.at[k], self.r_one.at[k], device)

    def second(self, k, row):
        device = {self.axes[0]: (self.one + k) % 4}
        place = self.o.at[self.core, row]
        return remote(place, place, self.s_two.at[k], self.r_two.at[k], device)

    def across(self, k, core):
        place = self.o.at[core, (self.one + 4 - k) % 4]
        device = {"core": 1 - self.core}
        return remote(place, place, self.s_core.at[k], self.r_core.at[k], device)

    def start(self):
        for k in (2, 1, 3):
            self.first(k, self.two).start()
        self.mine().start()

    def middle(self):
        self.mine().wait()
        for k in range(1, 4):
            self.first(k, (self.two + 4 - k) % 4).wait_recv()
        for k in (2, 1, 3):
            self.second(k, self.one).start()
        self.across(0, self.core).start()

    def late(self):
        for k in (1, 3, 2):
            self.second(k, (self.one + 4 - k) % 4).wait_recv()
            self.across(k, self.core).start()

    def end(self):
        for k in range(4):
            if k:
                self.first(k, self.two).wait_send()
                self.second(k, self.one).wait_send()
            self.across(k, self.core).wait_send()
            self.across(k, 1 - self.core).wait_recv()


class PlaneScatter:
    def __init__(self, axes, array, pair=False, kind=jnp.float32):
        self.axes, self.pair = axes, pair
        self.block = array.shape[3 if pair else 2 :]
        self.in_space = pltpu.VMEM
        self.out = jax.ShapeDtypeStruct(self.block, kind)
        self.out_space = pltpu.VMEM
        self.kind = array.dtype
        row = (4,) + self.block
        self.scratch = [
            pltpu.VMEM((4,) + row, self.kind),
            pltpu.VMEM(row, jnp.float32),
            pltpu.VMEM(row, self.kind),
            pltpu.VMEM(row, self.kind),
        ]
        if pair:
            self.scratch += [pltpu.VMEM((4,) + row, self.kind)] * 2
            self.scratch += [pltpu.SemaphoreType.DMA((4,))] * 2
        self.scratch += [pltpu.SemaphoreType.DMA((4,))] * 4

    def bind(self, source, target, scratch):
        self.x, self.o = source, target
        self.land, self.total, self.low, self.last = scratch[:4]
        if self.pair:
            self.half, self.summed, self.s_core, self.r_core = scratch[4:8]
        self.s_one, self.r_one, self.s_two, self.r_two = scratch[-4:]
        self.one, self.two = (lax.axis_index(axis) for axis in self.axes)
        self.core = lax.axis_index("core")
        self.stages = [self.start, self.middle, self.late, self.end]

    def across(self, k):
        to = (self.one + k) % 4
        source = self.x.at[to, :, 1 - self.core]
        device = {"core": 1 - self.core}
        return remote(source, self.half.at[to], self.s_core.at[k], self.r_core.at[k], device)

    def first(self, k, slot):
        to = (self.one + k) % 4
        source = self.summed if self.pair else self.x
        send, receive = self.s_one.at[k], self.r_one.at[k]
        return remote(source.at[to], self.land.at[slot], send, receive, {self.axes[0]: to})

    def second(self, k, slot):
        to = (self.two + k) % 4
        send, receive = self.s_two.at[k], self.r_two.at[k]
        return remote(self.low.at[to], self.last.at[slot], send, receive, {self.axes[1]: to})

    def start(self):
        for k in (2, 1, 3):
            if self.pair:
                self.across(k).start()
            else:
                self.first(k, self.one).start()
        if self.pair:
            self.across(0).start()

    def middle(self):
        if self.pair:
            for k in (2, 1, 3, 0):
                to = (self.one + k) % 4
                self.across(k).wait_recv()
                for item in range(4):
                    both = self.x[to, item, self.core].astype(jnp.float32)
                    both += self.half[to, item].astype(jnp.float32)
                    if k:
                        self.summed[to, item] = both.astype(self.kind)
                    else:
                        self.total[item] = both
                if k:
                    self.first(k, self.one).start()

    def late(self):
        slots = [(self.one + 4 - k) % 4 for k in range(4)]
        for k in range(1, 4):
            self.first(k, slots[k]).wait_recv()
        for item in range(4):
            if self.pair:
                total = self.total[item]
            else:
                total = self.x[self.one, item].astype(jnp.float32)
            for k in range(1, 4):
                total += self.land[slots[k], item].astype(jnp.float32)
            self.total[item] = total
            self.low[item] = total.astype(self.kind)
        for k in (2, 1, 3):
            self.second(k, self.two).start()

    def end(self):
        total = self.total[self.two]
        for k in range(1, 4):
            slot = (self.two + 4 - k) % 4
            self.second(k, slot).wait_recv()
            total += self.last[slot].astype(jnp.float32)
        self.o[...] = total.astype(self.o.dtype)
        for k in range(4):
            if k:
                self.first(k, self.one).wait_send()
                self.second(k, self.two).wait_send()
            if self.pair:
                self.across(k).wait_send()


class PlaneTotal:
    def __init__(self, axes, array):
        self.axes = axes
        self.scatter = PlaneScatter(axes, array, kind=array.dtype)
        self.gather = PlaneGather(axes, self.scatter.out)
        self.in_space = pltpu.VMEM
        self.out, self.out_space = self.gather.out, pl.ANY
        own = pltpu.VMEM(self.scatter.block, array.dtype)
        self.scratch = [own] + self.scatter.scratch + self.gather.scratch

    def bind(self, source, target, scratch):
        count = 1 + len(self.scatter.scratch)
        self.scatter.bind(source, scratch[0], scratch[1:count])
        self.gather.bind(scratch[0], target, scratch[count:])
        self.stages = self.scatter.stages + self.gather.stages


def split_point(rows):
    return rows if rows < 32 else (rows // 2 + 15) // 16 * 16


class RingGather:
    def __init__(self, axes, array):
        self.axes, self.n = axes, group_size(axes)
        self.block, self.dtype = array.shape, array.dtype
        self.cut = split_point(self.block[0])
        self.in_space = pltpu.VMEM
        self.out = jax.ShapeDtypeStruct((self.n, 2) + self.block, self.dtype)
        self.out_space = pl.ANY
        self.scratch = [pltpu.SemaphoreType.DMA] + [pltpu.SemaphoreType.DMA((4,))] * 4

    def bind(self, source, target, scratch):
        self.x, self.o = source, target
        self.local, self.send, self.receive, self.f_send, self.f_receive = scratch
        self.me, self.core = group_index(self.axes), lax.axis_index("core")
        self.stages = [self.start, self.middle, self.late, self.end]

    def at(self, shift, core):
        return self.o.at[(self.me + shift) % 4, core]

    def mine(self):
        return pltpu.make_async_copy(self.x, self.at(0, self.core), self.local)

    def copy(self, step, to, source, target):
        device = member(self.axes, (self.me + to) % 4)
        return remote(source, target, self.send.at[step], self.receive.at[step], device)

    def piece(self, shift, low):
        ref = self.at(shift, self.core)
        rows = pl.ds(0, self.cut) if low else pl.ds(self.cut, self.block[0] - self.cut)
        return ref.at[rows]

    def sends(self):
        place = self.at(0, self.core)
        low, high = self.piece(3, True), None
        found = [self.copy(0, 1, self.x, place), self.copy(1, 3, self.x, place)]
        found.append(self.copy(2, 1, low, low))
        if self.cut < self.block[0]:
            high = self.piece(1, False)
            found.append(self.copy(3, 3, high, high))
        return found

    def receipts(self):
        found = [
            self.copy(0, 1, self.x, self.at(3, self.core)),
            self.copy(1, 3, self.x, self.at(1, self.core)),
        ]
        low = self.piece(2, True)
        found.append(self.copy(2, 1, low, low))
        if self.cut < self.block[0]:
            high = self.piece(2, False)
            found.append(self.copy(3, 3, high, high))
        return found

    def forward(self, step, core):
        place = self.at((0, 3, 1, 2)[step], core)
        source = self.x if step == 0 else place
        device = {"core": 1 - self.core}
        return remote(source, place, self.f_send.at[step], self.f_receive.at[step], device)

    def start(self):
        sends = self.sends()
        sends[0].start()
        sends[1].start()
        self.mine().start()
        self.forward(0, self.core).start()

    def middle(self):
        sends, receipts = self.sends(), self.receipts()
        for step in range(2):
            receipts[step].wait_recv()
            if step + 2 < len(sends):
                sends[step + 2].start()
            self.forward(step + 1, self.core).start()

    def late(self):
        for receipt in self.receipts()[2:]:
            receipt.wait_recv()
        self.forward(3, self.core).start()

    def end(self):
        self.mine().wait()
        for send in self.sends():
            send.wait_send()
        for step in range(4):
            self.forward(step, self.core).wait_send()
            self.forward(step, 1 - self.core).wait_recv()


class RingScatter:
    def __init__(self, axes, array):
        self.axes = axes
        self.block = array.shape[2:]
        self.cut = split_point(self.block[0])
        self.in_space = pltpu.VMEM
        self.out = jax.ShapeDtypeStruct(self.block, jnp.float32)
        self.out_space = pltpu.VMEM
        rows = (self.cut, self.block[0] - self.cut)
        self.scratch = [pltpu.VMEM((4,) + self.block, array.dtype)] * 2
        self.scratch += [pltpu.VMEM((count,) + self.block[1:], array.dtype) for count in rows]
        self.scratch += [pltpu.VMEM((2,) + self.block, array.dtype)]
        self.scratch += [pltpu.SemaphoreType.DMA((4,))] * 4

    def bind(self, source, target, scratch):
        self.x, self.o = source, target
        self.half, self.summed = scratch[:2]
        self.via, self.land = scratch[2:4], scratch[4]
        self.s_one, self.r_one, self.send, self.receive = scratch[5:]
        self.me, self.core = group_index(self.axes), lax.axis_index("core")
        self.stages = [self.start, self.middle, self.late, self.end]

    def across(self, shift):
        to = (self.me + shift) % 4
        return remote(
            self.x.at[to, 1 - self.core],
            self.half.at[to],
            self.s_one.at[shift],
            self.r_one.at[shift],
            {"core": 1 - self.core},
        )

    def copy(self, step, to, source, target):
        device = member(self.axes, (self.me + to) % 4)
        return remote(source, target, self.send.at[step], self.receive.at[step], device)

    def copies(self):
        far = self.summed.at[(self.me + 2) % 4]
        low, high = pl.ds(0, self.cut), pl.ds(self.cut, self.block[0] - self.cut)
        return [
            self.copy(0, 1, far.at[low], self.via[0]),
            self.copy(1, 3, far.at[high], self.via[1]),
            self.copy(2, 1, self.summed.at[(self.me + 1) % 4], self.land.at[0]),
            self.copy(3, 3, self.summed.at[(self.me + 3) % 4], self.land.at[1]),
        ]

    def both(self, shift):
        self.across(shift).wait_recv()
        to = (self.me + shift) % 4
        return self.x[to, self.core].astype(jnp.float32) + self.half[to].astype(jnp.float32)

    def start(self):
        for shift in (2, 1, 3, 0):
            self.across(shift).start()

    def middle(self):
        copies = self.copies()
        kind = self.summed.dtype
        self.summed[(self.me + 2) % 4] = self.both(2).astype(kind)
        copies[0].start()
        copies[1].start()
        near, back = self.both(1), self.both(3)
        cut = self.cut
        after, before = (self.me + 1) % 4, (self.me + 3) % 4
        copies[0].wait_recv()
        self.summed[after, :cut] = (near[:cut] + self.via[0][...].astype(jnp.float32)).astype(kind)
        self.summed[after, cut:] = near[cut:].astype(kind)
        copies[2].start()
        copies[1].wait_recv()
        self.summed[before, cut:] = (back[cut:] + self.via[1][...].astype(jnp.float32)).astype(kind)
        self.summed[before, :cut] = back[:cut].astype(kind)
        copies[3].start()
        self.o[...] = self.both(0)

    def late(self):
        pass

    def end(self):
        copies = self.copies()
        for step in range(2):
            copies[step + 2].wait_recv()
            self.o[...] += self.land[step].astype(jnp.float32)
        for shift in range(4):
            self.across(shift).wait_send()
            copies[shift].wait_send()


class AxisScatter:
    def __init__(self, axes, array):
        self.axes = axes
        self.block, self.kind = array.shape[1:], array.dtype
        self.in_space = pltpu.VMEM
        self.out = jax.ShapeDtypeStruct(self.block, self.kind)
        self.out_space = pltpu.VMEM
        self.scratch = [pltpu.VMEM(array.shape, self.kind)] + [pltpu.SemaphoreType.DMA((4,))] * 2

    def bind(self, source, target, scratch):
        self.x, self.o = source, target
        self.land, self.send, self.receive = scratch
        self.me = lax.axis_index(self.axes[0])
        self.stages = [self.start, self.end]

    def outward(self, k, slot):
        to = (self.me + k) % 4
        send, receive = self.send.at[k], self.receive.at[k]
        return remote(self.x.at[to], self.land.at[slot], send, receive, {self.axes[0]: to})

    def start(self):
        for k in (2, 1, 3):
            self.outward(k, self.me).start()

    def end(self):
        slots = [(self.me + 4 - k) % 4 for k in range(4)]
        for k in range(1, 4):
            self.outward(k, slots[k]).wait_recv()
        for item in range(self.block[0] if len(self.block) > 2 else 1):
            at = (item,) if len(self.block) > 2 else ()
            total = self.x[(self.me,) + at].astype(jnp.float32)
            for k in range(1, 4):
                total += self.land[(slots[k],) + at].astype(jnp.float32)
            if at:
                self.o[item] = total.astype(self.kind)
            else:
                self.o[...] = total.astype(self.kind)
        for k in range(1, 4):
            self.outward(k, self.me).wait_send()


class AxisGather:
    def __init__(self, axes, array, share=False):
        self.axes, self.share = axes, share
        self.in_space = pltpu.VMEM
        lead = (2, 4) if share else (4,)
        self.out = jax.ShapeDtypeStruct(lead + array.shape, array.dtype)
        self.out_space = pl.ANY
        self.scratch = [pltpu.SemaphoreType.DMA] + [pltpu.SemaphoreType.DMA((4,))] * 4

    def bind(self, source, target, scratch):
        self.x, self.o, self.local = source, target, scratch[0]
        self.send, self.receive, self.f_send, self.f_receive = scratch[1:]
        self.me, self.core = lax.axis_index(self.axes[0]), lax.axis_index("core")
        self.stages = [self.start, self.late, self.end] if self.share else [self.start, self.end]

    def at(self, slot, core):
        return self.o.at[core, slot] if self.share else self.o.at[slot]

    def mine(self):
        return pltpu.make_async_copy(self.x, self.at(self.me, self.core), self.local)

    def outward(self, k, slot):
        send, receive = self.send.at[k], self.receive.at[k]
        device = {self.axes[0]: (self.me + k) % 4}
        return remote(self.x, self.at(slot, self.core), send, receive, device)

    def forward(self, k, core):
        place = self.at((self.me + 4 - k) % 4, core)
        send, receive = self.f_send.at[k], self.f_receive.at[k]
        source = place if k else self.x
        return remote(source, place, send, receive, {"core": 1 - self.core})

    def start(self):
        for k in (2, 1, 3):
            self.outward(k, self.me).start()
        self.mine().start()
        if self.share:
            self.forward(0, self.core).start()

    def late(self):
        for k in (1, 3, 2):
            self.outward(k, (self.me + 4 - k) % 4).wait_recv()
            self.forward(k, self.core).start()

    def end(self):
        self.mine().wait()
        for k in range(4):
            if k:
                self.outward(k, self.me).wait_send()
                if not self.share:
                    self.outward(k, (self.me + 4 - k) % 4).wait_recv()
            if self.share:
                self.forward(k, self.core).wait_send()
                self.forward(k, 1 - self.core).wait_recv()


class Deal:
    def __init__(self, axes, array):
        self.axes = axes + ROW
        self.scatter = AxisScatter(axes, array)
        self.exchange = Exchange(ROW, self.scatter.out)
        self.in_space = pltpu.VMEM
        self.out, self.out_space = self.exchange.out, pl.ANY
        own = pltpu.VMEM(self.scatter.block, array.dtype)
        self.scratch = [own] + self.scatter.scratch + self.exchange.scratch

    def bind(self, source, target, scratch):
        count = 1 + len(self.scatter.scratch)
        self.scatter.bind(source, scratch[0], scratch[1:count])
        self.exchange.bind(scratch[0], target, scratch[count:])
        self.stages = self.scatter.stages + self.exchange.stages


def run_stages(ops):
    longest = max(len(op.stages) for op in ops)
    for index in range(longest - 1):
        for op in ops:
            if index < len(op.stages) - 1:
                op.stages[index]()
    for op in ops:
        op.stages[-1]()


def communicate_kernel(ops, after, compute, inputs, *refs):
    refs = list(refs)
    count, more, waiting = len(ops), len(after), after
    sources, extra = refs[:count], refs[count : count + inputs]
    refs = refs[count + inputs :]
    targets, late_targets = refs[:count], refs[count : count + more]
    scratch = refs[count + more :]
    late_sources = [scratch.pop(0) for unused in after]
    axes = []
    for op, source, target in zip(ops + after, sources + late_sources, targets + late_targets):
        op.bind(source, target, [scratch.pop(0) for unused in op.scratch])
        axes += [axis for axis in op.axes if axis not in axes]
    barrier = pltpu.get_barrier_semaphore()
    devices = [{"core": 1 - lax.axis_index("core")}]
    for axis in axes:
        devices += [{axis: (lax.axis_index(axis) + k) % 4} for k in range(1, 4)]
    for device in devices:
        pl.semaphore_signal(barrier, inc=1, device_id=device, device_id_type=MESH)
    pl.semaphore_wait(barrier, len(devices))
    if compute is None:
        run_stages(ops)
    else:
        for op in ops:
            op.stages[0]()
        for function, count in compute:
            function(*extra, *late_sources)
            for op in after[:count]:
                op.stages[0]()
            after = after[count:]
        for stage in (1, 2, 3):
            for op in ops:
                op.stages[stage]()
        for op in waiting:
            op.stages[1]()


def communicate(name, identity, *requests, compute=None, inputs=(), after=()):
    arrays = [array for kind, axes, array in requests]
    ops = [kind(axes, array) for kind, axes, array in requests]
    late = [kind(axes, array) for kind, axes, array in after]
    held = [pltpu.VMEM(array.shape, array.dtype) for kind, axes, array in after]
    vmem = pl.BlockSpec(memory_space=pltpu.VMEM)
    return pl.pallas_call(
        functools.partial(communicate_kernel, ops, late, compute, len(inputs)),
        out_shape=tuple(op.out for op in ops + late),
        in_specs=[pl.BlockSpec(memory_space=op.in_space) for op in ops] + [vmem] * len(inputs),
        out_specs=tuple(pl.BlockSpec(memory_space=op.out_space) for op in ops + late),
        scratch_shapes=held + [item for op in ops + late for item in op.scratch],
        compiler_params=pltpu.CompilerParams(
            collective_id=identity,
            has_side_effects=True,
            vmem_limit_bytes=56 * 1024 * 1024,
        ),
        cost_estimate=pl.CostEstimate(flops=0, bytes_accessed=1_000_000, transcendentals=0),
        name=name,
    )(*arrays, *inputs)


ROWS = 16
GROUPS = 14
DOWN_ROWS = 48
DOWN_CUT = 512


def store_groups(index, value, target, swapped):
    for item in range(128 // ROWS):
        group = index * (128 // ROWS) + item
        owner, chip = group // GROUPS, group % GROUPS
        z, y = chip // 4, chip % 4
        spot = (y, z) if swapped else (z, y)
        target[spot + (owner,)] = value[item * ROWS : (item + 1) * ROWS]


def gate_or_up_grads(normed_ref, d_ref, target, swapped):
    for chip in range(GROUPS, 16):
        z, y = chip // 4, chip % 4
        target[(y, z) if swapped else (z, y)] = jnp.zeros(target.shape[2:], target.dtype)

    def step(index, unused):
        place = pl.ds(pl.multiple_of(index * 128, 128), 128)
        value = dot(normed_ref[:, place], d_ref[...], 0, 0).astype(jnp.bfloat16)
        store_groups(index, value, target, swapped)
        return unused

    lax.fori_loop(0, D // 128, step, 0)


def gate_grads(normed, cot, hidden, d_gate, d_up, gate, up, down, rest):
    gate_or_up_grads(normed, d_gate, gate, False)


def up_grads(normed, cot, hidden, d_gate, d_up, gate, up, down, rest):
    gate_or_up_grads(normed, d_up, up, True)


def down_grads(normed, cot_ref, hidden_ref, d_gate, d_up, gate, up, down_ref, rest_ref):
    part = hidden_ref.shape[1]
    for chip in range(part // DOWN_ROWS, 16):
        z, y = chip // 4, chip % 4
        down_ref[z, y] = jnp.zeros(down_ref.shape[2:], down_ref.dtype)
        rest_ref[y, z] = jnp.zeros(rest_ref.shape[2:], rest_ref.dtype)

    def step(index, target, swapped, start):
        place = pl.ds(pl.multiple_of(index * 128, 128), 128)
        down = dot(cot_ref[:, place], hidden_ref[...], 0, 0).T.astype(jnp.bfloat16)
        columns = pl.ds(pl.multiple_of(index * 128 - start, 128), 128)
        for chip in range(-(-part // DOWN_ROWS)):
            first = chip * DOWN_ROWS
            rows = min(DOWN_ROWS, part - first)
            z, y = chip // 4, chip % 4
            spot = (y, z) if swapped else (z, y)
            target[spot + (pl.ds(0, rows), columns)] = down[first : first + rows]

    def low_step(index, unused):
        step(index, down_ref, False, 0)
        return unused

    def high_step(index, unused):
        step(index, rest_ref, True, DOWN_CUT)
        return unused

    lax.fori_loop(0, DOWN_CUT // 128, low_step, 0)
    lax.fori_loop(DOWN_CUT // 128, D // 128, high_step, 0)


def widen_kernel(gate_ref, up_ref, gate_out_ref, up_out_ref):
    part = gate_ref.shape[-1]
    for source, target in ((gate_ref, gate_out_ref), (up_ref, up_out_ref)):
        for index in range(4):
            for core in range(2):
                first = (2 * index + core) * part
                for item in range(2):
                    spot = (core, 0, item, index) if source is gate_ref else (core, item, 0, index)
                    rows = slice(item * ROWS, (item + 1) * ROWS)
                    target[rows, first : first + part] = source[spot].astype(jnp.float32)


def widen(gate, up):
    part = gate.shape[-1]
    target = pl.BlockSpec((2 * ROWS, 8 * part), lambda index: (index, 0))
    wide = jax.ShapeDtypeStruct((ROWS * GROUPS, 8 * part), jnp.float32)
    return pl.pallas_call(
        widen_kernel,
        grid=(GROUPS // 2,),
        out_shape=(wide, wide),
        in_specs=[
            pl.BlockSpec(
                (2, 1, 2, 4, ROWS, part), lambda index: (0, index // 2, index % 2, 0, 0, 0)
            ),
            pl.BlockSpec(
                (2, 2, 1, 4, ROWS, part), lambda index: (0, index % 2, index // 2, 0, 0, 0)
            ),
        ],
        out_specs=(target, target),
        name="widen",
    )(gate, up)


def widen_down_kernel(low_ref, high_ref, out_ref):
    part = out_ref.shape[0] // 2
    for core in range(2):
        for chip in range(-(-part // DOWN_ROWS)):
            first = chip * DOWN_ROWS
            rows = min(DOWN_ROWS, part - first)
            z, y = chip // 4, chip % 4
            place = pl.ds(core * part + first, rows)
            out_ref[place, :DOWN_CUT] = low_ref[core, z, y, :rows].astype(jnp.float32)
            out_ref[place, DOWN_CUT:] = high_ref[core, y, z, :rows].astype(jnp.float32)


def widen_down(low, high, part):
    vmem = pl.BlockSpec(memory_space=pltpu.VMEM)
    return pl.pallas_call(
        widen_down_kernel,
        out_shape=jax.ShapeDtypeStruct((2 * part, D), jnp.float32),
        in_specs=[vmem, vmem],
        out_specs=vmem,
        compiler_params=pltpu.CompilerParams(vmem_limit_bytes=32 * 1024 * 1024),
        name="widen_down",
    )(low, high)


def split_sums_kernel(rows, top_ref, end_ref, qkv_ref, out_ref, vectors_ref):
    first = qkv_ref.shape[1] // 128
    for chip in range(16):
        target = qkv_ref if chip < first else out_ref
        place = (chip if chip < first else chip - first) * 128
        for core in range(2):
            z, y = chip // 4, chip % 4
            top = top_ref[core, z, y].astype(jnp.float32)
            end = end_ref[core, y, z].astype(jnp.float32)
            start, cut = core * rows, top.shape[0]
            target[start : start + cut, place : place + 128] = top
            target[start + cut : start + rows, place : place + 128] = end[: rows - cut]
        vectors_ref[:, chip * 128 : (chip + 1) * 128] = end[rows - cut : rows - cut + 8]


def split_sums(top, end, rows, columns):
    chips = 16
    vmem = pl.BlockSpec(memory_space=pltpu.VMEM)
    shapes = ((2 * rows, columns), (2 * rows, chips * 128 - columns), (8, chips * 128))
    return pl.pallas_call(
        functools.partial(split_sums_kernel, rows),
        out_shape=tuple(jax.ShapeDtypeStruct(shape, jnp.float32) for shape in shapes),
        in_specs=[vmem, vmem],
        out_specs=(vmem,) * 3,
        name="split_sums",
    )(top, end)


def rms_apply(values, gain):
    mean_square = jnp.mean(values * values, axis=-1, keepdims=True)
    return values * lax.rsqrt(mean_square + norm_eps) * gain


def half_turn(values):
    middle = values.shape[-1] // 2
    return jnp.concatenate([-values[..., middle:], values[..., :middle]], axis=-1)


def rotate(values, cosine, sine):
    return values * cosine + half_turn(values) * sine


def rope_tables(positions, head_dim):
    middle = head_dim // 2
    inverse = rope_base ** (-(jnp.arange(middle).astype(jnp.float32) * 2.0) / head_dim)
    angles = positions.astype(jnp.float32)[:, None] * inverse[None, :]
    angles = jnp.concatenate([angles, angles], axis=-1)
    return (jnp.cos(angles), jnp.sin(angles))


def swiglu(gate_in, up_in):
    return jax.nn.silu(gate_in) * up_in


def dot(a, b, ca=1, cb=0):
    return lax.dot_general(a, b, (((ca,), (cb,)), ((), ())), preferred_element_type=jnp.float32)


def causal_copy(order_ref, k_ref, v_ref, sorted_ref):
    def move(slot, unused):
        half, core, y, z = slot % 2, slot // 2 % 2, slot // 4 % 4, slot // 16
        k_place = pl.multiple_of((((core * 4 + z) * 4 + y) * 2 + half) * SPAN, SPAN)
        v_place = pl.multiple_of((((core * 4 + y) * 4 + z) * 2 + half) * SPAN, SPAN)
        target = pl.ds(pl.multiple_of(order_ref[slot] * SPAN, SPAN), SPAN)
        sorted_ref[target, :128] = k_ref[pl.ds(k_place, SPAN), :]
        sorted_ref[target, 128:] = v_ref[pl.ds(v_place, SPAN), :]
        return unused

    lax.fori_loop(0, k_ref.shape[0] // SPAN, move, 0)


def visible(start, place, rows):
    key_place = lax.broadcasted_iota(jnp.int32, (CHUNK, rows), 0) + start
    lane = lax.broadcasted_iota(jnp.int32, (CHUNK, rows), 1)
    return key_place <= place * SPAN + lane % SPAN


def head_tile(heads, half, group):
    lanes = slice(half * SPAN, (half + 1) * SPAN)
    first = group * GROUP
    return jnp.concatenate([heads[first + item][:, lanes] for item in range(GROUP)], axis=1)


def padded(tile, group):
    empty = jnp.zeros_like(tile)
    return jnp.concatenate([tile, empty] if group == 0 else [empty, tile], axis=0)


def token_rows(tiles):
    blocks = []
    for tile in tiles:
        turned = tile.T
        blocks += [turned[item * SPAN : (item + 1) * SPAN] for item in range(GROUP)]
    pairs = [
        jnp.concatenate([blocks[2 * item], blocks[2 * item + 1]], axis=1) for item in range(GROUP)
    ]
    return jnp.concatenate(pairs, axis=1)


def prepare_kernel(
    x_ref,
    gain_ref,
    weight_ref,
    bias_ref,
    cos_ref,
    sin_ref,
    normed_ref,
    q_ref,
    q_rows_ref,
    k_ref,
    v_ref,
):
    wide = x_ref[...].astype(jnp.float32)
    scale = lax.rsqrt(jnp.mean(wide * wide, axis=-1, keepdims=True) + norm_eps)
    normed = (wide * scale * gain_ref[...]).astype(jnp.bfloat16)
    normed_ref[...] = normed
    mixed = dot(normed, weight_ref[...]) + bias_ref[...]
    count = QH + KVH
    v_ref[...] = mixed[:, count * HD :].astype(jnp.bfloat16)
    turned = mixed[:, : count * HD].T
    cosine, sine = cos_ref[...], sin_ref[...]
    heads = []
    for head in range(count):
        first = turned[head * HD : head * HD + HD // 2]
        second = turned[head * HD + HD // 2 : (head + 1) * HD]
        rotated = [first * cosine - second * sine, second * cosine + first * sine]
        heads.append(jnp.concatenate(rotated, axis=0))
    k_ref[...] = jnp.concatenate(heads[QH:], axis=0).T.astype(jnp.bfloat16)
    for half in range(2):
        for group in range(KVH):
            tile = padded(head_tile(heads, half, group) * HD**-0.5, group)
            q_ref[half, group] = tile.astype(jnp.bfloat16)
            q_rows_ref[half, group] = tile.T.astype(jnp.bfloat16)


def prepare(inputs, gain, weight, bias, cosine, sine):
    tokens = inputs.shape[0]
    rows = GROUP * SPAN
    vmem = pl.BlockSpec(memory_space=pltpu.VMEM)
    low = functools.partial(jax.ShapeDtypeStruct, dtype=jnp.bfloat16)
    return pl.pallas_call(
        prepare_kernel,
        out_shape=(
            low((tokens, D)),
            low((2, KVH, 128, rows)),
            low((2, KVH, rows, 128)),
            low((tokens, KVH * HD)),
            low((tokens, KVH * HD)),
        ),
        in_specs=[vmem] * 6,
        out_specs=(vmem,) * 5,
        compiler_params=pltpu.CompilerParams(vmem_limit_bytes=32 * 1024 * 1024),
        cost_estimate=pl.CostEstimate(flops=0, bytes_accessed=1_000_000, transcendentals=0),
        name="prepare",
    )(inputs, gain, weight, bias, cosine, sine)


def attend_kernel(
    order_ref,
    mine_ref,
    k_ref,
    v_ref,
    q_ref,
    x_ref,
    weight_ref,
    gain_ref,
    out_ref,
    lse_ref,
    attended_ref,
    residual_ref,
    normed_ref,
    sorted_ref,
):
    causal_copy(order_ref, k_ref, v_ref, sorted_ref)
    rows = q_ref.shape[-1]
    for half in range(2):
        place = mine_ref[half]
        last = place * SPAN // CHUNK

        def step(index, carry, masked, half=half, place=place):
            start = pl.multiple_of(index * CHUNK, CHUNK)
            keys = sorted_ref[pl.ds(start, CHUNK), :128]
            values = sorted_ref[pl.ds(start, CHUNK), 128:]
            result = []
            for head in range(KVH):
                top, total, mixed = carry[head]
                scores = dot(keys, q_ref[half, head])
                if masked:
                    scores = jnp.where(visible(start, place, rows), scores, masked_score)
                new_top = jnp.maximum(top, jnp.max(scores, axis=0, keepdims=True))
                shrink = jnp.exp(top - new_top)
                weights = jnp.exp(scores - new_top)
                total = total * shrink + jnp.sum(weights, axis=0, keepdims=True)
                mixed = mixed * shrink + dot(values, weights.astype(jnp.bfloat16), 0, 0)
                result.append((new_top, total, mixed))
            return tuple(result)

        empty = tuple(
            (
                jnp.full((1, rows), masked_score, jnp.float32),
                jnp.zeros((1, rows), jnp.float32),
                jnp.zeros((128, rows), jnp.float32),
            )
            for head in range(KVH)
        )
        carry = lax.fori_loop(0, last, functools.partial(step, masked=False), empty)
        carry = step(last, carry, True)
        tiles = []
        for head in range(KVH):
            top, total, mixed = carry[head]
            tiles.append(mixed[head * HD : (head + 1) * HD] / total)
            out_ref[half, head] = tiles[head]
            lse_ref[half, head] = top + jnp.log(total)
        place = pl.ds(half * SPAN, SPAN)
        attended_ref[place, :] = token_rows(tiles).astype(jnp.bfloat16)
    residual = x_ref[...].astype(jnp.float32) + dot(attended_ref[...], weight_ref[...])
    residual_ref[...] = residual
    scale = lax.rsqrt(jnp.mean(residual * residual, axis=-1, keepdims=True) + norm_eps)
    normed_ref[...] = (residual * scale * gain_ref[...]).astype(jnp.bfloat16)


def attend(order, mine, k_all, v_all, q_pad, inputs, weight, gain):
    halves, heads, unused, rows = q_pad.shape
    smem = pl.BlockSpec(memory_space=pltpu.SMEM)
    vmem = pl.BlockSpec(memory_space=pltpu.VMEM)
    return pl.pallas_call(
        attend_kernel,
        out_shape=(
            jax.ShapeDtypeStruct((halves, heads, HD, rows), jnp.float32),
            jax.ShapeDtypeStruct((halves, heads, 1, rows), jnp.float32),
            jax.ShapeDtypeStruct(inputs.shape, jnp.bfloat16),
            jax.ShapeDtypeStruct(inputs.shape, jnp.float32),
            jax.ShapeDtypeStruct(inputs.shape, jnp.bfloat16),
        ),
        in_specs=[smem, smem] + [vmem] * 6,
        out_specs=(vmem,) * 5,
        scratch_shapes=[pltpu.VMEM((k_all.shape[0], 256), k_all.dtype)],
        compiler_params=pltpu.CompilerParams(vmem_limit_bytes=48 * 1024 * 1024),
        cost_estimate=pl.CostEstimate(
            flops=0, bytes_accessed=1_000_000, transcendentals=0
        ),
        name="attend",
    )(order, mine, k_all, v_all, q_pad, inputs, weight, gain)


def attend_back_kernel(
    order_ref,
    mine_ref,
    k_ref,
    v_ref,
    q_ref,
    q_rows_ref,
    out_ref,
    lse_ref,
    d_normed_ref,
    residual_ref,
    cot_ref,
    gain_ref,
    weight_ref,
    cos_ref,
    sin_ref,
    dq_ref,
    dk_ref,
    dv_ref,
    d_residual_ref,
    d_branch_ref,
    gain_grad_ref,
    sorted_ref,
    sum_ref,
    do_ref,
    do_rows_ref,
    delta_ref,
):
    residual, d_normed = residual_ref[...], d_normed_ref[...]
    scale = lax.rsqrt(jnp.mean(residual * residual, axis=-1, keepdims=True) + norm_eps)
    unit = residual * scale
    gain_grad_ref[...] = jnp.sum(d_normed * unit, axis=0, keepdims=True)
    weighted = d_normed * gain_ref[...]
    inner = jnp.mean(weighted * unit, axis=-1, keepdims=True)
    d_residual = cot_ref[...].astype(jnp.float32) + scale * (weighted - unit * inner)
    d_residual_ref[...] = d_residual
    d_branch = d_residual.astype(jnp.bfloat16)
    d_branch_ref[...] = d_branch
    d_attended = dot(d_branch, weight_ref[...], 1, 1).astype(jnp.bfloat16).astype(jnp.float32)
    turned = d_attended.T
    heads = [turned[head * HD : (head + 1) * HD] for head in range(QH)]
    for half in range(2):
        for group in range(KVH):
            tile = head_tile(heads, half, group)
            product = tile * out_ref[half, group]
            delta_ref[half, group] = jnp.sum(product, axis=0, keepdims=True)
            tile = padded(tile, group)
            do_ref[half, group] = tile.astype(jnp.bfloat16)
            do_rows_ref[half, group] = tile.T.astype(jnp.bfloat16)
    causal_copy(order_ref, k_ref, v_ref, sorted_ref)
    sum_ref[...] = jnp.zeros_like(sum_ref)
    rows = q_ref.shape[-1]
    for half in range(2):
        place = mine_ref[half]
        last = place * SPAN // CHUNK

        def step(index, carry, masked, half=half, place=place):
            start = pl.multiple_of(index * CHUNK, CHUNK)
            keys = sorted_ref[pl.ds(start, CHUNK), :128]
            values = sorted_ref[pl.ds(start, CHUNK), 128:]
            d_keys = sum_ref[pl.ds(start, CHUNK), :128]
            d_values = sum_ref[pl.ds(start, CHUNK), 128:]
            result = []
            for head in range(KVH):
                scores = dot(keys, q_ref[half, head])
                probs = jnp.exp(scores - lse_ref[half, head])
                if masked:
                    probs = jnp.where(visible(start, place, rows), probs, 0.0)
                d_probs = dot(values, do_ref[half, head])
                d_scores = (probs * (d_probs - delta_ref[half, head])).astype(jnp.bfloat16)
                d_values += dot(probs.astype(jnp.bfloat16), do_rows_ref[half, head])
                d_keys += dot(d_scores, q_rows_ref[half, head])
                result.append(carry[head] + dot(keys, d_scores, 0, 0))
            sum_ref[pl.ds(start, CHUNK), :128] = d_keys
            sum_ref[pl.ds(start, CHUNK), 128:] = d_values
            return tuple(result)

        empty = tuple(jnp.zeros((128, rows), jnp.float32) for head in range(KVH))
        carry = lax.fori_loop(0, last, functools.partial(step, masked=False), empty)
        carry = step(last, carry, True)
        lanes = slice(half * SPAN, (half + 1) * SPAN)
        cosine = jnp.concatenate([cos_ref[:, lanes]] * GROUP, axis=1)
        sine = jnp.concatenate([sin_ref[:, lanes]] * GROUP, axis=1)
        tiles = []
        for head in range(KVH):
            middle = head * HD + HD // 2
            first = carry[head][head * HD : middle] * (HD**-0.5)
            second = carry[head][middle : (head + 1) * HD] * (HD**-0.5)
            turned = [first * cosine + second * sine, second * cosine - first * sine]
            tiles.append(jnp.concatenate(turned, axis=0))
        dq_ref[pl.ds(half * SPAN, SPAN), :] = token_rows(tiles).astype(jnp.bfloat16)

    def move(slot, unused):
        rest, y, z = slot % 4, slot // 4 % 4, slot // 16
        k_place = pl.multiple_of(slot * SPAN, SPAN)
        v_place = pl.multiple_of(((y * 4 + z) * 4 + rest) * SPAN, SPAN)
        source = pl.ds(pl.multiple_of(order_ref[slot] * SPAN, SPAN), SPAN)
        dk_ref[pl.ds(k_place, SPAN), :] = sum_ref[source, :128].astype(jnp.bfloat16)
        dv_ref[pl.ds(v_place, SPAN), :] = sum_ref[source, 128:].astype(jnp.bfloat16)
        return unused

    lax.fori_loop(0, dk_ref.shape[0] // SPAN, move, 0)


def attend_back(order, mine, k_all, v_all, q_pad, *rest):
    halves, heads, unused, rows = q_pad.shape
    tokens = 2 * SPAN
    smem = pl.BlockSpec(memory_space=pltpu.SMEM)
    vmem = pl.BlockSpec(memory_space=pltpu.VMEM)
    return pl.pallas_call(
        attend_back_kernel,
        out_shape=(
            jax.ShapeDtypeStruct((tokens, D), jnp.bfloat16),
            jax.ShapeDtypeStruct(k_all.shape, jnp.bfloat16),
            jax.ShapeDtypeStruct(v_all.shape, jnp.bfloat16),
            jax.ShapeDtypeStruct((tokens, D), jnp.float32),
            jax.ShapeDtypeStruct((tokens, D), jnp.bfloat16),
            jax.ShapeDtypeStruct((1, D), jnp.float32),
        ),
        in_specs=[smem, smem] + [vmem] * (3 + len(rest)),
        out_specs=(vmem,) * 6,
        scratch_shapes=[
            pltpu.VMEM((k_all.shape[0], 256), k_all.dtype),
            pltpu.VMEM((k_all.shape[0], 256), jnp.float32),
            pltpu.VMEM((halves, heads, 128, rows), jnp.bfloat16),
            pltpu.VMEM((halves, heads, rows, 128), jnp.bfloat16),
            pltpu.VMEM((halves, heads, 1, rows), jnp.float32),
        ],
        compiler_params=pltpu.CompilerParams(vmem_limit_bytes=48 * 1024 * 1024),
        cost_estimate=pl.CostEstimate(flops=0, bytes_accessed=1_000_000, transcendentals=0),
        name="attend_back",
    )(order, mine, k_all, v_all, q_pad, *rest)


def body(
    inputs,
    cotangent,
    span_order,
    positions,
    attn_gain,
    qkv_weight,
    qkv_bias,
    out_weight,
    mlp_gain,
    gate_weight,
    up_weight,
    down_weight,
):
    token_count = inputs.shape[0]
    q_cols = QH * HD
    k_cols = KVH * HD
    slices = lax.axis_size("dp")
    own_rows = D // slices
    part = FF // (slices * 2)
    dp = lax.axis_index("dp")
    core = lax.axis_index("core")
    slot = (lax.axis_index("z") * lax.axis_size("y") + lax.axis_index("y")) * 2 + core

    small = jnp.concatenate([attn_gain, mlp_gain, qkv_bias])
    small = jnp.pad(small, (0, 2048 - small.shape[0])).reshape(16, 128)
    qkv_half = lax.dynamic_slice_in_dim(qkv_weight, core * (own_rows // 2), own_rows // 2)
    qkv_full, small = communicate(
        "qkv_in", 0, (RingGather, ROW, qkv_half), (RingGather, ROW, small)
    )
    qkv_full, out_weight = lax.optimization_barrier((qkv_full.reshape(D, -1), out_weight))
    small = small[:, 0].reshape(slices, -1)
    gain_one_wide = small[:, :own_rows].reshape(D).astype(jnp.float32)
    gain_two_wide = small[:, own_rows : 2 * own_rows].reshape(D).astype(jnp.float32)
    bias_full = small[:, 2 * own_rows : 2 * own_rows + qkv_bias.shape[0]]
    bias_full = bias_full.reshape(-1).astype(jnp.float32)
    out_full = lax.all_gather(out_weight, "dp", axis=0, tiled=True)

    def column_blocks(weight):
        parts = [weight[:, part * index : part * (index + 1)] for index in range(2 * slices)]
        return [jnp.where(core == 0, parts[2 * p], parts[2 * p + 1]) for p in range(slices)]

    gate_blocks, up_blocks = column_blocks(gate_weight), column_blocks(up_weight)
    gate_up = jnp.stack(
        [jnp.concatenate([gate_blocks[p], up_blocks[p]], axis=0) for p in range(slices)]
    )
    gate_up = lax.all_to_all(gate_up, "dp", 0, 0, tiled=True)
    gate_part = gate_up[:, :own_rows].reshape(D, part)
    up_part = gate_up[:, own_rows:].reshape(D, part)
    down_part = lax.dynamic_slice_in_dim(down_weight, core * part, part, axis=0)
    cot_all = lax.all_gather(cotangent, ("dp", "core"), axis=0, tiled=True)

    inputs_wide = inputs.astype(jnp.float32)
    cosine, sine = rope_tables(positions, HD)
    cos_turned, sin_turned = cosine[:, : HD // 2].T, sine[:, : HD // 2].T
    cosine = cosine[:, None, :]
    sine = sine[:, None, :]
    normed_one, q_pad, q_rows, key_rot, value_low = prepare(
        inputs, gain_one_wide[None], qkv_full, bias_full[None], cos_turned, sin_turned
    )
    normed_one_all = lax.all_gather(normed_one, ("dp", "core"), axis=0, tiled=True)
    k_all, v_all = communicate(
        "kv_in", 1, (PlaneGather, PLANE, key_rot), (PlaneGather, ENALP, value_low)
    )
    k_all = k_all.reshape(-1, k_cols)
    v_all = v_all.reshape(-1, k_cols)
    mine = lax.dynamic_slice_in_dim(span_order, 2 * slot, 2)
    attended_cols, lse, attended_low, residual, normed_two = attend(
        span_order, mine, k_all, v_all, q_pad, inputs, out_full, gain_two_wide[None]
    )
    attended_all = lax.all_gather(attended_low, ("dp", "core"), axis=0, tiled=True)
    (normed_all,) = communicate("normed_in", 2, (RingGather, ROW, normed_two))
    normed_all = normed_all.reshape(-1, D)
    gate_proj = dot(normed_all, gate_part)
    up_proj = dot(normed_all, up_part)
    hidden_low = swiglu(gate_proj, up_proj).astype(jnp.bfloat16)
    out_sum = dot(hidden_low, down_part).astype(jnp.bfloat16)
    d_hidden = dot(cot_all, down_part, 1, 1)
    d_gate, d_up = jax.vjp(swiglu, gate_proj, up_proj)[1](d_hidden)
    d_gate = d_gate.astype(jnp.bfloat16)
    d_up = d_up.astype(jnp.bfloat16)
    d_norm_sum = (dot(d_gate, gate_part, 1, 1) + dot(d_up, up_part, 1, 1)).astype(jnp.bfloat16)
    blocks = (slices, 2, token_count, D)
    d_norm_sum, normed_one_all = lax.optimization_barrier((d_norm_sum, normed_one_all))
    low = functools.partial(jax.ShapeDtypeStruct, dtype=jnp.bfloat16)
    columns = low((4, 4, slices, ROWS, part))
    d_normed_two, out_rows, gate_grad, up_grad, down_low, down_high = communicate(
        "d_normed_out",
        3,
        (RingScatter, ROW, d_norm_sum.reshape(blocks)),
        (RingScatter, ROW, out_sum.reshape(blocks)),
        compute=((gate_grads, 1), (up_grads, 1), (down_grads, 2)),
        inputs=(normed_all, cot_all, hidden_low, d_gate, d_up),
        after=(
            (AxisScatter, ("z",), columns),
            (AxisScatter, ("y",), columns),
            (AxisScatter, ("z",), low((4, 4, DOWN_ROWS, DOWN_CUT))),
            (AxisScatter, ("y",), low((4, 4, DOWN_ROWS, D - DOWN_CUT))),
        ),
    )
    output = (residual + out_rows).astype(jnp.bfloat16)

    d_normed_two, attended_all = lax.optimization_barrier((d_normed_two, attended_all))
    d_query_low, d_k_all, d_v_all, d_residual, d_branch, gain_two_grad = attend_back(
        span_order,
        mine,
        k_all,
        v_all,
        q_pad,
        q_rows,
        attended_cols,
        lse,
        d_normed_two,
        residual,
        cotangent,
        gain_two_wide[None],
        out_full,
        cos_turned,
        sin_turned,
    )

    def turn_back(grads):
        scaled = grads * sine
        middle = HD // 2
        back = jnp.concatenate([scaled[..., middle:], -scaled[..., :middle]], axis=-1)
        return grads * cosine + back

    paired = functools.partial(PlaneScatter, pair=True)
    pairs = (4, 4, 2, token_count, k_cols)
    d_k, d_v, d_query_all, d_branch_all, gate_grad, up_grad, down_low, down_high = communicate(
        "d_kv_out",
        4,
        (paired, PLANE, d_k_all.reshape(pairs)),
        (paired, ENALP, d_v_all.reshape(pairs)),
        (RingGather, ROW, d_query_low),
        (RingGather, ROW, d_branch),
        (Deal, ("y",), gate_grad),
        (Deal, ("z",), up_grad),
        (AxisScatter, ("y",), down_low),
        (AxisScatter, ("z",), down_high),
    )
    d_key_raw = turn_back(d_k.reshape(token_count, KVH, HD))
    d_kv_low = jnp.concatenate(
        [d_key_raw.reshape(token_count, k_cols), d_v], axis=1
    ).astype(jnp.bfloat16)
    d_mixed = jnp.concatenate([d_query_low, d_kv_low], axis=1)
    d_normed_one = dot(d_mixed, qkv_full, 1, 1)
    d_input_part, gain_one_grad = jax.vjp(rms_apply, inputs_wide, gain_one_wide)[1](d_normed_one)
    input_grad = (d_input_part + d_residual).astype(jnp.bfloat16)
    gain_grads = jnp.concatenate([gain_one_grad, gain_two_grad[0]])
    gain_grads = jnp.pad(gain_grads, (0, 2048 - 2 * D)).reshape(16, 128)
    d_kv_rows, gain_grads, gate_grad, up_grad, down_low, down_high = communicate(
        "d_kv_in",
        5,
        (RingGather, ROW, d_kv_low),
        (RingGather, ROW, gain_grads),
        (AxisGather, ("y",), gate_grad),
        (AxisGather, ("z",), up_grad),
        (PlaneGather, PLANE, down_low),
        (PlaneGather, ENALP, down_high),
    )
    d_mixed_all = jnp.concatenate(
        [d_query_all.reshape(-1, q_cols), d_kv_rows.reshape(-1, 2 * k_cols)], axis=1
    )
    gain_grads = jnp.sum(gain_grads.reshape(2 * slices, -1), axis=0)
    bias_grad = jnp.sum(d_mixed_all.astype(jnp.float32), axis=0)

    half_rows = own_rows // 2
    first = dp * own_rows + core * half_rows

    def my_columns(tokens):
        return lax.dynamic_slice_in_dim(tokens, first, half_rows, axis=1)

    out_grad = dot(my_columns(attended_all), d_branch_all.reshape(-1, D), 0, 0)
    qkv_grad = dot(my_columns(normed_one_all), d_mixed_all, 0, 0)
    chips = 16
    width = chips * 128
    sums = jnp.concatenate(
        [
            jnp.concatenate([qkv_grad, out_grad], axis=1),
            jnp.pad(bias_grad, (0, width - bias_grad.shape[0]))[None],
            jnp.pad(gain_grads, (0, width - gain_grads.shape[0]))[None],
            jnp.zeros((14, width), jnp.float32),
        ],
        axis=0,
    ).astype(jnp.bfloat16)
    sums = sums.reshape(128, 4, 4, 128).transpose(1, 2, 0, 3)
    shared = functools.partial(AxisGather, share=True)
    sums_top, sums_end, gate_grad, up_grad = communicate(
        "grads",
        6,
        (PlaneTotal, PLANE, sums[:, :, :64]),
        (PlaneTotal, ENALP, sums[:, :, 64:].transpose(1, 0, 2, 3)),
        (shared, ("z",), gate_grad),
        (shared, ("y",), up_grad),
    )
    qkv_grad, out_grad, vectors = split_sums(
        sums_top, sums_end, half_rows, q_cols + 2 * k_cols
    )
    bias_grad, gain_grads = vectors[0], vectors[1]

    def owned(vector, start, count):
        width = count // slices
        return lax.dynamic_slice_in_dim(vector, start + dp * width, width)

    gate_grad, up_grad = widen(gate_grad, up_grad)
    down_grad = widen_down(down_low, down_high, part)
    return (
        output,
        input_grad,
        owned(gain_grads, 0, D),
        qkv_grad,
        owned(bias_grad, 0, q_cols + k_cols),
        owned(bias_grad, q_cols + k_cols, k_cols),
        out_grad,
        owned(gain_grads, D, D),
        gate_grad,
        up_grad,
        down_grad,
    )


def solution(mesh):
    grid = Mesh(mesh.devices.reshape(4, 4, 4, 2), ("dp", "z", "y", "core"))
    tokens = ("dp",) + CTX
    return jax.shard_map(
        body,
        mesh=grid,
        in_specs=(
            P(tokens, None),
            P(tokens, None),
            P(),
            P(tokens),
            P("dp"),
            P("dp", None),
            P("dp"),
            P("dp", None),
            P("dp"),
            P("dp", None),
            P("dp", None),
            P("dp", None),
        ),
        out_specs=(
            P(tokens, None),
            P(tokens, None),
            P("dp"),
            P("dp", None),
            P("dp"),
            P("dp"),
            P("dp", None),
            P("dp"),
            P("dp", None),
            P("dp", None),
            P("dp", None),
        ),
        check_vma=False,
    )
```

```python
import functools

import jax
import jax.numpy as jnp
from jax import lax
from jax.experimental import pallas as pl
from jax.experimental.pallas import tpu as pltpu
from jax.sharding import Mesh, PartitionSpec as P

QH = 14
KVH = 2
HD = 64
GROUP = QH // KVH
D = 896
FF = 4864
SPAN = 64
CHUNK = 512

norm_eps = 1e-06
rope_base = 1000000.0
masked_score = -1e30
CTX = ("z", "y", "core")
ROW = ("dp",)
PLANE = ("z", "y")
ENALP = ("y", "z")

MESH = pl.DeviceIdType.MESH
SIZES = {"dp": 4, "z": 4, "y": 4}


def group_size(axes):
    size = 1
    for axis in axes:
        size *= SIZES[axis]
    return size


def group_index(axes):
    index = 0
    for axis in axes:
        index = index * SIZES[axis] + lax.axis_index(axis)
    return index


def member(axes, index):
    found = {}
    for axis in reversed(axes):
        found[axis] = index % SIZES[axis]
        index = index // SIZES[axis]
    return found


def remote(source, target, send, receive, device):
    return pltpu.make_async_remote_copy(
        src_ref=source,
        dst_ref=target,
        send_sem=send,
        recv_sem=receive,
        device_id=device,
        device_id_type=MESH,
    )


class Exchange:
    def __init__(self, axes, array):
        self.axes, self.n = axes, group_size(axes)
        self.in_space = pltpu.VMEM
        self.out = jax.ShapeDtypeStruct(array.shape, array.dtype)
        self.out_space = pl.ANY
        self.scratch = [pltpu.SemaphoreType.DMA] + [pltpu.SemaphoreType.DMA((self.n,))] * 2

    def bind(self, source, target, scratch):
        self.x, self.o = source, target
        self.local, self.send, self.receive = scratch
        self.me = group_index(self.axes)
        self.stages = [self.start, self.end]

    def mine(self):
        return pltpu.make_async_copy(self.x.at[self.me], self.o.at[self.me], self.local)

    def outward(self, k, slot):
        to = (self.me + k) % self.n
        device = member(self.axes, to)
        send, receive = self.send.at[k], self.receive.at[k]
        return remote(self.x.at[to], self.o.at[slot], send, receive, device)

    def start(self):
        self.mine().start()
        for k in range(1, self.n):
            self.outward(k, self.me).start()

    def end(self):
        self.mine().wait()
        for k in range(1, self.n):
            self.outward(k, self.me).wait_send()
            self.outward(k, (self.me + self.n - k) % self.n).wait_recv()


class PlaneGather:
    def __init__(self, axes, array):
        self.axes = axes
        self.in_space = pltpu.VMEM
        self.out = jax.ShapeDtypeStruct((2, 4, 4) + array.shape, array.dtype)
        self.out_space = pl.ANY
        self.scratch = [pltpu.SemaphoreType.DMA] + [pltpu.SemaphoreType.DMA((4,))] * 6

    def bind(self, source, target, scratch):
        self.x, self.o, self.local = source, target, scratch[0]
        self.s_one, self.r_one, self.s_two, self.r_two, self.s_core, self.r_core = scratch[1:]
        self.one, self.two = (lax.axis_index(axis) for axis in self.axes)
        self.core = lax.axis_index("core")
        self.stages = [self.start, self.middle, self.late, self.end]

    def mine(self):
        place = self.o.at[self.core, self.one, self.two]
        return pltpu.make_async_copy(self.x, place, self.local)

    def first(self, k, slot):
        device = {self.axes[1]: (self.two + k) % 4}
        place = self.o.at[self.core, self.one, slot]
        return remote(self.x, place, self.s_one.at[k], self.r_one.at[k], device)

    def second(self, k, row):
        device = {self.axes[0]: (self.one + k) % 4}
        place = self.o.at[self.core, row]
        return remote(place, place, self.s_two.at[k], self.r_two.at[k], device)

    def across(self, k, core):
        place = self.o.at[core, (self.one + 4 - k) % 4]
        device = {"core": 1 - self.core}
        return remote(place, place, self.s_core.at[k], self.r_core.at[k], device)

    def start(self):
        for k in (2, 1, 3):
            self.first(k, self.two).start()
        self.mine().start()

    def middle(self):
        self.mine().wait()
        for k in range(1, 4):
            self.first(k, (self.two + 4 - k) % 4).wait_recv()
        for k in (2, 1, 3):
            self.second(k, self.one).start()
        self.across(0, self.core).start()

    def late(self):
        for k in (1, 3, 2):
            self.second(k, (self.one + 4 - k) % 4).wait_recv()
            self.across(k, self.core).start()

    def end(self):
        for k in range(4):
            if k:
                self.first(k, self.two).wait_send()
                self.second(k, self.one).wait_send()
            self.across(k, self.core).wait_send()
            self.across(k, 1 - self.core).wait_recv()


class PlaneScatter:
    def __init__(self, axes, array, pair=False, kind=jnp.float32):
        self.axes, self.pair = axes, pair
        self.block = array.shape[3 if pair else 2 :]
        self.in_space = pltpu.VMEM
        self.out = jax.ShapeDtypeStruct(self.block, kind)
        self.out_space = pltpu.VMEM
        self.kind = array.dtype
        row = (4,) + self.block
        self.scratch = [
            pltpu.VMEM((4,) + row, self.kind),
            pltpu.VMEM(row, jnp.float32),
            pltpu.VMEM(row, self.kind),
            pltpu.VMEM(row, self.kind),
        ]
        if pair:
            self.scratch += [pltpu.VMEM((4,) + row, self.kind)] * 2
            self.scratch += [pltpu.SemaphoreType.DMA((4,))] * 2
        self.scratch += [pltpu.SemaphoreType.DMA((4,))] * 4

    def bind(self, source, target, scratch):
        self.x, self.o = source, target
        self.land, self.total, self.low, self.last = scratch[:4]
        if self.pair:
            self.half, self.summed, self.s_core, self.r_core = scratch[4:8]
        self.s_one, self.r_one, self.s_two, self.r_two = scratch[-4:]
        self.one, self.two = (lax.axis_index(axis) for axis in self.axes)
        self.core = lax.axis_index("core")
        self.stages = [self.start, self.middle, self.late, self.end]

    def across(self, k):
        to = (self.one + k) % 4
        source = self.x.at[to, :, 1 - self.core]
        device = {"core": 1 - self.core}
        return remote(source, self.half.at[to], self.s_core.at[k], self.r_core.at[k], device)

    def first(self, k, slot):
        to = (self.one + k) % 4
        source = self.summed if self.pair else self.x
        send, receive = self.s_one.at[k], self.r_one.at[k]
        return remote(source.at[to], self.land.at[slot], send, receive, {self.axes[0]: to})

    def second(self, k, slot):
        to = (self.two + k) % 4
        send, receive = self.s_two.at[k], self.r_two.at[k]
        return remote(self.low.at[to], self.last.at[slot], send, receive, {self.axes[1]: to})

    def start(self):
        for k in (2, 1, 3):
            if self.pair:
                self.across(k).start()
            else:
                self.first(k, self.one).start()
        if self.pair:
            self.across(0).start()

    def middle(self):
        if self.pair:
            for k in (2, 1, 3, 0):
                to = (self.one + k) % 4
                self.across(k).wait_recv()
                for item in range(4):
                    both = self.x[to, item, self.core].astype(jnp.float32)
                    both += self.half[to, item].astype(jnp.float32)
                    if k:
                        self.summed[to, item] = both.astype(self.kind)
                    else:
                        self.total[item] = both
                if k:
                    self.first(k, self.one).start()

    def late(self):
        slots = [(self.one + 4 - k) % 4 for k in range(4)]
        for k in range(1, 4):
            self.first(k, slots[k]).wait_recv()
        for item in range(4):
            if self.pair:
                total = self.total[item]
            else:
                total = self.x[self.one, item].astype(jnp.float32)
            for k in range(1, 4):
                total += self.land[slots[k], item].astype(jnp.float32)
            self.total[item] = total
            self.low[item] = total.astype(self.kind)
        for k in (2, 1, 3):
            self.second(k, self.two).start()

    def end(self):
        total = self.total[self.two]
        for k in range(1, 4):
            slot = (self.two + 4 - k) % 4
            self.second(k, slot).wait_recv()
            total += self.last[slot].astype(jnp.float32)
        self.o[...] = total.astype(self.o.dtype)
        for k in range(4):
            if k:
                self.first(k, self.one).wait_send()
                self.second(k, self.two).wait_send()
            if self.pair:
                self.across(k).wait_send()


class PlaneTotal:
    def __init__(self, axes, array):
        self.axes = axes
        self.scatter = PlaneScatter(axes, array, kind=array.dtype)
        self.gather = PlaneGather(axes, self.scatter.out)
        self.in_space = pltpu.VMEM
        self.out, self.out_space = self.gather.out, pl.ANY
        own = pltpu.VMEM(self.scatter.block, array.dtype)
        self.scratch = [own] + self.scatter.scratch + self.gather.scratch

    def bind(self, source, target, scratch):
        count = 1 + len(self.scatter.scratch)
        self.scatter.bind(source, scratch[0], scratch[1:count])
        self.gather.bind(scratch[0], target, scratch[count:])
        self.stages = self.scatter.stages + self.gather.stages


def split_point(rows):
    return rows if rows < 32 else (rows // 2 + 15) // 16 * 16


class RingGather:
    def __init__(self, axes, array):
        self.axes, self.n = axes, group_size(axes)
        self.block, self.dtype = array.shape, array.dtype
        self.cut = split_point(self.block[0])
        self.in_space = pltpu.VMEM
        self.out = jax.ShapeDtypeStruct((self.n, 2) + self.block, self.dtype)
        self.out_space = pl.ANY
        self.scratch = [pltpu.SemaphoreType.DMA] + [pltpu.SemaphoreType.DMA((4,))] * 4

    def bind(self, source, target, scratch):
        self.x, self.o = source, target
        self.local, self.send, self.receive, self.f_send, self.f_receive = scratch
        self.me, self.core = group_index(self.axes), lax.axis_index("core")
        self.stages = [self.start, self.middle, self.late, self.end]

    def at(self, shift, core):
        return self.o.at[(self.me + shift) % 4, core]

    def mine(self):
        return pltpu.make_async_copy(self.x, self.at(0, self.core), self.local)

    def copy(self, step, to, source, target):
        device = member(self.axes, (self.me + to) % 4)
        return remote(source, target, self.send.at[step], self.receive.at[step], device)

    def piece(self, shift, low):
        ref = self.at(shift, self.core)
        rows = pl.ds(0, self.cut) if low else pl.ds(self.cut, self.block[0] - self.cut)
        return ref.at[rows]

    def sends(self):
        place = self.at(0, self.core)
        low, high = self.piece(3, True), None
        found = [self.copy(0, 1, self.x, place), self.copy(1, 3, self.x, place)]
        found.append(self.copy(2, 1, low, low))
        if self.cut < self.block[0]:
            high = self.piece(1, False)
            found.append(self.copy(3, 3, high, high))
        return found

    def receipts(self):
        found = [
            self.copy(0, 1, self.x, self.at(3, self.core)),
            self.copy(1, 3, self.x, self.at(1, self.core)),
        ]
        low = self.piece(2, True)
        found.append(self.copy(2, 1, low, low))
        if self.cut < self.block[0]:
            high = self.piece(2, False)
            found.append(self.copy(3, 3, high, high))
        return found

    def forward(self, step, core):
        place = self.at((0, 3, 1, 2)[step], core)
        source = self.x if step == 0 else place
        device = {"core": 1 - self.core}
        return remote(source, place, self.f_send.at[step], self.f_receive.at[step], device)

    def start(self):
        sends = self.sends()
        sends[0].start()
        sends[1].start()
        self.mine().start()
        self.forward(0, self.core).start()

    def middle(self):
        sends, receipts = self.sends(), self.receipts()
        for step in range(2):
            receipts[step].wait_recv()
            if step + 2 < len(sends):
                sends[step + 2].start()
            self.forward(step + 1, self.core).start()

    def late(self):
        for receipt in self.receipts()[2:]:
            receipt.wait_recv()
        self.forward(3, self.core).start()

    def end(self):
        self.mine().wait()
        for send in self.sends():
            send.wait_send()
        for step in range(4):
            self.forward(step, self.core).wait_send()
            self.forward(step, 1 - self.core).wait_recv()


class RingScatter:
    def __init__(self, axes, array):
        self.axes = axes
        self.block = array.shape[2:]
        self.cut = split_point(self.block[0])
        self.in_space = pltpu.VMEM
        self.out = jax.ShapeDtypeStruct(self.block, jnp.float32)
        self.out_space = pltpu.VMEM
        rows = (self.cut, self.block[0] - self.cut)
        self.scratch = [pltpu.VMEM((4,) + self.block, array.dtype)] * 2
        self.scratch += [pltpu.VMEM((count,) + self.block[1:], array.dtype) for count in rows]
        self.scratch += [pltpu.VMEM((2,) + self.block, array.dtype)]
        self.scratch += [pltpu.SemaphoreType.DMA((4,))] * 4

    def bind(self, source, target, scratch):
        self.x, self.o = source, target
        self.half, self.summed = scratch[:2]
        self.via, self.land = scratch[2:4], scratch[4]
        self.s_one, self.r_one, self.send, self.receive = scratch[5:]
        self.me, self.core = group_index(self.axes), lax.axis_index("core")
        self.stages = [self.start, self.middle, self.late, self.end]

    def across(self, shift):
        to = (self.me + shift) % 4
        return remote(
            self.x.at[to, 1 - self.core],
            self.half.at[to],
            self.s_one.at[shift],
            self.r_one.at[shift],
            {"core": 1 - self.core},
        )

    def copy(self, step, to, source, target):
        device = member(self.axes, (self.me + to) % 4)
        return remote(source, target, self.send.at[step], self.receive.at[step], device)

    def copies(self):
        far = self.summed.at[(self.me + 2) % 4]
        low, high = pl.ds(0, self.cut), pl.ds(self.cut, self.block[0] - self.cut)
        return [
            self.copy(0, 1, far.at[low], self.via[0]),
            self.copy(1, 3, far.at[high], self.via[1]),
            self.copy(2, 1, self.summed.at[(self.me + 1) % 4], self.land.at[0]),
            self.copy(3, 3, self.summed.at[(self.me + 3) % 4], self.land.at[1]),
        ]

    def both(self, shift):
        self.across(shift).wait_recv()
        to = (self.me + shift) % 4
        return self.x[to, self.core].astype(jnp.float32) + self.half[to].astype(jnp.float32)

    def start(self):
        for shift in (2, 1, 3, 0):
            self.across(shift).start()

    def middle(self):
        copies = self.copies()
        kind = self.summed.dtype
        self.summed[(self.me + 2) % 4] = self.both(2).astype(kind)
        copies[0].start()
        copies[1].start()
        near, back = self.both(1), self.both(3)
        cut = self.cut
        after, before = (self.me + 1) % 4, (self.me + 3) % 4
        copies[0].wait_recv()
        self.summed[after, :cut] = (near[:cut] + self.via[0][...].astype(jnp.float32)).astype(kind)
        self.summed[after, cut:] = near[cut:].astype(kind)
        copies[2].start()
        copies[1].wait_recv()
        self.summed[before, cut:] = (back[cut:] + self.via[1][...].astype(jnp.float32)).astype(kind)
        self.summed[before, :cut] = back[:cut].astype(kind)
        copies[3].start()
        self.o[...] = self.both(0)

    def late(self):
        pass

    def end(self):
        copies = self.copies()
        for step in range(2):
            copies[step + 2].wait_recv()
            self.o[...] += self.land[step].astype(jnp.float32)
        for shift in range(4):
            self.across(shift).wait_send()
            copies[shift].wait_send()


class AxisScatter:
    def __init__(self, axes, array):
        self.axes = axes
        self.block, self.kind = array.shape[1:], array.dtype
        self.in_space = pltpu.VMEM
        self.out = jax.ShapeDtypeStruct(self.block, self.kind)
        self.out_space = pltpu.VMEM
        self.scratch = [pltpu.VMEM(array.shape, self.kind)] + [pltpu.SemaphoreType.DMA((4,))] * 2

    def bind(self, source, target, scratch):
        self.x, self.o = source, target
        self.land, self.send, self.receive = scratch
        self.me = lax.axis_index(self.axes[0])
        self.stages = [self.start, self.end]

    def outward(self, k, slot):
        to = (self.me + k) % 4
        send, receive = self.send.at[k], self.receive.at[k]
        return remote(self.x.at[to], self.land.at[slot], send, receive, {self.axes[0]: to})

    def start(self):
        for k in (2, 1, 3):
            self.outward(k, self.me).start()

    def end(self):
        slots = [(self.me + 4 - k) % 4 for k in range(4)]
        for k in range(1, 4):
            self.outward(k, slots[k]).wait_recv()
        for item in range(self.block[0] if len(self.block) > 2 else 1):
            at = (item,) if len(self.block) > 2 else ()
            total = self.x[(self.me,) + at].astype(jnp.float32)
            for k in range(1, 4):
                total += self.land[(slots[k],) + at].astype(jnp.float32)
            if at:
                self.o[item] = total.astype(self.kind)
            else:
                self.o[...] = total.astype(self.kind)
        for k in range(1, 4):
            self.outward(k, self.me).wait_send()


class AxisGather:
    def __init__(self, axes, array, share=False):
        self.axes, self.share = axes, share
        self.in_space = pltpu.VMEM
        lead = (2, 4) if share else (4,)
        self.out = jax.ShapeDtypeStruct(lead + array.shape, array.dtype)
        self.out_space = pl.ANY
        self.scratch = [pltpu.SemaphoreType.DMA] + [pltpu.SemaphoreType.DMA((4,))] * 4

    def bind(self, source, target, scratch):
        self.x, self.o, self.local = source, target, scratch[0]
        self.send, self.receive, self.f_send, self.f_receive = scratch[1:]
        self.me, self.core = lax.axis_index(self.axes[0]), lax.axis_index("core")
        self.stages = [self.start, self.late, self.end] if self.share else [self.start, self.end]

    def at(self, slot, core):
        return self.o.at[core, slot] if self.share else self.o.at[slot]

    def mine(self):
        return pltpu.make_async_copy(self.x, self.at(self.me, self.core), self.local)

    def outward(self, k, slot):
        send, receive = self.send.at[k], self.receive.at[k]
        device = {self.axes[0]: (self.me + k) % 4}
        return remote(self.x, self.at(slot, self.core), send, receive, device)

    def forward(self, k, core):
        place = self.at((self.me + 4 - k) % 4, core)
        send, receive = self.f_send.at[k], self.f_receive.at[k]
        source = place if k else self.x
        return remote(source, place, send, receive, {"core": 1 - self.core})

    def start(self):
        for k in (2, 1, 3):
            self.outward(k, self.me).start()
        self.mine().start()
        if self.share:
            self.forward(0, self.core).start()

    def late(self):
        for k in (1, 3, 2):
            self.outward(k, (self.me + 4 - k) % 4).wait_recv()
            self.forward(k, self.core).start()

    def end(self):
        self.mine().wait()
        for k in range(4):
            if k:
                self.outward(k, self.me).wait_send()
                if not self.share:
                    self.outward(k, (self.me + 4 - k) % 4).wait_recv()
            if self.share:
                self.forward(k, self.core).wait_send()
                self.forward(k, 1 - self.core).wait_recv()


class Deal:
    def __init__(self, axes, array):
        self.axes = axes + ROW
        self.scatter = AxisScatter(axes, array)
        self.exchange = Exchange(ROW, self.scatter.out)
        self.in_space = pltpu.VMEM
        self.out, self.out_space = self.exchange.out, pl.ANY
        own = pltpu.VMEM(self.scatter.block, array.dtype)
        self.scratch = [own] + self.scatter.scratch + self.exchange.scratch

    def bind(self, source, target, scratch):
        count = 1 + len(self.scatter.scratch)
        self.scatter.bind(source, scratch[0], scratch[1:count])
        self.exchange.bind(scratch[0], target, scratch[count:])
        self.stages = self.scatter.stages + self.exchange.stages


def run_stages(ops):
    longest = max(len(op.stages) for op in ops)
    for index in range(longest - 1):
        for op in ops:
            if index < len(op.stages) - 1:
                op.stages[index]()
    for op in ops:
        op.stages[-1]()


def communicate_kernel(ops, after, compute, inputs, outputs, *refs):
    refs = list(refs)
    count, more, waiting = len(ops), len(after), after
    sources, extra = refs[:count], refs[count : count + inputs]
    refs = refs[count + inputs :]
    targets, late_targets = refs[:count], refs[count : count + more]
    made, scratch = refs[count + more : count + more + outputs], refs[count + more + outputs :]
    late_sources = [scratch.pop(0) for unused in after]
    axes = []
    for op, source, target in zip(ops + after, sources + late_sources, targets + late_targets):
        op.bind(source, target, [scratch.pop(0) for unused in op.scratch])
        axes += [axis for axis in op.axes if axis not in axes]
    barrier = pltpu.get_barrier_semaphore()
    devices = [{"core": 1 - lax.axis_index("core")}]
    for axis in axes:
        devices += [{axis: (lax.axis_index(axis) + k) % 4} for k in range(1, 4)]
    for device in devices:
        pl.semaphore_signal(barrier, inc=1, device_id=device, device_id_type=MESH)
    pl.semaphore_wait(barrier, len(devices))
    if compute is None:
        run_stages(ops)
    else:
        for op in ops:
            op.stages[0]()
        for function, count in compute:
            function(*extra, *made, *late_sources)
            for op in after[:count]:
                op.stages[0]()
            after = after[count:]
        for stage in (1, 2, 3):
            for op in ops:
                op.stages[stage]()
        for op in waiting:
            op.stages[1]()


def communicate(name, identity, *requests, compute=None, inputs=(), outputs=(), after=()):
    arrays = [array for kind, axes, array in requests]
    ops = [kind(axes, array) for kind, axes, array in requests]
    late = [kind(axes, array) for kind, axes, array in after]
    held = [pltpu.VMEM(array.shape, array.dtype) for kind, axes, array in after]
    vmem = pl.BlockSpec(memory_space=pltpu.VMEM)
    return pl.pallas_call(
        functools.partial(communicate_kernel, ops, late, compute, len(inputs), len(outputs)),
        out_shape=tuple(op.out for op in ops + late) + tuple(outputs),
        in_specs=[pl.BlockSpec(memory_space=op.in_space) for op in ops] + [vmem] * len(inputs),
        out_specs=tuple(pl.BlockSpec(memory_space=op.out_space) for op in ops + late)
        + (vmem,) * len(outputs),
        scratch_shapes=held + [item for op in ops + late for item in op.scratch],
        compiler_params=pltpu.CompilerParams(
            collective_id=identity,
            has_side_effects=True,
            vmem_limit_bytes=56 * 1024 * 1024,
        ),
        cost_estimate=pl.CostEstimate(flops=0, bytes_accessed=1_000_000, transcendentals=0),
        name=name,
    )(*arrays, *inputs)


def hidden_grads(cot_ref, down_ref, target):
    def step(index, unused):
        rows = pl.ds(pl.multiple_of(index * 256, 256), 256)
        target[rows, :] = dot(cot_ref[rows, :], down_ref[...], 1, 1)
        return unused

    lax.fori_loop(0, cot_ref.shape[0] // 256, step, 0)


ROWS = 16
GROUPS = 14
DOWN_ROWS = 48
DOWN_CUT = 512


def store_groups(index, value, target, swapped):
    for item in range(128 // ROWS):
        group = index * (128 // ROWS) + item
        owner, chip = group // GROUPS, group % GROUPS
        z, y = chip // 4, chip % 4
        spot = (y, z) if swapped else (z, y)
        target[spot + (owner,)] = value[item * ROWS : (item + 1) * ROWS]


def gate_or_up_grads(normed_ref, d_ref, target, swapped):
    for chip in range(GROUPS, 16):
        z, y = chip // 4, chip % 4
        target[(y, z) if swapped else (z, y)] = jnp.zeros(target.shape[2:], target.dtype)

    def step(index, unused):
        place = pl.ds(pl.multiple_of(index * 128, 128), 128)
        value = dot(normed_ref[:, place], d_ref[...], 0, 0).astype(jnp.bfloat16)
        store_groups(index, value, target, swapped)
        return unused

    lax.fori_loop(0, D // 128, step, 0)


def gate_grads(normed, cot, hidden, d_gate, d_up, gate, up, down, rest):
    gate_or_up_grads(normed, d_gate, gate, False)


def up_grads(normed, cot, hidden, d_gate, d_up, gate, up, down, rest):
    gate_or_up_grads(normed, d_up, up, True)


def down_grads(normed, cot_ref, hidden_ref, d_gate, d_up, gate, up, down_ref, rest_ref):
    part = hidden_ref.shape[1]
    for chip in range(part // DOWN_ROWS, 16):
        z, y = chip // 4, chip % 4
        down_ref[z, y] = jnp.zeros(down_ref.shape[2:], down_ref.dtype)
        rest_ref[y, z] = jnp.zeros(rest_ref.shape[2:], rest_ref.dtype)

    def step(index, target, swapped, start):
        place = pl.ds(pl.multiple_of(index * 128, 128), 128)
        down = dot(cot_ref[:, place], hidden_ref[...], 0, 0).T.astype(jnp.bfloat16)
        columns = pl.ds(pl.multiple_of(index * 128 - start, 128), 128)
        for chip in range(-(-part // DOWN_ROWS)):
            first = chip * DOWN_ROWS
            rows = min(DOWN_ROWS, part - first)
            z, y = chip // 4, chip % 4
            spot = (y, z) if swapped else (z, y)
            target[spot + (pl.ds(0, rows), columns)] = down[first : first + rows]

    def low_step(index, unused):
        step(index, down_ref, False, 0)
        return unused

    def high_step(index, unused):
        step(index, rest_ref, True, DOWN_CUT)
        return unused

    lax.fori_loop(0, DOWN_CUT // 128, low_step, 0)
    lax.fori_loop(DOWN_CUT // 128, D // 128, high_step, 0)


def widen_kernel(gate_ref, up_ref, gate_out_ref, up_out_ref):
    part = gate_ref.shape[-1]
    for source, target in ((gate_ref, gate_out_ref), (up_ref, up_out_ref)):
        for index in range(4):
            for core in range(2):
                first = (2 * index + core) * part
                for item in range(2):
                    spot = (core, 0, item, index) if source is gate_ref else (core, item, 0, index)
                    rows = slice(item * ROWS, (item + 1) * ROWS)
                    target[rows, first : first + part] = source[spot].astype(jnp.float32)


def widen(gate, up):
    part = gate.shape[-1]
    target = pl.BlockSpec((2 * ROWS, 8 * part), lambda index: (index, 0))
    wide = jax.ShapeDtypeStruct((ROWS * GROUPS, 8 * part), jnp.float32)
    return pl.pallas_call(
        widen_kernel,
        grid=(GROUPS // 2,),
        out_shape=(wide, wide),
        in_specs=[
            pl.BlockSpec(
                (2, 1, 2, 4, ROWS, part), lambda index: (0, index // 2, index % 2, 0, 0, 0)
            ),
            pl.BlockSpec(
                (2, 2, 1, 4, ROWS, part), lambda index: (0, index % 2, index // 2, 0, 0, 0)
            ),
        ],
        out_specs=(target, target),
        name="widen",
    )(gate, up)


def widen_down_kernel(low_ref, high_ref, out_ref):
    part = out_ref.shape[0] // 2
    for core in range(2):
        for chip in range(-(-part // DOWN_ROWS)):
            first = chip * DOWN_ROWS
            rows = min(DOWN_ROWS, part - first)
            z, y = chip // 4, chip % 4
            place = pl.ds(core * part + first, rows)
            out_ref[place, :DOWN_CUT] = low_ref[core, z, y, :rows].astype(jnp.float32)
            out_ref[place, DOWN_CUT:] = high_ref[core, y, z, :rows].astype(jnp.float32)


def widen_down(low, high, part):
    vmem = pl.BlockSpec(memory_space=pltpu.VMEM)
    return pl.pallas_call(
        widen_down_kernel,
        out_shape=jax.ShapeDtypeStruct((2 * part, D), jnp.float32),
        in_specs=[vmem, vmem],
        out_specs=vmem,
        compiler_params=pltpu.CompilerParams(vmem_limit_bytes=32 * 1024 * 1024),
        name="widen_down",
    )(low, high)


def split_sums_kernel(rows, top_ref, end_ref, qkv_ref, out_ref, vectors_ref):
    first = qkv_ref.shape[1] // 128
    for chip in range(16):
        target = qkv_ref if chip < first else out_ref
        place = (chip if chip < first else chip - first) * 128
        for core in range(2):
            z, y = chip // 4, chip % 4
            top = top_ref[core, z, y].astype(jnp.float32)
            end = end_ref[core, y, z].astype(jnp.float32)
            start, cut = core * rows, top.shape[0]
            target[start : start + cut, place : place + 128] = top
            target[start + cut : start + rows, place : place + 128] = end[: rows - cut]
        vectors_ref[:, chip * 128 : (chip + 1) * 128] = end[rows - cut : rows - cut + 8]


def split_sums(top, end, rows, columns):
    chips = 16
    vmem = pl.BlockSpec(memory_space=pltpu.VMEM)
    shapes = ((2 * rows, columns), (2 * rows, chips * 128 - columns), (8, chips * 128))
    return pl.pallas_call(
        functools.partial(split_sums_kernel, rows),
        out_shape=tuple(jax.ShapeDtypeStruct(shape, jnp.float32) for shape in shapes),
        in_specs=[vmem, vmem],
        out_specs=(vmem,) * 3,
        name="split_sums",
    )(top, end)


def rms_apply(values, gain):
    mean_square = jnp.mean(values * values, axis=-1, keepdims=True)
    return values * lax.rsqrt(mean_square + norm_eps) * gain


def half_turn(values):
    middle = values.shape[-1] // 2
    return jnp.concatenate([-values[..., middle:], values[..., :middle]], axis=-1)


def rotate(values, cosine, sine):
    return values * cosine + half_turn(values) * sine


def rope_tables(positions, head_dim):
    middle = head_dim // 2
    inverse = rope_base ** (-(jnp.arange(middle).astype(jnp.float32) * 2.0) / head_dim)
    angles = positions.astype(jnp.float32)[:, None] * inverse[None, :]
    angles = jnp.concatenate([angles, angles], axis=-1)
    return (jnp.cos(angles), jnp.sin(angles))


def swiglu(gate_in, up_in):
    return jax.nn.silu(gate_in) * up_in


def dot(a, b, ca=1, cb=0):
    return lax.dot_general(a, b, (((ca,), (cb,)), ((), ())), preferred_element_type=jnp.float32)


def causal_copy(order_ref, k_ref, v_ref, sorted_ref):
    def move(slot, unused):
        half, core, y, z = slot % 2, slot // 2 % 2, slot // 4 % 4, slot // 16
        k_place = pl.multiple_of((((core * 4 + z) * 4 + y) * 2 + half) * SPAN, SPAN)
        v_place = pl.multiple_of((((core * 4 + y) * 4 + z) * 2 + half) * SPAN, SPAN)
        target = pl.ds(pl.multiple_of(order_ref[slot] * SPAN, SPAN), SPAN)
        sorted_ref[target, :128] = k_ref[pl.ds(k_place, SPAN), :]
        sorted_ref[target, 128:] = v_ref[pl.ds(v_place, SPAN), :]
        return unused

    lax.fori_loop(0, k_ref.shape[0] // SPAN, move, 0)


def visible(start, place, rows):
    key_place = lax.broadcasted_iota(jnp.int32, (CHUNK, rows), 0) + start
    lane = lax.broadcasted_iota(jnp.int32, (CHUNK, rows), 1)
    return key_place <= place * SPAN + lane % SPAN


def head_tile(heads, half, group):
    lanes = slice(half * SPAN, (half + 1) * SPAN)
    first = group * GROUP
    return jnp.concatenate([heads[first + item][:, lanes] for item in range(GROUP)], axis=1)


def padded(tile, group):
    empty = jnp.zeros_like(tile)
    return jnp.concatenate([tile, empty] if group == 0 else [empty, tile], axis=0)


def token_rows(tiles):
    blocks = []
    for tile in tiles:
        turned = tile.T
        blocks += [turned[item * SPAN : (item + 1) * SPAN] for item in range(GROUP)]
    pairs = [
        jnp.concatenate([blocks[2 * item], blocks[2 * item + 1]], axis=1) for item in range(GROUP)
    ]
    return jnp.concatenate(pairs, axis=1)


def prepare_kernel(
    x_ref,
    gain_ref,
    weight_ref,
    bias_ref,
    cos_ref,
    sin_ref,
    normed_ref,
    q_ref,
    q_rows_ref,
    k_ref,
    v_ref,
):
    wide = x_ref[...].astype(jnp.float32)
    scale = lax.rsqrt(jnp.mean(wide * wide, axis=-1, keepdims=True) + norm_eps)
    normed = (wide * scale * gain_ref[...]).astype(jnp.bfloat16)
    normed_ref[...] = normed
    mixed = dot(normed, weight_ref[...]) + bias_ref[...]
    count = QH + KVH
    v_ref[...] = mixed[:, count * HD :].astype(jnp.bfloat16)
    turned = mixed[:, : count * HD].T
    cosine, sine = cos_ref[...], sin_ref[...]
    heads = []
    for head in range(count):
        first = turned[head * HD : head * HD + HD // 2]
        second = turned[head * HD + HD // 2 : (head + 1) * HD]
        rotated = [first * cosine - second * sine, second * cosine + first * sine]
        heads.append(jnp.concatenate(rotated, axis=0))
    k_ref[...] = jnp.concatenate(heads[QH:], axis=0).T.astype(jnp.bfloat16)
    for half in range(2):
        for group in range(KVH):
            tile = padded(head_tile(heads, half, group) * HD**-0.5, group)
            q_ref[half, group] = tile.astype(jnp.bfloat16)
            q_rows_ref[half, group] = tile.T.astype(jnp.bfloat16)


def prepare(inputs, gain, weight, bias, cosine, sine):
    tokens = inputs.shape[0]
    rows = GROUP * SPAN
    vmem = pl.BlockSpec(memory_space=pltpu.VMEM)
    low = functools.partial(jax.ShapeDtypeStruct, dtype=jnp.bfloat16)
    return pl.pallas_call(
        prepare_kernel,
        out_shape=(
            low((tokens, D)),
            low((2, KVH, 128, rows)),
            low((2, KVH, rows, 128)),
            low((tokens, KVH * HD)),
            low((tokens, KVH * HD)),
        ),
        in_specs=[vmem] * 6,
        out_specs=(vmem,) * 5,
        compiler_params=pltpu.CompilerParams(vmem_limit_bytes=32 * 1024 * 1024),
        cost_estimate=pl.CostEstimate(flops=0, bytes_accessed=1_000_000, transcendentals=0),
        name="prepare",
    )(inputs, gain, weight, bias, cosine, sine)


def attend_kernel(
    order_ref,
    mine_ref,
    k_ref,
    v_ref,
    q_ref,
    x_ref,
    weight_ref,
    gain_ref,
    out_ref,
    lse_ref,
    attended_ref,
    residual_ref,
    normed_ref,
    sorted_ref,
):
    causal_copy(order_ref, k_ref, v_ref, sorted_ref)
    rows = q_ref.shape[-1]
    for half in range(2):
        place = mine_ref[half]
        last = place * SPAN // CHUNK

        def step(index, carry, masked, half=half, place=place):
            start = pl.multiple_of(index * CHUNK, CHUNK)
            keys = sorted_ref[pl.ds(start, CHUNK), :128]
            values = sorted_ref[pl.ds(start, CHUNK), 128:]
            result = []
            for head in range(KVH):
                top, total, mixed = carry[head]
                scores = dot(keys, q_ref[half, head])
                if masked:
                    scores = jnp.where(visible(start, place, rows), scores, masked_score)
                new_top = jnp.maximum(top, jnp.max(scores, axis=0, keepdims=True))
                shrink = jnp.exp(top - new_top)
                weights = jnp.exp(scores - new_top)
                total = total * shrink + jnp.sum(weights, axis=0, keepdims=True)
                mixed = mixed * shrink + dot(values, weights.astype(jnp.bfloat16), 0, 0)
                result.append((new_top, total, mixed))
            return tuple(result)

        empty = tuple(
            (
                jnp.full((1, rows), masked_score, jnp.float32),
                jnp.zeros((1, rows), jnp.float32),
                jnp.zeros((128, rows), jnp.float32),
            )
            for head in range(KVH)
        )
        carry = lax.fori_loop(0, last, functools.partial(step, masked=False), empty)
        carry = step(last, carry, True)
        tiles = []
        for head in range(KVH):
            top, total, mixed = carry[head]
            tiles.append(mixed[head * HD : (head + 1) * HD] / total)
            out_ref[half, head] = tiles[head]
            lse_ref[half, head] = top + jnp.log(total)
        place = pl.ds(half * SPAN, SPAN)
        attended_ref[place, :] = token_rows(tiles).astype(jnp.bfloat16)
    residual = x_ref[...].astype(jnp.float32) + dot(attended_ref[...], weight_ref[...])
    residual_ref[...] = residual
    scale = lax.rsqrt(jnp.mean(residual * residual, axis=-1, keepdims=True) + norm_eps)
    normed_ref[...] = (residual * scale * gain_ref[...]).astype(jnp.bfloat16)


def attend(order, mine, k_all, v_all, q_pad, inputs, weight, gain):
    halves, heads, unused, rows = q_pad.shape
    smem = pl.BlockSpec(memory_space=pltpu.SMEM)
    vmem = pl.BlockSpec(memory_space=pltpu.VMEM)
    return pl.pallas_call(
        attend_kernel,
        out_shape=(
            jax.ShapeDtypeStruct((halves, heads, HD, rows), jnp.float32),
            jax.ShapeDtypeStruct((halves, heads, 1, rows), jnp.float32),
            jax.ShapeDtypeStruct(inputs.shape, jnp.bfloat16),
            jax.ShapeDtypeStruct(inputs.shape, jnp.float32),
            jax.ShapeDtypeStruct(inputs.shape, jnp.bfloat16),
        ),
        in_specs=[smem, smem] + [vmem] * 6,
        out_specs=(vmem,) * 5,
        scratch_shapes=[pltpu.VMEM((k_all.shape[0], 256), k_all.dtype)],
        compiler_params=pltpu.CompilerParams(vmem_limit_bytes=48 * 1024 * 1024),
        cost_estimate=pl.CostEstimate(
            flops=0, bytes_accessed=1_000_000, transcendentals=0
        ),
        name="attend",
    )(order, mine, k_all, v_all, q_pad, inputs, weight, gain)


def attend_back_kernel(
    order_ref,
    mine_ref,
    k_ref,
    v_ref,
    q_ref,
    q_rows_ref,
    out_ref,
    lse_ref,
    d_normed_ref,
    residual_ref,
    cot_ref,
    gain_ref,
    weight_ref,
    cos_ref,
    sin_ref,
    dq_ref,
    dk_ref,
    dv_ref,
    d_residual_ref,
    d_branch_ref,
    gain_grad_ref,
    sorted_ref,
    sum_ref,
    do_ref,
    do_rows_ref,
    delta_ref,
):
    residual, d_normed = residual_ref[...], d_normed_ref[...]
    scale = lax.rsqrt(jnp.mean(residual * residual, axis=-1, keepdims=True) + norm_eps)
    unit = residual * scale
    gain_grad_ref[...] = jnp.sum(d_normed * unit, axis=0, keepdims=True)
    weighted = d_normed * gain_ref[...]
    inner = jnp.mean(weighted * unit, axis=-1, keepdims=True)
    d_residual = cot_ref[...].astype(jnp.float32) + scale * (weighted - unit * inner)
    d_residual_ref[...] = d_residual
    d_branch = d_residual.astype(jnp.bfloat16)
    d_branch_ref[...] = d_branch
    d_attended = dot(d_branch, weight_ref[...], 1, 1).astype(jnp.bfloat16).astype(jnp.float32)
    turned = d_attended.T
    heads = [turned[head * HD : (head + 1) * HD] for head in range(QH)]
    for half in range(2):
        for group in range(KVH):
            tile = head_tile(heads, half, group)
            product = tile * out_ref[half, group]
            delta_ref[half, group] = jnp.sum(product, axis=0, keepdims=True)
            tile = padded(tile, group)
            do_ref[half, group] = tile.astype(jnp.bfloat16)
            do_rows_ref[half, group] = tile.T.astype(jnp.bfloat16)
    causal_copy(order_ref, k_ref, v_ref, sorted_ref)
    sum_ref[...] = jnp.zeros_like(sum_ref)
    rows = q_ref.shape[-1]
    for half in range(2):
        place = mine_ref[half]
        last = place * SPAN // CHUNK

        def step(index, carry, masked, half=half, place=place):
            start = pl.multiple_of(index * CHUNK, CHUNK)
            keys = sorted_ref[pl.ds(start, CHUNK), :128]
            values = sorted_ref[pl.ds(start, CHUNK), 128:]
            d_keys = sum_ref[pl.ds(start, CHUNK), :128]
            d_values = sum_ref[pl.ds(start, CHUNK), 128:]
            result = []
            for head in range(KVH):
                scores = dot(keys, q_ref[half, head])
                probs = jnp.exp(scores - lse_ref[half, head])
                if masked:
                    probs = jnp.where(visible(start, place, rows), probs, 0.0)
                d_probs = dot(values, do_ref[half, head])
                d_scores = (probs * (d_probs - delta_ref[half, head])).astype(jnp.bfloat16)
                d_values += dot(probs.astype(jnp.bfloat16), do_rows_ref[half, head])
                d_keys += dot(d_scores, q_rows_ref[half, head])
                result.append(carry[head] + dot(keys, d_scores, 0, 0))
            sum_ref[pl.ds(start, CHUNK), :128] = d_keys
            sum_ref[pl.ds(start, CHUNK), 128:] = d_values
            return tuple(result)

        empty = tuple(jnp.zeros((128, rows), jnp.float32) for head in range(KVH))
        carry = lax.fori_loop(0, last, functools.partial(step, masked=False), empty)
        carry = step(last, carry, True)
        lanes = slice(half * SPAN, (half + 1) * SPAN)
        cosine = jnp.concatenate([cos_ref[:, lanes]] * GROUP, axis=1)
        sine = jnp.concatenate([sin_ref[:, lanes]] * GROUP, axis=1)
        tiles = []
        for head in range(KVH):
            middle = head * HD + HD // 2
            first = carry[head][head * HD : middle] * (HD**-0.5)
            second = carry[head][middle : (head + 1) * HD] * (HD**-0.5)
            turned = [first * cosine + second * sine, second * cosine - first * sine]
            tiles.append(jnp.concatenate(turned, axis=0))
        dq_ref[pl.ds(half * SPAN, SPAN), :] = token_rows(tiles).astype(jnp.bfloat16)

    def move(slot, unused):
        rest, y, z = slot % 4, slot // 4 % 4, slot // 16
        k_place = pl.multiple_of(slot * SPAN, SPAN)
        v_place = pl.multiple_of(((y * 4 + z) * 4 + rest) * SPAN, SPAN)
        source = pl.ds(pl.multiple_of(order_ref[slot] * SPAN, SPAN), SPAN)
        dk_ref[pl.ds(k_place, SPAN), :] = sum_ref[source, :128].astype(jnp.bfloat16)
        dv_ref[pl.ds(v_place, SPAN), :] = sum_ref[source, 128:].astype(jnp.bfloat16)
        return unused

    lax.fori_loop(0, dk_ref.shape[0] // SPAN, move, 0)


def attend_back(order, mine, k_all, v_all, q_pad, *rest):
    halves, heads, unused, rows = q_pad.shape
    tokens = 2 * SPAN
    smem = pl.BlockSpec(memory_space=pltpu.SMEM)
    vmem = pl.BlockSpec(memory_space=pltpu.VMEM)
    return pl.pallas_call(
        attend_back_kernel,
        out_shape=(
            jax.ShapeDtypeStruct((tokens, D), jnp.bfloat16),
            jax.ShapeDtypeStruct(k_all.shape, jnp.bfloat16),
            jax.ShapeDtypeStruct(v_all.shape, jnp.bfloat16),
            jax.ShapeDtypeStruct((tokens, D), jnp.float32),
            jax.ShapeDtypeStruct((tokens, D), jnp.bfloat16),
            jax.ShapeDtypeStruct((1, D), jnp.float32),
        ),
        in_specs=[smem, smem] + [vmem] * (3 + len(rest)),
        out_specs=(vmem,) * 6,
        scratch_shapes=[
            pltpu.VMEM((k_all.shape[0], 256), k_all.dtype),
            pltpu.VMEM((k_all.shape[0], 256), jnp.float32),
            pltpu.VMEM((halves, heads, 128, rows), jnp.bfloat16),
            pltpu.VMEM((halves, heads, rows, 128), jnp.bfloat16),
            pltpu.VMEM((halves, heads, 1, rows), jnp.float32),
        ],
        compiler_params=pltpu.CompilerParams(vmem_limit_bytes=48 * 1024 * 1024),
        cost_estimate=pl.CostEstimate(flops=0, bytes_accessed=1_000_000, transcendentals=0),
        name="attend_back",
    )(order, mine, k_all, v_all, q_pad, *rest)


def body(
    inputs,
    cotangent,
    span_order,
    positions,
    attn_gain,
    qkv_weight,
    qkv_bias,
    out_weight,
    mlp_gain,
    gate_weight,
    up_weight,
    down_weight,
):
    token_count = inputs.shape[0]
    q_cols = QH * HD
    k_cols = KVH * HD
    slices = lax.axis_size("dp")
    own_rows = D // slices
    part = FF // (slices * 2)
    dp = lax.axis_index("dp")
    core = lax.axis_index("core")
    slot = (lax.axis_index("z") * lax.axis_size("y") + lax.axis_index("y")) * 2 + core

    small = jnp.concatenate([attn_gain, mlp_gain, qkv_bias])
    small = jnp.pad(small, (0, 2048 - small.shape[0])).reshape(16, 128)
    qkv_half = lax.dynamic_slice_in_dim(qkv_weight, core * (own_rows // 2), own_rows // 2)
    qkv_full, small = communicate(
        "qkv_in", 0, (RingGather, ROW, qkv_half), (RingGather, ROW, small)
    )
    qkv_full, out_weight = lax.optimization_barrier((qkv_full.reshape(D, -1), out_weight))
    small = small[:, 0].reshape(slices, -1)
    gain_one_wide = small[:, :own_rows].reshape(D).astype(jnp.float32)
    gain_two_wide = small[:, own_rows : 2 * own_rows].reshape(D).astype(jnp.float32)
    bias_full = small[:, 2 * own_rows : 2 * own_rows + qkv_bias.shape[0]]
    bias_full = bias_full.reshape(-1).astype(jnp.float32)
    out_full = lax.all_gather(out_weight, "dp", axis=0, tiled=True)

    def column_blocks(weight):
        parts = [weight[:, part * index : part * (index + 1)] for index in range(2 * slices)]
        return [jnp.where(core == 0, parts[2 * p], parts[2 * p + 1]) for p in range(slices)]

    gate_blocks, up_blocks = column_blocks(gate_weight), column_blocks(up_weight)
    gate_up = jnp.stack(
        [jnp.concatenate([gate_blocks[p], up_blocks[p]], axis=0) for p in range(slices)]
    )
    gate_up = lax.all_to_all(gate_up, "dp", 0, 0, tiled=True)
    gate_part = gate_up[:, :own_rows].reshape(D, part)
    up_part = gate_up[:, own_rows:].reshape(D, part)
    down_part = lax.dynamic_slice_in_dim(down_weight, core * part, part, axis=0)
    cot_all = lax.all_gather(cotangent, ("dp", "core"), axis=0, tiled=True)

    inputs_wide = inputs.astype(jnp.float32)
    cosine, sine = rope_tables(positions, HD)
    cos_turned, sin_turned = cosine[:, : HD // 2].T, sine[:, : HD // 2].T
    cosine = cosine[:, None, :]
    sine = sine[:, None, :]
    normed_one, q_pad, q_rows, key_rot, value_low = prepare(
        inputs, gain_one_wide[None], qkv_full, bias_full[None], cos_turned, sin_turned
    )
    normed_one_all = lax.all_gather(normed_one, ("dp", "core"), axis=0, tiled=True)
    k_all, v_all = communicate(
        "kv_in", 1, (PlaneGather, PLANE, key_rot), (PlaneGather, ENALP, value_low)
    )
    k_all = k_all.reshape(-1, k_cols)
    v_all = v_all.reshape(-1, k_cols)
    mine = lax.dynamic_slice_in_dim(span_order, 2 * slot, 2)
    attended_cols, lse, attended_low, residual, normed_two = attend(
        span_order, mine, k_all, v_all, q_pad, inputs, out_full, gain_two_wide[None]
    )
    attended_all = lax.all_gather(attended_low, ("dp", "core"), axis=0, tiled=True)
    normed_all, d_hidden = communicate(
        "normed_in",
        2,
        (RingGather, ROW, normed_two),
        compute=((hidden_grads, 0),),
        inputs=(cot_all, down_part),
        outputs=(jax.ShapeDtypeStruct((cot_all.shape[0], part), jnp.float32),),
    )
    normed_all = normed_all.reshape(-1, D)
    gate_proj = dot(normed_all, gate_part)
    up_proj = dot(normed_all, up_part)
    hidden_low = swiglu(gate_proj, up_proj).astype(jnp.bfloat16)
    out_sum = dot(hidden_low, down_part).astype(jnp.bfloat16)
    d_gate, d_up = jax.vjp(swiglu, gate_proj, up_proj)[1](d_hidden)
    d_gate = d_gate.astype(jnp.bfloat16)
    d_up = d_up.astype(jnp.bfloat16)
    d_norm_sum = (dot(d_gate, gate_part, 1, 1) + dot(d_up, up_part, 1, 1)).astype(jnp.bfloat16)
    blocks = (slices, 2, token_count, D)
    d_norm_sum, normed_one_all = lax.optimization_barrier((d_norm_sum, normed_one_all))
    low = functools.partial(jax.ShapeDtypeStruct, dtype=jnp.bfloat16)
    columns = low((4, 4, slices, ROWS, part))
    d_normed_two, out_rows, gate_grad, up_grad, down_low, down_high = communicate(
        "d_normed_out",
        3,
        (RingScatter, ROW, d_norm_sum.reshape(blocks)),
        (RingScatter, ROW, out_sum.reshape(blocks)),
        compute=((gate_grads, 1), (up_grads, 1), (down_grads, 2)),
        inputs=(normed_all, cot_all, hidden_low, d_gate, d_up),
        after=(
            (AxisScatter, ("z",), columns),
            (AxisScatter, ("y",), columns),
            (AxisScatter, ("z",), low((4, 4, DOWN_ROWS, DOWN_CUT))),
            (AxisScatter, ("y",), low((4, 4, DOWN_ROWS, D - DOWN_CUT))),
        ),
    )
    output = (residual + out_rows).astype(jnp.bfloat16)

    d_normed_two, attended_all = lax.optimization_barrier((d_normed_two, attended_all))
    d_query_low, d_k_all, d_v_all, d_residual, d_branch, gain_two_grad = attend_back(
        span_order,
        mine,
        k_all,
        v_all,
        q_pad,
        q_rows,
        attended_cols,
        lse,
        d_normed_two,
        residual,
        cotangent,
        gain_two_wide[None],
        out_full,
        cos_turned,
        sin_turned,
    )

    def turn_back(grads):
        scaled = grads * sine
        middle = HD // 2
        back = jnp.concatenate([scaled[..., middle:], -scaled[..., :middle]], axis=-1)
        return grads * cosine + back

    paired = functools.partial(PlaneScatter, pair=True)
    pairs = (4, 4, 2, token_count, k_cols)
    d_k, d_v, d_query_all, d_branch_all, gate_grad, up_grad, down_low, down_high = communicate(
        "d_kv_out",
        4,
        (paired, PLANE, d_k_all.reshape(pairs)),
        (paired, ENALP, d_v_all.reshape(pairs)),
        (RingGather, ROW, d_query_low),
        (RingGather, ROW, d_branch),
        (Deal, ("y",), gate_grad),
        (Deal, ("z",), up_grad),
        (AxisScatter, ("y",), down_low),
        (AxisScatter, ("z",), down_high),
    )
    d_key_raw = turn_back(d_k.reshape(token_count, KVH, HD))
    d_kv_low = jnp.concatenate(
        [d_key_raw.reshape(token_count, k_cols), d_v], axis=1
    ).astype(jnp.bfloat16)
    d_mixed = jnp.concatenate([d_query_low, d_kv_low], axis=1)
    d_normed_one = dot(d_mixed, qkv_full, 1, 1)
    d_input_part, gain_one_grad = jax.vjp(rms_apply, inputs_wide, gain_one_wide)[1](d_normed_one)
    input_grad = (d_input_part + d_residual).astype(jnp.bfloat16)
    gain_grads = jnp.concatenate([gain_one_grad, gain_two_grad[0]])
    gain_grads = jnp.pad(gain_grads, (0, 2048 - 2 * D)).reshape(16, 128)
    d_kv_rows, gain_grads, gate_grad, up_grad, down_low, down_high = communicate(
        "d_kv_in",
        5,
        (RingGather, ROW, d_kv_low),
        (RingGather, ROW, gain_grads),
        (AxisGather, ("y",), gate_grad),
        (AxisGather, ("z",), up_grad),
        (PlaneGather, PLANE, down_low),
        (PlaneGather, ENALP, down_high),
    )
    d_mixed_all = jnp.concatenate(
        [d_query_all.reshape(-1, q_cols), d_kv_rows.reshape(-1, 2 * k_cols)], axis=1
    )
    gain_grads = jnp.sum(gain_grads.reshape(2 * slices, -1), axis=0)
    bias_grad = jnp.sum(d_mixed_all.astype(jnp.float32), axis=0)

    half_rows = own_rows // 2
    first = dp * own_rows + core * half_rows

    def my_columns(tokens):
        return lax.dynamic_slice_in_dim(tokens, first, half_rows, axis=1)

    out_grad = dot(my_columns(attended_all), d_branch_all.reshape(-1, D), 0, 0)
    qkv_grad = dot(my_columns(normed_one_all), d_mixed_all, 0, 0)
    chips = 16
    width = chips * 128
    sums = jnp.concatenate(
        [
            jnp.concatenate([qkv_grad, out_grad], axis=1),
            jnp.pad(bias_grad, (0, width - bias_grad.shape[0]))[None],
            jnp.pad(gain_grads, (0, width - gain_grads.shape[0]))[None],
            jnp.zeros((14, width), jnp.float32),
        ],
        axis=0,
    ).astype(jnp.bfloat16)
    sums = sums.reshape(128, 4, 4, 128).transpose(1, 2, 0, 3)
    shared = functools.partial(AxisGather, share=True)
    sums_top, sums_end, gate_grad, up_grad = communicate(
        "grads",
        6,
        (PlaneTotal, PLANE, sums[:, :, :64]),
        (PlaneTotal, ENALP, sums[:, :, 64:].transpose(1, 0, 2, 3)),
        (shared, ("z",), gate_grad),
        (shared, ("y",), up_grad),
    )
    qkv_grad, out_grad, vectors = split_sums(
        sums_top, sums_end, half_rows, q_cols + 2 * k_cols
    )
    bias_grad, gain_grads = vectors[0], vectors[1]

    def owned(vector, start, count):
        width = count // slices
        return lax.dynamic_slice_in_dim(vector, start + dp * width, width)

    gate_grad, up_grad = widen(gate_grad, up_grad)
    down_grad = widen_down(down_low, down_high, part)
    return (
        output,
        input_grad,
        owned(gain_grads, 0, D),
        qkv_grad,
        owned(bias_grad, 0, q_cols + k_cols),
        owned(bias_grad, q_cols + k_cols, k_cols),
        out_grad,
        owned(gain_grads, D, D),
        gate_grad,
        up_grad,
        down_grad,
    )


def solution(mesh):
    grid = Mesh(mesh.devices.reshape(4, 4, 4, 2), ("dp", "z", "y", "core"))
    tokens = ("dp",) + CTX
    return jax.shard_map(
        body,
        mesh=grid,
        in_specs=(
            P(tokens, None),
            P(tokens, None),
            P(),
            P(tokens),
            P("dp"),
            P("dp", None),
            P("dp"),
            P("dp", None),
            P("dp"),
            P("dp", None),
            P("dp", None),
            P("dp", None),
        ),
        out_specs=(
            P(tokens, None),
            P(tokens, None),
            P("dp"),
            P("dp", None),
            P("dp"),
            P("dp"),
            P("dp", None),
            P("dp"),
            P("dp", None),
            P("dp", None),
            P("dp", None),
        ),
        check_vma=False,
    )
```
